128 devices in a mesh: section: 2 (over z_lo), dp: 16 (over x, z_hi, core), tensor: 4 (over y).
Axes of the slice: x: 4, y: 4, z: 4 (z_hi: 2, z_lo: 2; z = z_hi * 2 + z_lo), core: 2. Of those that a mesh axis runs over, the one named last changes fastest.
Arguments:
- inputs: bfloat16 [2, 32, 1024, 512], P('section', 'dp', 'tensor'), may hold values from -6 to 6
- lengths: int32 [32, 16], P('dp'), may hold values from 1 to 160, 1004 in all within a row
- w_qkv: bfloat16 [2, 3, 512, 512], P('section', None, None, 'tensor'), may hold values from -0.25 to 0.25
- w_out: bfloat16 [2, 512, 512], P('section', 'tensor'), may hold values from -1.5 to 1.5
- w_cross: bfloat16 [2, 2, 512, 512], P('section', None, None, 'tensor'), may hold values from -0.375 to 0.375
- w_up: bfloat16 [2, 512, 2048], P('section', None, 'tensor'), may hold values from -0.25 to 0.25
- w_down: bfloat16 [2, 2048, 512], P('section', 'tensor'), may hold values from -0.1875 to 0.1875
- norm_gain: float32 [2, 3, 512], P('section'), may hold values from 0.25 to 1.75
- norm_bias: float32 [2, 3, 512], P('section'), may hold values from -1.75 to 1.75
- cotangent: float32 [2, 32, 1024, 512], P('section', 'dp', 'tensor'), may hold values from -6 to 6
Outputs:
- outputs: float32 [2, 32, 1024, 512], P('section', 'dp', 'tensor')
- d_inputs: float32 [2, 32, 1024, 512], P('section', 'dp', 'tensor')
- grad_qkv: float32 [2, 3, 512, 512], P('section', None, None, 'tensor')
- grad_out: float32 [2, 512, 512], P('section', 'tensor')
- grad_cross: float32 [2, 2, 512, 512], P('section', None, None, 'tensor')
- grad_up: float32 [2, 512, 2048], P('section', None, 'tensor')
- grad_down: float32 [2, 2048, 512], P('section', 'tensor')
- grad_gain: float32 [2, 3, 512], P('section')
- grad_bias: float32 [2, 3, 512], P('section')
The draws below stay inside these ranges and needn't reach their ends.
Inputs may be any that keep to these rules, and one draw needn't show every extreme that they name: In each row the 16 lengths sum to 1004, and the largest is 160.
All inputs are finite; a program needn't handle non-finite values.
Results may differ from the reference program's by a relative error of at most 0.038.
Values may be sent and summed in bfloat16 or wider, within the bound.
A program may use at most 192 MiB of HBM per device.

```python
import math
import jax
import jax.numpy as jnp
import numpy as np
from jax import lax

D = 512
H = 8
HD = 64
FF = 2048
MEM = 20
L = 1024
SEGS = 16
MOST = 160
ROWS = 32


def block_levels(rng, shape, pieces, least, top_value):
    loudness, own = 1.0, jax.random.fold_in(rng, 6)
    for dim, parts in pieces:
        heights = jnp.exp(jax.random.uniform(jax.random.fold_in(own, dim), (parts,), jnp.float32, least / len(pieces), top_value / len(pieces)))
        loudness = loudness * jnp.repeat(heights, shape[dim] // parts).reshape([-1 if axis == dim else 1 for axis in range(len(shape))])
    return loudness


def split_up(amount, total, bound, skew):
    loads = [(1 << 20) // math.isqrt(grade ** skew) + 1 for grade in range(2, amount + 1)]
    spare, counts = total - bound - (amount - 1), [1] * (amount - 1)
    while spare > 0:
        free = [i for i in range(amount - 1) if counts[i] < bound]
        whole, remaining = sum([loads[i] for i in free]), spare
        for i in free:
            addition = min(bound - counts[i], max(1, remaining * loads[i] // whole), spare)
            counts[i] = counts[i] + addition
            spare = spare - addition
    return np.array([bound] + counts)


def uneven_parts(stream_key, count, total, most, slope):
    if count == 2:
        one = jax.random.randint(stream_key, (), max(1, total - most), min(most, total - 1) + 1)
        return jnp.stack([one, total - one])
    tallies = jnp.asarray(split_up(count, total, most, slope), jnp.int32)
    pairs = (count - 1) // 2
    donor, receiver = tallies[1:1 + 2 * pairs:2], tallies[2:2 + 2 * pairs:2]
    slack = jnp.minimum(donor - 1, most - receiver)
    shifted = jax.random.randint(jax.random.fold_in(stream_key, 1), (pairs,), 0, 1 << 20) % (slack + 1)
    tallies = tallies.at[1:1 + 2 * pairs:2].set(donor - shifted).at[2:2 + 2 * pairs:2].set(receiver + shifted)
    return tallies[jax.random.permutation(jax.random.fold_in(stream_key, 2), count)]


def noise(own_key, dims, scale, most, pieces=(), kind=jnp.bfloat16):
    result = jax.random.normal(own_key, dims, jnp.float32) * scale
    if len(pieces) > 0:
        result = block_levels(own_key, dims, pieces, -0.22, 0.18) * result
    return jnp.clip(result, min=-most, max=most).astype(kind)


def setup_inputs(seed: int = 0) -> dict:
    arg_keys = jax.random.split(jax.random.key(seed), 11)
    return {
        "inputs": noise(arg_keys[0], (2, ROWS, L, D), 1.0, 6.0, ((0, 2), (1, 16), (2, 4))),
        "lengths": jax.vmap(lambda own: uneven_parts(own, SEGS, L - MEM, MOST, 2))(jax.random.split(arg_keys[1], ROWS)).reshape((ROWS, SEGS)).astype(jnp.int32),
        "w_qkv": noise(arg_keys[2], (2, 3, D, D), D ** -0.5, 0.25, ((0, 2), (3, 4))),
        "w_out": noise(arg_keys[3], (2, D, D), (D // 32) ** -0.5, 1.5, ((0, 2), (1, 4))),
        "w_cross": noise(arg_keys[4], (2, 2, D, D), (D // 2) ** -0.5, 0.375, ((0, 2), (3, 4))),
        "w_up": noise(arg_keys[5], (2, D, FF), D ** -0.5, 0.25, ((0, 2), (2, 4))),
        "w_down": noise(arg_keys[6], (2, FF, D), (FF // 2) ** -0.5, 0.1875, ((0, 2), (1, 4))),
        "norm_gain": jnp.clip(1.0 + 0.15 * jax.random.normal(arg_keys[7], (2, 3, D), jnp.float32), 0.25, 1.75),
        "norm_bias": noise(arg_keys[8], (2, 3, D), 0.3, 1.75, ((0, 2),), jnp.float32),
        "cotangent": noise(arg_keys[9], (2, ROWS, L, D), 1.0, 6.0, ((0, 2), (1, 16), (2, 4)), jnp.float32),
    }


NORM_EPS = 1e-05
MASK_FILL = -1e+30

@jax.custom_vjp
def low(v):
    return lax.optimization_barrier(v.astype(jnp.bfloat16)).astype(jnp.float32)

@jax.custom_vjp
def low_back(v):
    return v

def low_keep(v):
    return (low(v), None)

def low_pass(kept, grad):
    return (grad,)

def back_keep(v):
    return (v, None)

def back_low(kept, grad):
    return (low(grad),)
low.defvjp(low_keep, low_pass)
low_back.defvjp(back_keep, back_low)

def round_both(value):
    return low_back(low(value))

def matmul_hi(left, right):
    return jnp.matmul(left, right, precision=lax.Precision.HIGHEST)

def layer_norm(summed_in, gain_vec, bias_vec):
    average = lax.optimization_barrier(jnp.mean(summed_in, axis=-1, keepdims=True))
    centred = summed_in - average
    spread = lax.optimization_barrier(jnp.mean(centred * centred, axis=-1, keepdims=True))
    return centred * lax.rsqrt(spread + NORM_EPS) * gain_vec + bias_vec

def segment_ids(seg_lengths):
    seg_ends = jnp.cumsum(seg_lengths, dtype=jnp.int32)
    offset_pos = jnp.arange(L, dtype=jnp.int32) - MEM
    seg_count = lax.optimization_barrier(jnp.sum((offset_pos[:, None] >= seg_ends[None, :]).astype(jnp.int32), axis=-1, dtype=jnp.int32))
    return jnp.where(offset_pos >= 0, seg_count + 1, 0)

def split_heads(row_vals):
    return row_vals.reshape(row_vals.shape[0], H, HD)

def attend(queries, key_rows, value_rows, allowed):
    scores = jnp.einsum('qhd,khd->hqk', split_heads(queries), split_heads(key_rows), precision=lax.Precision.HIGHEST)
    scores = low_back(scores * HD ** (-0.5))
    if allowed is not None:
        scores = jnp.where(allowed[None], scores, MASK_FILL)
    attn_probs = low(jax.nn.softmax(scores, axis=-1))
    context = jnp.einsum('hqk,khd->qhd', attn_probs, split_heads(value_rows), precision=lax.Precision.HIGHEST)
    return round_both(context.reshape(queries.shape[0], H * HD))

def self_block(section, rows_in, w_qkv, w_out, allowed):
    entered = low(rows_in)
    queries = round_both(matmul_hi(entered, w_qkv[section, 0]))
    key_rows = round_both(matmul_hi(entered, w_qkv[section, 1]))
    value_rows = round_both(matmul_hi(entered, w_qkv[section, 2]))
    context = attend(queries, key_rows, value_rows, allowed)
    return rows_in + low_back(matmul_hi(context, w_out[section]))

def feed_forward(section, hidden, w_up, w_down):
    up_proj = low_back(matmul_hi(low(hidden), w_up[section]))
    activated = low(jax.nn.gelu(up_proj, approximate=True))
    return hidden + low_back(matmul_hi(activated, w_down[section]))

def layer_pair(params, source, target, seg_ids):
    w_qkv, w_out, w_cross, w_up, w_down, norm_gain, norm_bias = params
    same_seg = seg_ids[:, None] == seg_ids[None, :]
    open_mask = same_seg | (seg_ids[:, None] == 0) | (seg_ids[None, :] == 0)
    positions = jnp.arange(L, dtype=jnp.int32)
    causal = same_seg & (positions[None, :] <= positions[:, None])
    h_enc = layer_norm(self_block(0, source, w_qkv, w_out, open_mask), norm_gain[0, 0], norm_bias[0, 0])
    enc_out = layer_norm(feed_forward(0, h_enc, w_up, w_down), norm_gain[0, 1], norm_bias[0, 1])
    memory = low(layer_norm(enc_out[:MEM], norm_gain[0, 2], norm_bias[0, 2]))
    mem_keys = round_both(matmul_hi(memory, w_cross[0, 0]))
    mem_values = round_both(matmul_hi(memory, w_cross[0, 1]))
    h_one = layer_norm(self_block(1, target, w_qkv, w_out, causal), norm_gain[1, 0], norm_bias[1, 0])
    cross_query = round_both(matmul_hi(low(h_one), w_cross[1, 0]))
    cross_term = low_back(matmul_hi(attend(cross_query, mem_keys, mem_values, None), w_cross[1, 1].T))
    h_two = layer_norm(h_one + cross_term, norm_gain[1, 1], norm_bias[1, 1])
    dec_out = layer_norm(feed_forward(1, h_two, w_up, w_down), norm_gain[1, 2], norm_bias[1, 2])
    return (enc_out, dec_out)

def reference(inputs, lengths, w_qkv, w_out, w_cross, w_up, w_down, norm_gain, norm_bias, cotangent):
    params = (w_qkv.astype(jnp.float32), w_out.astype(jnp.float32), w_cross.astype(jnp.float32), w_up.astype(jnp.float32), w_down.astype(jnp.float32), norm_gain, norm_bias)

    def one_row(running, row_data):
        source, target, seg_lengths, cot_source, cot_target = row_data
        seg_ids = segment_ids(seg_lengths)

        def bound_pair(weights, source_in, target_in):
            return layer_pair(weights, source_in, target_in, seg_ids)
        row_outs, pullback = jax.vjp(bound_pair, params, source.astype(jnp.float32), target.astype(jnp.float32))
        d_params, d_source, d_target = pullback((cot_source, cot_target))
        running = jax.tree.map(jnp.add, running, d_params)
        return (running, (row_outs[0], row_outs[1], d_source, d_target))
    zero_grads = jax.tree.map(jnp.zeros_like, params)
    totals, stacked = lax.scan(one_row, zero_grads, (inputs[0], inputs[1], lengths, cotangent[0], cotangent[1]))
    enc_outs, dec_outs, d_source, d_target = stacked
    return (jnp.stack([enc_outs, dec_outs]), jnp.stack([d_source, d_target]), totals[0], totals[1], totals[2], totals[3], totals[4], totals[5], totals[6])
```

```python
import jax
import jax.numpy as jnp
from jax import lax
from jax.experimental import pallas as pl
from jax.experimental.pallas import tpu as pltpu
from jax.sharding import PartitionSpec as P

F32 = jnp.float32
BF = jnp.bfloat16
MESH = pl.DeviceIdType.MESH

MEM = 20
MP = 32
R = 2
T = 256
HALO = 160
D = 512
NT = 4
W_ENC = T + 2 * HALO + MP
W_DEC = T + HALO
MEM_AT = T + 2 * HALO
EPS = 1e-05
FILL = -1e30
SCALE = 0.125

G_DOWN, G_UP, G_CROSS, G_OUT, G_QKV, G_ROWS = 0, 2048, 4096, 5120, 5632, 7168
QKV, OUT, CROSS, UP, DOWN = range(5)
W_ROWS = (512, 128, 512, 512, 512)


def dot(a, b):
    return lax.dot_general(a, b, (((1,), (0,)), ((), ())), preferred_element_type=F32)


def dot_nt(a, b):
    return lax.dot_general(a, b, (((1,), (1,)), ((), ())), preferred_element_type=F32)


def dot_tn(a, b):
    return lax.dot_general(a, b, (((0,), (0,)), ((), ())), preferred_element_type=F32)


def remote(src, dst, send, recv, **device):
    return pltpu.make_async_remote_copy(
        src_ref=src, dst_ref=dst, send_sem=send, recv_sem=recv, device_id=device, device_id_type=MESH
    )


def normed(v):
    c = v - jnp.mean(v, axis=1, keepdims=True)
    rs = lax.rsqrt(jnp.mean(c * c, axis=1, keepdims=True) + EPS)
    return c * rs, rs


def norm_back(xhat, rs, gain, dy):
    dxh = dy * gain
    m1 = jnp.mean(dxh, axis=1, keepdims=True)
    m2 = jnp.mean(dxh * xhat, axis=1, keepdims=True)
    return rs * (dxh - m1 - xhat * m2)


def gelu_both(u):
    k = 0.7978845608028654
    u2 = u * u
    th = jnp.tanh(k * u * (1.0 + 0.044715 * u2))
    half = 0.5 * (1.0 + th)
    grad = half + 0.5 * u * (1.0 - th * th) * (k * (1.0 + 3.0 * 0.044715 * u2))
    return u * half, grad


def layer_kernel(
    lens, x_in, cot_in, wqkv_in, wout_in, wcross_in, wup_in, wdown_in, gain, bias,
    y_out, dx_out, g_out, ng_out,
    x_ext, cotm, cot, wqkv, wout, wcross, wup, wdown,
    kk, vv, kt, vt, qs, pt, ctx, mask, hmask,
    xh1, xh2, xh3, rs1, rs2, rs3, h32, hb, h1b, act, gp, du, d32, dab, dr,
    dkv, dqkv, halo_s, halo_r, memd_s, memd_r,
    ex_o, ex_st, ex_f, ex_m, ex_h, ex_dq, qm,
    kvm, dkvm_s, dkvm_r, kblk, vblk, cpt, cq, cctx,
    mx1, mx2, mx3, mr1, mr2, mr3, mh, mact, mgp, mc, mm, mst, md,
    lsem, wsend, wrecv, xsend, xrecv, msend, mrecv, esend, erecv, ksend, krecv, dsend, drecv,
    hsend, hrecv, gsend, grecv, qsend, qrecv,
):
    sec = lax.axis_index("section")
    dp = lax.axis_index("dp")
    t = lax.axis_index("tensor")
    core = lax.rem(dp, 2)
    sib = dp + 1 - 2 * core
    is_enc = sec == 0
    is_dec = sec == 1
    left = lax.rem(t + 3, NT)
    right = lax.rem(t + 1, NT)
    opp = lax.rem(t + 2, NT)
    other = 1 - sec

    ins = (wqkv_in, wout_in, wcross_in, wup_in, wdown_in)
    ws = (wqkv, wout, wcross, wup, wdown)

    def part(i, ref, start, n):
        if i in (QKV, CROSS):
            return ref.at[:, pl.ds(start, n), :]
        return ref.at[pl.ds(start, n), :]

    def slot(i, a, start, n):
        if i in (QKV, CROSS):
            return ws[i].at[a, :, pl.ds(start, n), :]
        return ws[i].at[a, pl.ds(start, n), :]

    barrier = pltpu.get_barrier_semaphore()
    for off in (1, 2, 3):
        pl.semaphore_signal(barrier, inc=1, device_id={"tensor": lax.rem(t + off, NT)}, device_id_type=MESH)
    pl.semaphore_signal(barrier, inc=1, device_id={"dp": sib}, device_id_type=MESH)
    for b in range(NT):
        pl.semaphore_signal(barrier, inc=1, device_id={"section": other, "tensor": b}, device_id_type=MESH)

    locals_ = [
        pltpu.make_async_copy(x_in, x_ext.at[:, pl.ds(0, T), :], lsem.at[0]),
        pltpu.make_async_copy(cot_in, cot, lsem.at[1]),
    ]
    for i in range(5):
        locals_.append(pltpu.make_async_copy(ins[i], ws[i].at[t], lsem.at[2 + i]))
    for c in locals_:
        c.start()

    pl.semaphore_wait(barrier, 8)

    x_right = remote(x_in.at[:, pl.ds(T - HALO, HALO), :], x_ext.at[:, pl.ds(T, HALO), :],
                     xsend.at[0], xrecv.at[0], tensor=right)
    x_left = remote(x_in.at[:, pl.ds(0, HALO), :], x_ext.at[:, pl.ds(T + HALO, HALO), :],
                    xsend.at[1], xrecv.at[1], tensor=left)
    x_right.start()

    mem_copies = []
    for off in (1, 2, 3):
        to = lax.rem(t + off, NT)
        mem_copies.append(remote(x_in.at[:, pl.ds(0, MP), :], x_ext.at[:, pl.ds(MEM_AT, MP), :],
                                 msend.at[0, off - 1], mrecv.at[0], tensor=to))
        mem_copies.append(remote(cot_in.at[:, pl.ds(0, MP), :], cotm, msend.at[1, off - 1], mrecv.at[1], tensor=to))
    mem_local = [
        pltpu.make_async_copy(x_in.at[:, pl.ds(0, MP), :], x_ext.at[:, pl.ds(MEM_AT, MP), :], lsem.at[7]),
        pltpu.make_async_copy(cot_in.at[:, pl.ds(0, MP), :], cotm, lsem.at[8]),
    ]

    @pl.when(is_enc)
    def _():
        x_left.start()

        @pl.when(t == 0)
        def _():
            for c in mem_copies + mem_local:
                c.start()

    def w_copies(i):
        rows = W_ROWS[i]
        hf, qt = rows // 2, rows // 4
        mine = core * hf
        y_right = remote(part(i, ins[i], mine, hf), slot(i, t, mine, hf), wsend.at[i, 0], wrecv.at[i, 0], tensor=right)
        y_left = remote(part(i, ins[i], mine, hf), slot(i, t, mine, hf), wsend.at[i, 1], wrecv.at[i, 1], tensor=left)
        on_right = remote(slot(i, left, mine, qt), slot(i, left, mine, qt), wsend.at[i, 2], wrecv.at[i, 2], tensor=right)
        on_left = remote(slot(i, right, mine + qt, qt), slot(i, right, mine + qt, qt), wsend.at[i, 3], wrecv.at[i, 3],
                         tensor=left)
        s_left = remote(slot(i, left, mine, hf), slot(i, left, mine, hf), wsend.at[i, 4], wrecv.at[i, 4], dp=sib)
        s_right = remote(slot(i, right, mine, hf), slot(i, right, mine, hf), wsend.at[i, 5], wrecv.at[i, 5], dp=sib)
        s_opp = remote(slot(i, opp, mine, hf), slot(i, opp, mine, hf), wsend.at[i, 6], wrecv.at[i, 6], dp=sib)
        return y_right, y_left, on_right, on_left, s_left, s_right, s_opp

    copies = [w_copies(i) for i in range(5)]

    def send_first(i):
        copies[i][0].start()
        copies[i][1].start()

    def send_on(i):
        y_right, y_left, on_right, on_left, s_left, s_right, s_opp = copies[i]
        y_right.wait_recv()
        on_right.start()
        s_left.start()
        y_left.wait_recv()
        on_left.start()
        s_right.start()

    def send_opp(i):
        copies[i][2].wait_recv()
        copies[i][3].wait_recv()
        copies[i][6].start()

    def ready(i, rel):
        copies[i][4 + rel].wait_recv()

    send_first(QKV)
    send_first(OUT)

    lane = lax.broadcasted_iota(jnp.int32, (T, 128), 1)
    hmask[0] = jnp.where(lane < 64, 1.0, 0.0).astype(BF)
    hmask[1] = jnp.where(lane < 64, 0.0, 1.0).astype(BF)

    def segments(pos, r):
        off = pos - MEM
        seg = jnp.where(off >= 0, 1, 0)
        end = jnp.int32(0)
        for k in range(16):
            end = end + lens[r, k]
            seg = seg + jnp.where(off >= end, 1, 0)
        return seg

    def make_masks(width, encoder):
        for r in range(R):
            for half in range(2):
                i = lax.broadcasted_iota(jnp.int32, (width, 128), 0)
                pos = jnp.where(i < T, i, jnp.where(i < T + HALO, i - T - HALO, i - HALO)) + t * T
                qpos = lax.broadcasted_iota(jnp.int32, (8, 128), 1) + (t * T + half * 128)
                ks = segments(pos, r)
                q_seg = segments(qpos, r)[0:1]
                same = ks == q_seg
                if encoder:
                    ok = jnp.logical_or(jnp.logical_and(i < MEM_AT, jnp.logical_and(same, ks > 0)),
                                        jnp.logical_and(i >= MEM_AT, i < MEM_AT + MEM))
                else:
                    ok = jnp.logical_and(same, jnp.logical_and(pos <= qpos[0:1], pos >= 0))
                mask[r, 0:width, half * 128:half * 128 + 128] = jnp.where(ok, 0.0, FILL)

    @pl.when(is_enc)
    def _():
        make_masks(W_ENC, True)

    @pl.when(is_dec)
    def _():
        make_masks(W_DEC, False)

    locals_[0].wait()
    x_right.wait_recv()

    @pl.when(is_enc)
    def _():
        x_left.wait_recv()

        @pl.when(t == 0)
        def _():
            for c in mem_local:
                c.wait()

        @pl.when(t > 0)
        def _():
            mem_copies[0].wait_recv()
            mem_copies[1].wait_recv()

    for c in locals_[1:]:
        c.wait()

    def shard_at(step):
        return lax.rem(t + jnp.where(step == 0, 0, jnp.where(step == 1, 3, step - 1)), NT)

    lane_m = lax.broadcasted_iota(jnp.int32, (MP, 128), 1)
    low_m = lane_m < 64

    def project(a, width, encoder):
        wkv = jnp.concatenate([wqkv[a, 1], wqkv[a, 2]], axis=1)
        for r in range(R):
            kv = dot(x_ext[r, 0:width], wkv)
            k32, v32 = kv[:, 0:128], kv[:, 128:256]
            kk[a, r, 0:width] = k32.astype(BF)
            vv[a, r, 0:width] = v32.astype(BF)
            kt[a, r, :, 0:width] = k32.T.astype(BF)
            vt[a, r, :, 0:width] = v32.T.astype(BF)
            q = dot(x_ext[r, 0:T], wqkv[a, 0]).astype(BF)
            qs[a, r] = (q.astype(F32) * SCALE).astype(BF)
            if encoder:
                m32 = dot(x_ext[r, MEM_AT:MEM_AT + MP], wqkv[a, 0]).astype(BF).astype(F32) * SCALE
                lhs = jnp.concatenate([jnp.where(low_m, m32, 0.0), jnp.where(low_m, 0.0, m32)], axis=0).astype(BF)
                qm[a, r] = lhs
                s = dot_nt(lhs, k32[0:T].astype(BF))
                top = jnp.max(s, axis=1, keepdims=True)
                p = jnp.exp(s - top)
                total = jnp.sum(p, axis=1, keepdims=True)
                o = dot(p.astype(BF), v32[0:T].astype(BF)) / total
                ex_o[t, a, r * MP:r * MP + MP] = jnp.where(low_m, o[0:MP], o[MP:2 * MP]).astype(BF)
                st = ex_st[t, r * MP:r * MP + MP]
                st = jnp.where(lane_m == 2 * a, top[0:MP], st)
                st = jnp.where(lane_m == 2 * a + 1, top[MP:2 * MP], st)
                st = jnp.where(lane_m == 2 * a + 8, total[0:MP], st)
                st = jnp.where(lane_m == 2 * a + 9, total[MP:2 * MP], st)
                ex_st[t, r * MP:r * MP + MP] = st

    ex_st[t] = jnp.zeros((R * MP, 128), F32)

    @pl.loop(0, NT)
    def _(step):
        @pl.when(step == 1)
        def _():
            send_on(QKV)
            send_on(OUT)

            @pl.when(is_dec)
            def _():
                send_first(CROSS)

            send_first(UP)
            send_first(DOWN)
            ready(QKV, 0)

        @pl.when(step == 2)
        def _():
            ready(QKV, 1)

        @pl.when(step == 3)
        def _():
            send_opp(QKV)
            send_opp(OUT)
            ready(QKV, 2)

        a = shard_at(step)

        @pl.when(is_enc)
        def _():
            project(a, W_ENC, True)

        @pl.when(is_dec)
        def _():
            project(a, W_DEC, False)

    def ex_copies(e, buf):
        out = []
        for off in (1, 2, 3):
            out.append(remote(buf.at[t], buf.at[t], esend.at[e, off - 1], erecv.at[e, off - 1],
                              tensor=lax.rem(t + off, NT)))
        return out

    exchanges = [ex_copies(e, buf) for e, buf in enumerate((ex_o, ex_st, ex_f, ex_m, ex_h))]

    def ex_start(e):
        for c in exchanges[e]:
            c.start()

    def ex_wait(e):
        for c in exchanges[e]:
            c.wait_recv()

    @pl.when(is_enc)
    def _():
        ex_start(0)
        ex_start(1)

    def attend(a, r, width):
        tops = []
        for h in range(2):
            s = dot_nt(kk[a, r, 0:width], qs[a, r] * hmask[h]) + mask[r, 0:width]
            p = jnp.exp(s - jnp.max(s, axis=0, keepdims=True))
            p = (p * (1.0 / jnp.sum(p, axis=0, keepdims=True))).astype(BF)
            pt[a, r, h, 0:width] = p
            tops.append(dot(vt[a, r, h * 64:h * 64 + 64, 0:width], p))
        ctx[r, a] = jnp.concatenate(tops, axis=0).T.astype(BF)

    @pl.loop(0, NT * R)
    def _(i):
        a = shard_at(lax.div(i, 2))
        r = lax.rem(i, 2)

        @pl.when(is_enc)
        def _():
            attend(a, r, W_ENC)

        @pl.when(is_dec)
        def _():
            attend(a, r, W_DEC)

    for rel in range(3):
        ready(OUT, rel)

    def wide(ref, r):
        return jnp.concatenate([ref[r, a] for a in range(NT)], axis=1)

    w_out_full = wout[...].reshape(D, D)

    @pl.loop(0, R)
    def _(r):
        a0 = x_ext[r, 0:T].astype(F32) + dot(wide(ctx, r), w_out_full)
        xh, rs = normed(a0)
        xh1[r] = xh
        rs1[r] = rs
        h = xh * gain[0:1] + bias[0:1]
        h32[r] = h
        hb[r] = h.astype(BF)

    def mem_combine():
        for r in range(R):
            rows = slice(r * MP, r * MP + MP)
            sts = [ex_st[s, rows] for s in range(NT)]
            top = jnp.maximum(jnp.maximum(sts[0], sts[1]), jnp.maximum(sts[2], sts[3]))
            ws_ = [pltpu.roll(sts[s], 120, 1) * jnp.exp(sts[s] - top) for s in range(NT)]
            total = ws_[0] + ws_[1] + ws_[2] + ws_[3]
            inv = 1.0 / jnp.where(lane_m < 8, total, 1.0)
            mst[0, rows] = jnp.where(lane_m < 8, top + jnp.log(jnp.where(lane_m < 8, total, 1.0)), 0.0)
            for a in range(NT):
                acc = jnp.zeros((MP, 128), F32)
                for s in range(NT):
                    w = ws_[s] * inv
                    wide_w = jnp.where(low_m, w[:, 2 * a:2 * a + 1], w[:, 2 * a + 1:2 * a + 2])
                    acc = acc + wide_w * ex_o[s, a, rows].astype(F32)
                mc[rows, a * 128:a * 128 + 128] = acc

    def mem_first():
        mem_combine()
        xm = jnp.concatenate([x_ext[r, MEM_AT:MEM_AT + MP] for r in range(R)], axis=0).astype(F32)
        xh, rs = normed(xm + dot(mc[...].astype(BF), w_out_full))
        mx1[...] = xh
        mr1[...] = rs
        h = xh * gain[0:1] + bias[0:1]
        mh[...] = h
        av, gv = gelu_both(dot(h.astype(BF), wup[t]))
        mact[...] = av.astype(BF)
        mgp[...] = gv
        ex_f[t] = dot(av.astype(BF), wdown[t]).astype(BF)
        ex_start(2)

    kv_copies = [remote(kvm.at[t], kvm.at[t], ksend.at[b], krecv.at[t], section=other, tensor=b) for b in range(NT)]

    def mem_second():
        ex_wait(2)
        third = mh[...]
        for s in range(NT):
            third = third + ex_f[s].astype(F32)
        xh, rs = normed(third)
        mx2[...] = xh
        mr2[...] = rs
        y = xh * gain[1:2] + bias[1:2]
        md[...] = y
        xh, rs = normed(y)
        mx3[...] = xh
        mr3[...] = rs
        m = (xh * gain[2:3] + bias[2:3]).astype(BF)
        mm[...] = m
        kvm[t, 0] = dot(m, wcross[t, 0]).astype(BF)
        kvm[t, 1] = dot(m, wcross[t, 1]).astype(BF)
        for c in kv_copies:
            c.start()

    @pl.when(is_enc)
    def _():
        ex_wait(0)
        ex_wait(1)
        mem_first()

    @pl.when(is_dec)
    def _():
        send_on(CROSS)

    send_on(UP)
    send_on(DOWN)

    @pl.when(is_enc)
    def _():
        mem_second()

    @pl.when(is_dec)
    def _():
        send_opp(CROSS)

    send_opp(UP)
    send_opp(DOWN)

    pad_mask = jnp.where(
        lax.rem(lax.broadcasted_iota(jnp.int32, (256, T), 0), MP) < MEM, 0.0, FILL)

    def full_cross(j):
        return jnp.concatenate([wcross[a, j] for a in range(NT)], axis=1)

    def cross_forward():
        for rel in range(3):
            ready(CROSS, rel)
        for b in range(NT):
            remote(kvm.at[b], kvm.at[b], ksend.at[b], krecv.at[b], section=other, tensor=b).wait_recv()
        kblk[...] = jnp.zeros(kblk.shape, BF)
        vblk[...] = jnp.zeros(vblk.shape, BF)
        for r in range(R):
            for a in range(NT):
                for h in range(2):
                    at = slice(a * 64 + h * MP, a * 64 + h * MP + MP)
                    kblk[r, at, a * 128:a * 128 + 128] = kvm[a, 0, r * MP:r * MP + MP] * hmask[h, 0:MP]
                    vblk[r, at, a * 128:a * 128 + 128] = kvm[a, 1, r * MP:r * MP + MP] * hmask[h, 0:MP]
        wc0 = full_cross(0)
        wc1 = full_cross(1)

        @pl.loop(0, R)
        def _(r):
            h1b[r] = hb[r]
            q = dot(hb[r], wc0).astype(BF)
            q = (q.astype(F32) * SCALE).astype(BF)
            cq[r] = q
            s = dot_nt(kblk[r], q) + pad_mask
            s = s.reshape(8, MP, T)
            p = jnp.exp(s - jnp.max(s, axis=1, keepdims=True))
            p = p * (1.0 / jnp.sum(p, axis=1, keepdims=True))
            p = p.reshape(256, T).astype(BF)
            cpt[r] = p
            c = dot_tn(p, vblk[r]).astype(BF)
            cctx[r] = c
            xh, rs = normed(h32[r] + dot_nt(c, wc1))
            xh2[r] = xh
            rs2[r] = rs
            h = xh * gain[1:2] + bias[1:2]
            h32[r] = h
            hb[r] = h.astype(BF)

    @pl.when(is_dec)
    def _():
        cross_forward()

    for rel in range(3):
        ready(UP, rel)

    @pl.loop(0, NT * R)
    def _(i):
        a = lax.div(i, 2)
        r = lax.rem(i, 2)
        av, gv = gelu_both(dot(hb[r], wup[a]))
        act[r, a] = av.astype(BF)
        gp[r, a] = gv.astype(BF)

    for rel in range(3):
        ready(DOWN, rel)

    last = jnp.where(is_enc, 1, 2)
    g_last = jnp.where(is_enc, gain[1:2], gain[2:3])
    b_last = jnp.where(is_enc, bias[1:2], bias[2:3])
    ng_out[...] = jnp.zeros(ng_out.shape, F32)

    def add_norm(at, xh, dy):
        ng_out[pl.ds(at, 1)] += jnp.sum(dy * xh, axis=0, keepdims=True)
        ng_out[pl.ds(at + 3, 1)] += jnp.sum(dy, axis=0, keepdims=True)

    row_i = lax.broadcasted_iota(jnp.int32, (T, D), 0)
    is_mem_row = jnp.logical_and(row_i < MEM, jnp.logical_and(is_enc, t == 0))

    @pl.loop(0, R)
    def _(r):
        third = h32[r]
        for a in range(NT):
            third = third + dot(act[r, a], wdown[a])
        xh, rs = normed(third)
        y_out[r] = xh * g_last + b_last
        dy = jnp.where(is_mem_row, 0.0, cot[r])
        d3 = norm_back(xh, rs, g_last, dy)
        ng_out[pl.ds(last, 1)] += jnp.sum(dy * xh, axis=0, keepdims=True)
        ng_out[pl.ds(last + 3, 1)] += jnp.sum(dy, axis=0, keepdims=True)
        d32[r] = d3
        dab[r] = d3.astype(BF)

    @pl.when(jnp.logical_and(is_enc, t == 0))
    def _():
        for r in range(R):
            y_out[r, 0:24] = jnp.where(
                lax.broadcasted_iota(jnp.int32, (24, D), 0) < MEM, md[r * MP:r * MP + 24], y_out[r, 0:24])

    @pl.loop(0, NT)
    def _(a):
        for r in range(R):
            du[r, a] = (dot_nt(dab[r], wdown[a]) * gp[r, a].astype(F32)).astype(BF)
        wd = dot_tn(act[0, a], dab[0]) + dot_tn(act[1, a], dab[1])
        wu = dot_tn(hb[0], du[0, a]) + dot_tn(hb[1], du[1, a])
        for j in range(4):
            g_out[a, G_DOWN + D * j:G_DOWN + D * (j + 1)] = wd[:, 128 * j:128 * j + 128].astype(BF)
            g_out[a, G_UP + D * j:G_UP + D * (j + 1)] = wu[:, 128 * j:128 * j + 128].astype(BF)

    @pl.loop(0, R)
    def _(r):
        d = d32[r]
        for a in range(NT):
            d = d + dot_nt(du[r, a], wup[a])
        d32[r] = d

    dkv_copies = [
        remote(dkvm_s.at[b], dkvm_r.at[t], dsend.at[b], drecv.at[t], section=other, tensor=b) for b in range(NT)
    ]

    def cross_backward():
        wc0 = full_cross(0)
        wc1 = full_cross(1)

        @pl.loop(0, R)
        def _(r):
            dy = d32[r]
            add_norm(1, xh2[r], dy)
            d2 = norm_back(xh2[r], rs2[r], gain[1:2], dy)
            d32[r] = d2
            dcb = d2.astype(BF)
            dab[r] = dcb
            dc = dot(dcb, wc1).astype(BF)
            p = cpt[r].astype(F32).reshape(8, MP, T)
            dp_ = dot_nt(vblk[r], dc).reshape(8, MP, T)
            ds = p * (dp_ - jnp.sum(p * dp_, axis=1, keepdims=True))
            ds = ds.reshape(256, T).astype(BF)
            dk = dot(ds, cq[r])
            dv = dot(cpt[r], dc)
            rows = pl.ds(pl.multiple_of(r * MP, MP), MP)
            for a in range(NT):
                for j, val in ((0, dk), (1, dv)):
                    dkvm_s[a, j, rows] = jnp.where(
                        low_m, val[64 * a:64 * a + MP, 128 * a:128 * a + 128],
                        val[64 * a + MP:64 * a + 2 * MP, 128 * a:128 * a + 128])
            dq = (dot_tn(ds, kblk[r]) * SCALE).astype(BF)
            cq[r] = dq

        for c in dkv_copies:
            c.start()

        gq = dot_tn(h1b[0], cq[0]) + dot_tn(h1b[1], cq[1])
        go = dot_tn(dab[0], cctx[0]) + dot_tn(dab[1], cctx[1])
        for a in range(NT):
            g_out[a, G_CROSS:G_CROSS + D] = gq[:, 128 * a:128 * a + 128].astype(BF)
            g_out[a, G_CROSS + D:G_CROSS + 2 * D] = go[:, 128 * a:128 * a + 128].astype(BF)

        @pl.loop(0, R)
        def _(r):
            d32[r] += dot_nt(cq[r], wc0)

    @pl.when(is_dec)
    def _():
        cross_backward()

    @pl.loop(0, R)
    def _(r):
        dy = d32[r]
        add_norm(0, xh1[r], dy)
        d1 = norm_back(xh1[r], rs1[r], gain[0:1], dy)
        dx_out[r] = d1
        db = d1.astype(BF)
        dab[r] = db
        drr = dot_nt(db, w_out_full).astype(BF)
        for a in range(NT):
            dr[r, a] = drr[:, 128 * a:128 * a + 128]

    def attend_back(a, r, width, encoder):
        dk = jnp.zeros((width, 128), F32)
        dv = jnp.zeros((width, 128), F32)
        dqs = []
        for h in range(2):
            q_h = qs[a, r] * hmask[h]
            dr_h = dr[r, a] * hmask[h]
            pb = pt[a, r, h, 0:width]
            p = pb.astype(F32)
            dp_ = dot_nt(vv[a, r, 0:width], dr_h)
            ds = (p * (dp_ - jnp.sum(p * dp_, axis=0, keepdims=True))).astype(BF)
            dqs.append(dot(kt[a, r, h * 64:h * 64 + 64, 0:width], ds))
            dk = dk + dot(ds, q_h)
            dv = dv + dot(pb, dr_h)
        dqkv[r, a, :, 0:128] = (jnp.concatenate(dqs, axis=0).T * SCALE).astype(BF)
        for j, val in ((0, dk), (1, dv)):
            dkv[a, r, j] = val[0:T]
            halo_s[0, a, r, j] = val[T:T + HALO].astype(BF)
            if encoder:
                halo_s[1, a, r, j] = val[T + HALO:T + 2 * HALO].astype(BF)
                memd_s[a, r, j] = val[MEM_AT:MEM_AT + MP].astype(BF)

    def halo_copies(a):
        return (remote(halo_s.at[0, a], halo_r.at[0, a], hsend.at[0, a], hrecv.at[0, a], tensor=left),
                remote(halo_s.at[1, a], halo_r.at[1, a], hsend.at[1, a], hrecv.at[1, a], tensor=right))

    @pl.loop(0, NT)
    def _(a):
        for r in range(R):
            @pl.when(is_enc)
            def _():
                attend_back(a, r, W_ENC, True)

            @pl.when(is_dec)
            def _():
                attend_back(a, r, W_DEC, False)

        to_left, to_right = halo_copies(a)
        to_left.start()

        @pl.when(is_enc)
        def _():
            to_right.start()

    to_first = remote(memd_s, memd_r.at[t], gsend.at[0], grecv.at[t], tensor=0)

    @pl.when(jnp.logical_and(is_enc, t > 0))
    def _():
        to_first.start()

    def out_grad():
        wo = dot_tn(wide(ctx, 0), dab[0]) + dot_tn(wide(ctx, 1), dab[1])
        for a in range(NT):
            for j in range(4):
                g_out[a, G_OUT + 128 * j:G_OUT + 128 * j + 128] = (
                    wo[128 * a:128 * a + 128, 128 * j:128 * j + 128].astype(BF))

    out_grad()

    first = jnp.where(t == 0, 1.0, 0.0)
    dq_copy = remote(ex_dq.at[t], ex_dq.at[t], qsend.at[0], qrecv.at[t], tensor=0)

    def add_g(start, val):
        n = val.shape[0]
        g_out[t, start:start + n] = (g_out[t, start:start + n].astype(F32) + val).astype(BF)

    def add_norm_m(at, xh, dy):
        ng_out[at:at + 1] += first * jnp.sum(dy * xh, axis=0, keepdims=True)
        ng_out[at + 3:at + 4] += first * jnp.sum(dy, axis=0, keepdims=True)

    def mem_backward():
        for b in range(NT):
            remote(dkvm_s.at[b], dkvm_r.at[b], dsend.at[b], drecv.at[b], section=other, tensor=b).wait_recv()
        grads = []
        for j in range(2):
            tot = dkvm_r[0, j] + dkvm_r[1, j] + dkvm_r[2, j] + dkvm_r[3, j]
            grads.append(tot.astype(BF))
        ex_m[t] = (dot_nt(grads[0], wcross[t, 0]) + dot_nt(grads[1], wcross[t, 1])).astype(BF)
        ex_start(3)
        for a in range(NT):
            g_out[a, G_CROSS:G_CROSS + 2 * D] = jnp.zeros((2 * D, 128), BF)
        for j in range(2):
            g_out[t, G_CROSS + D * j:G_CROSS + D * j + D] = dot_tn(mm[...], grads[j]).astype(BF)
        ex_wait(3)
        dm = ex_m[0].astype(F32)
        for s in range(1, NT):
            dm = dm + ex_m[s].astype(F32)
        add_norm_m(2, mx3[...], dm)
        rows_m = lax.broadcasted_iota(jnp.int32, (R * MP, D), 0)
        cm = jnp.concatenate([cotm[0], cotm[1]], axis=0)
        cm = jnp.where(lax.rem(rows_m, MP) < MEM, cm, 0.0)
        dy = cm + norm_back(mx3[...], mr3[...], gain[2:3], dm)
        add_norm_m(1, mx2[...], dy)
        d3 = norm_back(mx2[...], mr2[...], gain[1:2], dy)
        d3b = d3.astype(BF)
        dum = (dot_nt(d3b, wdown[t]) * mgp[...]).astype(BF)
        ex_h[t] = dot_nt(dum, wup[t]).astype(BF)
        ex_start(4)
        wd = dot_tn(mact[...], d3b)
        wu = dot_tn(mh[...].astype(BF), dum)
        for j in range(4):
            add_g(G_DOWN + D * j, wd[:, 128 * j:128 * j + 128])
            add_g(G_UP + D * j, wu[:, 128 * j:128 * j + 128])
        ex_wait(4)
        d2 = d3
        for s in range(NT):
            d2 = d2 + ex_h[s].astype(F32)
        add_norm_m(0, mx1[...], d2)
        d1 = norm_back(mx1[...], mr1[...], gain[0:1], d2)
        md[...] = d1
        d1b = d1.astype(BF)
        drm = dot_nt(d1b, w_out_full).astype(BF).astype(F32)
        prod = drm * mc[...]
        for r in range(R):
            acc = jnp.zeros((MP, 128), F32)
            for hh in range(8):
                part_ = prod[r * MP:r * MP + MP, (hh // 2) * 128:(hh // 2) * 128 + 128]
                part_ = jnp.where(low_m if hh % 2 == 0 else jnp.logical_not(low_m), part_, 0.0)
                acc = jnp.where(lane_m == hh, jnp.sum(part_, axis=1, keepdims=True), acc)
            mst[1, r * MP:r * MP + MP] = acc
        for a in range(NT):
            @pl.when(t == a)
            def _():
                wo = dot_tn(mc[:, 128 * a:128 * a + 128].astype(BF), d1b)
                for j in range(4):
                    add_g(G_OUT + 128 * j, wo[:, 128 * j:128 * j + 128])
        for a in range(NT):
            for r in range(R):
                rows = slice(r * MP, r * MP + MP)
                lse = mst[0, rows]
                dlt = mst[1, rows]
                lse = jnp.concatenate([lse[:, 2 * a:2 * a + 1], lse[:, 2 * a + 1:2 * a + 2]], axis=0)
                dlt = jnp.concatenate([dlt[:, 2 * a:2 * a + 1], dlt[:, 2 * a + 1:2 * a + 2]], axis=0)
                lhs = qm[a, r]
                ko, vo = kk[a, r, 0:T], vv[a, r, 0:T]
                p = jnp.exp(dot_nt(lhs, ko) - lse)
                dra = drm[rows, 128 * a:128 * a + 128]
                dra = jnp.concatenate([jnp.where(low_m, dra, 0.0), jnp.where(low_m, 0.0, dra)], axis=0).astype(BF)
                ds = (p * (dot_nt(dra, vo) - dlt)).astype(BF)
                dq = dot(ds, ko)
                ex_dq[t, a, rows] = (jnp.where(low_m, dq[0:MP], dq[MP:2 * MP]) * SCALE).astype(BF)
                dkv[a, r, 0] += dot_tn(ds, lhs)
                dkv[a, r, 1] += dot_tn(p.astype(BF), dra)

        @pl.when(t > 0)
        def _():
            dq_copy.start()

        @pl.when(t == 0)
        def _():
            for r in range(R):
                dx_out[r, 0:MP] += md[r * MP:r * MP + MP]
            for s in range(1, NT):
                remote(memd_s, memd_r.at[s], gsend.at[0], grecv.at[s], tensor=0).wait_recv()
                remote(ex_dq.at[s], ex_dq.at[s], qsend.at[0], qrecv.at[s], tensor=0).wait_recv()
            for a in range(NT):
                for r in range(R):
                    rows = slice(r * MP, r * MP + MP)
                    for j in range(2):
                        tot = memd_s[a, r, j].astype(F32)
                        for s in range(1, NT):
                            tot = tot + memd_r[s, a, r, j].astype(F32)
                        dkv[a, r, j, 0:MP] += tot
                    tot = ex_dq[0, a, rows].astype(F32)
                    for s in range(1, NT):
                        tot = tot + ex_dq[s, a, rows].astype(F32)
                    dqkv[r, a, 0:MP, 0:128] = (dqkv[r, a, 0:MP, 0:128].astype(F32) + tot).astype(BF)

    @pl.when(is_enc)
    def _():
        mem_backward()

    @pl.loop(0, NT)
    def _(a):
        to_left, to_right = halo_copies(a)
        to_left.wait_recv()

        @pl.when(is_enc)
        def _():
            to_right.wait_recv()

        for r in range(R):
            for j in range(2):
                dkv[a, r, j, T - HALO:T] += halo_r[0, a, r, j].astype(F32)

                @pl.when(is_enc)
                def _():
                    dkv[a, r, j, 0:HALO] += halo_r[1, a, r, j].astype(F32)

                dqkv[r, a, :, 128 * (j + 1):128 * (j + 2)] = dkv[a, r, j].astype(BF)
        gw = dot_tn(x_ext[0, 0:T], dqkv[0, a]) + dot_tn(x_ext[1, 0:T], dqkv[1, a])
        for j in range(3):
            g_out[a, G_QKV + D * j:G_QKV + D * j + D] = gw[:, 128 * j:128 * j + 128].astype(BF)
        wfull = jnp.concatenate([wqkv[a, j] for j in range(3)], axis=1)
        for r in range(R):
            dx_out[r] += dot_nt(dqkv[r, a], wfull)

    for i in range(5):
        def drain(i=i):
            for c in copies[i]:
                c.wait_send()
        if i == CROSS:
            pl.when(is_dec)(drain)
        else:
            drain()
    x_right.wait_send()
    for a in range(NT):
        halo_copies(a)[0].wait_send()

    @pl.when(is_dec)
    def _():
        for c in dkv_copies:
            c.wait_send()

    @pl.when(is_enc)
    def _():
        x_left.wait_send()
        for a in range(NT):
            halo_copies(a)[1].wait_send()
        for e in range(5):
            for c in exchanges[e]:
                c.wait_send()
        for c in kv_copies:
            c.wait_send()

        @pl.when(t == 0)
        def _():
            for c in mem_copies:
                c.wait_send()

        @pl.when(t > 0)
        def _():
            to_first.wait_send()
            dq_copy.wait_send()


def layer_call(lens, x, cot, wqkv, wout, wcross, wup, wdown, gain, bias):
    any_ = pl.BlockSpec(memory_space=pl.ANY)
    vmem = pl.BlockSpec(memory_space=pltpu.VMEM)
    M = R * MP
    W = W_ENC
    V = pltpu.VMEM
    S = pltpu.SemaphoreType.DMA
    scratch = [
        V((R, W, D), BF), V((R, MP, D), F32), V((R, T, D), F32),
        V((NT, 3, D, 128), BF), V((NT, 128, D), BF), V((NT, 2, D, 128), BF), V((NT, D, D), BF), V((NT, D, D), BF),
        V((NT, R, W, 128), BF), V((NT, R, W, 128), BF), V((NT, R, 128, W), BF), V((NT, R, 128, W), BF),
        V((NT, R, T, 128), BF), V((NT, R, 2, W, T), BF), V((R, NT, T, 128), BF), V((R, W, T), F32), V((2, T, 128), BF),
        V((R, T, D), F32), V((R, T, D), F32), V((8, 128), F32),
        V((R, T, 1), F32), V((R, T, 1), F32), V((8, 128), F32),
        V((R, T, D), F32), V((R, T, D), BF), V((R, T, D), BF),
        V((R, NT, T, D), BF), V((R, NT, T, D), BF), V((R, NT, T, D), BF),
        V((R, T, D), F32), V((R, T, D), BF), V((R, NT, T, 128), BF),
        V((NT, R, 2, T, 128), F32), V((R, NT, T, 384), BF), V((2, NT, R, 2, HALO, 128), BF),
        V((2, NT, R, 2, HALO, 128), BF), V((NT, R, 2, MP, 128), BF), V((NT, NT, R, 2, MP, 128), BF),
        V((NT, NT, M, 128), BF), V((NT, M, 128), F32), V((NT, M, D), BF), V((NT, M, D), BF), V((NT, M, D), BF),
        V((NT, NT, M, 128), BF), V((NT, R, 2 * MP, 128), BF),
        V((NT, 2, M, 128), BF), V((NT, 2, M, 128), F32), V((NT, 2, M, 128), F32),
        V((R, 256, D), BF), V((R, 256, D), BF), V((R, 256, T), BF), V((R, T, D), BF), V((R, T, D), BF),
        V((M, D), F32), V((M, D), F32), V((M, D), F32), V((M, 1), F32), V((M, 1), F32), V((M, 1), F32),
        V((M, D), F32), V((M, D), BF), V((M, D), F32), V((M, D), F32), V((M, D), BF), V((2, M, 128), F32),
        V((M, D), F32),
        S((9,)), S((5, 7)), S((5, 7)), S((2,)), S((2,)), S((2, 3)), S((2,)), S((5, 3)), S((5, 3)),
        S((NT,)), S((NT,)), S((NT,)), S((NT,)), S((2, NT)), S((2, NT)), S((1,)), S((NT,)), S((1,)), S((NT,)),
    ]
    return pl.pallas_call(
        layer_kernel,
        out_shape=(
            jax.ShapeDtypeStruct((R, T, D), F32),
            jax.ShapeDtypeStruct((R, T, D), F32),
            jax.ShapeDtypeStruct((NT, G_ROWS, 128), BF),
            jax.ShapeDtypeStruct((8, D), F32),
        ),
        in_specs=[pl.BlockSpec(memory_space=pltpu.SMEM)] + [any_] * 7 + [vmem] * 2,
        out_specs=(vmem,) * 4,
        scratch_shapes=scratch,
        compiler_params=pltpu.CompilerParams(
            collective_id=0, has_side_effects=True, vmem_limit_bytes=60 * 1024 * 1024
        ),
        name="layers",
    )(lens, x, cot, wqkv, wout, wcross, wup, wdown, gain, bias)


CHUNKS = ((G_DOWN, 2048), (G_UP, 2048), (G_CROSS, 1024), (G_OUT, 2048))
HALF = G_ROWS // 2


def reduce_kernel(
    chips, g, ng, o_qkv, o_out, o_cross, o_up, o_down, o_gain, o_bias,
    r1, h, r2, y, r3, full, ny, nc, nx,
    s1, q1, s2, q2, s3, q3, s4, q4, s5, q5, ns, nq,
):
    dp = lax.axis_index("dp")
    t = lax.axis_index("tensor")
    core = lax.rem(dp, 2)
    chip = lax.div(dp, 2)
    sib = dp + 1 - 2 * core

    def chip_at(off):
        return lax.rem(chip + off, chips)

    barrier = pltpu.get_barrier_semaphore()
    for off in (1, 2, 3):
        pl.semaphore_signal(barrier, inc=1, device_id={"tensor": lax.rem(t + off, NT)}, device_id_type=MESH)
    pl.semaphore_signal(barrier, inc=1, device_id={"dp": sib}, device_id_type=MESH)
    for off in range(1, chips):
        pl.semaphore_signal(barrier, inc=1, device_id={"dp": chip_at(off) * 2 + core}, device_id_type=MESH)
    pl.semaphore_wait(barrier, 4 + chips - 1)

    def at(k):
        return CHUNKS[k][0] // 2, CHUNKS[k][1] // 2

    def piece(k):
        return CHUNKS[k][1] // 2 // chips

    def c1(k):
        start, n = CHUNKS[k]
        lo, hf = at(k)
        return [remote(g.at[:, pl.ds(start + (1 - core) * hf, hf), :], r1.at[:, pl.ds(lo, hf), :],
                       s1.at[k], q1.at[k], dp=sib)]

    def c2(k):
        lo, hf = at(k)
        out = []
        for off in (1, 2, 3):
            to = lax.rem(t + off, NT)
            out.append(remote(h.at[to, pl.ds(lo, hf), :], r2.at[off - 1, pl.ds(lo, hf), :],
                              s2.at[k, off - 1], q2.at[k, off - 1], tensor=to))
        return out

    def c3(k):
        lo, hf = at(k)
        n = piece(k)
        out = []
        for off in range(1, chips):
            to = chip_at(off)
            out.append(remote(y.at[pl.ds(lo + to * n, n), :], r3.at[off - 1, pl.ds(lo // chips, n), :],
                              s3.at[k, off - 1], q3.at[k, off - 1], dp=to * 2 + core))
        return out

    def c4(k):
        start, _ = CHUNKS[k]
        lo, hf = at(k)
        n = piece(k)
        mine = full.at[pl.ds(start + core * hf + chip * n, n), :]
        out = []
        for off in range(1, chips):
            out.append(remote(mine, mine, s4.at[k, off - 1], q4.at[k, off - 1], dp=chip_at(off) * 2 + core))
        return out

    def c5(k):
        start, _ = CHUNKS[k]
        lo, hf = at(k)
        mine = full.at[pl.ds(start + core * hf, hf), :]
        return [remote(mine, mine, s5.at[k], q5.at[k], dp=sib)]

    def go(copies):
        for c in copies:
            c.start()

    def come(copies):
        for c in copies:
            c.wait_recv()

    def gone(copies):
        for c in copies:
            c.wait_send()

    def stage(k, step):
        start, _ = CHUNKS[k]
        lo, hf = at(k)
        n = piece(k)
        if step == 0:
            go(c1(k))
        if step == 1:
            come(c1(k))
            for a in range(NT):
                h[a, lo:lo + hf] = (g[a, pl.ds(start + core * hf, hf)].astype(F32)
                                    + r1[a, lo:lo + hf].astype(F32)).astype(BF)
            go(c2(k))
        if step == 2:
            come(c2(k))
            tot = h[t, lo:lo + hf].astype(F32)
            for o in range(3):
                tot = tot + r2[o, lo:lo + hf].astype(F32)
            y[lo:lo + hf] = tot.astype(BF)
            go(c3(k))
        if step == 3:
            come(c3(k))
            tot = y[pl.ds(lo + chip * n, n)].astype(F32)
            for o in range(chips - 1):
                tot = tot + r3[o, lo // chips:lo // chips + n].astype(F32)
            full[pl.ds(start + core * hf + chip * n, n)] = tot.astype(BF)
            go(c4(k))
        if step == 4:
            come(c4(k))
            go(c5(k))
        if step == 5:
            come(c5(k))

    ny[t] = ng[...]
    n1 = [remote(ny.at[t], ny.at[t], ns.at[o - 1], nq.at[o - 1], tensor=lax.rem(t + o, NT)) for o in (1, 2, 3)]
    n2 = [remote(nc.at[0], nc.at[1], ns.at[3], nq.at[3], dp=sib)]
    n3 = [remote(nx.at[chip], nx.at[chip], ns.at[3 + o], nq.at[3 + o], dp=chip_at(o) * 2 + core)
          for o in range(1, chips)]
    go(n1)

    for tick in range(len(CHUNKS) + 5):
        for k in range(len(CHUNKS)):
            if 0 <= tick - k < 6:
                stage(k, tick - k)
        if tick == 1:
            come(n1)
            nc[0] = ny[0] + ny[1] + ny[2] + ny[3]
            go(n2)
        if tick == 2:
            come(n2)
            nx[chip] = nc[0] + nc[1]
            go(n3)
        if tick == 4:
            come(n3)
            tot = nx[0]
            for o in range(1, chips):
                tot = tot + nx[o]
            o_gain[...] = tot[0:3]
            o_bias[...] = tot[3:6]

    for j in range(3):
        o_qkv[j] = full[G_QKV + D * j:G_QKV + D * j + D].astype(F32)
    for j in range(2):
        o_cross[j] = full[G_CROSS + D * j:G_CROSS + D * j + D].astype(F32)
    for j in range(4):
        cols = slice(128 * j, 128 * j + 128)
        o_out[:, cols] = full[G_OUT + 128 * j:G_OUT + 128 * j + 128].astype(F32)
        o_up[:, cols] = full[G_UP + D * j:G_UP + D * j + D].astype(F32)
        o_down[:, cols] = full[G_DOWN + D * j:G_DOWN + D * j + D].astype(F32)

    for k in range(len(CHUNKS)):
        for c in (c1, c2, c3, c4, c5):
            gone(c(k))
    gone(n1)
    gone(n2)
    gone(n3)


def reduce_call(chips, g, ng):
    vmem = pl.BlockSpec(memory_space=pltpu.VMEM)
    V = pltpu.VMEM
    S = pltpu.SemaphoreType.DMA
    K = len(CHUNKS)
    o = max(chips - 1, 1)
    scratch = [
        V((NT, HALF, 128), BF), V((NT, HALF, 128), BF), V((3, HALF, 128), BF), V((HALF, 128), BF),
        V((o, HALF // chips, 128), BF), V((G_ROWS, 128), BF), V((NT, 8, D), F32), V((2, 8, D), F32),
        V((chips, 8, D), F32),
        S((K,)), S((K,)), S((K, 3)), S((K, 3)), S((K, o)), S((K, o)), S((K, o)), S((K, o)), S((K,)), S((K,)),
        S((4 + o,)), S((4 + o,)),
    ]

    def kernel(*refs):
        reduce_kernel(chips, *refs)

    return pl.pallas_call(
        kernel,
        out_shape=tuple(
            jax.ShapeDtypeStruct(s, F32)
            for s in ((3, D, 128), (128, D), (2, D, 128), (D, D), (D, D), (3, D), (3, D))
        ),
        in_specs=[vmem] * 2,
        out_specs=(vmem,) * 7,
        scratch_shapes=scratch,
        compiler_params=pltpu.CompilerParams(
            collective_id=1, has_side_effects=True, vmem_limit_bytes=60 * 1024 * 1024
        ),
        name="reduce",
    )(g, ng)


def solution(mesh):
    chips = mesh.shape["dp"] // 2

    def shards(inputs, lengths, w_qkv, w_out, w_cross, w_up, w_down, norm_gain, norm_bias, cotangent):
        y, dx, g, ng = layer_call(
            lengths, inputs[0], cotangent[0], w_qkv[0], w_out[0], w_cross[0], w_up[0], w_down[0],
            norm_gain[0], norm_bias[0])
        rest = reduce_call(chips, g, ng)
        return (y[None], dx[None]) + tuple(v[None] for v in rest)

    return jax.shard_map(
        shards,
        mesh=mesh,
        in_specs=(
            P("section", "dp", "tensor", None),
            P("dp", None),
            P("section", None, None, "tensor"),
            P("section", "tensor", None),
            P("section", None, None, "tensor"),
            P("section", None, "tensor"),
            P("section", "tensor", None),
            P("section", None, None),
            P("section", None, None),
            P("section", "dp", "tensor", None),
        ),
        out_specs=(
            P("section", "dp", "tensor", None),
            P("section", "dp", "tensor", None),
            P("section", None, None, "tensor"),
            P("section", "tensor", None),
            P("section", None, None, "tensor"),
            P("section", None, "tensor"),
            P("section", "tensor", None),
            P("section", None, None),
            P("section", None, None),
        ),
        check_vma=False,
    )
```

```python
import jax
import jax.numpy as jnp
from jax import lax
from jax.experimental import pallas as pl
from jax.experimental.pallas import tpu as pltpu
from jax.sharding import PartitionSpec as P

F32 = jnp.float32
BF = jnp.bfloat16
MESH = pl.DeviceIdType.MESH
VMEM_BYTES = 62 * 1024 * 1024

MEM = 20
MP = 32
R = 2
T = 256
HALO = 160
D = 512
NT = 4
W_ENC = T + 2 * HALO + MP
W_DEC = T + HALO
MEM_AT = T + 2 * HALO
EPS = 1e-05
FILL = -1e30
SCALE = 0.125

G_DOWN, G_UP, G_CROSS, G_OUT, G_QKV, G_ROWS = 0, 2048, 4096, 5120, 5632, 7168
CHUNKS = ((G_DOWN, 2048), (G_UP, 2048), (G_CROSS, 1024), (G_OUT, 512), (G_QKV, 1536))
C_DOWN, C_UP, C_CROSS, C_OUT, C_QKV = range(5)
LATE = G_CROSS // 2
HALF = G_ROWS // 2
QKV, OUT, CROSS, UP, DOWN = range(5)
W_ROWS = (512, 128, 512, 512, 512)


def dot(a, b):
    return lax.dot_general(a, b, (((1,), (0,)), ((), ())), preferred_element_type=F32)


def dot_nt(a, b):
    return lax.dot_general(a, b, (((1,), (1,)), ((), ())), preferred_element_type=F32)


def dot_tn(a, b):
    return lax.dot_general(a, b, (((0,), (0,)), ((), ())), preferred_element_type=F32)


def remote(src, dst, send, recv, **device):
    return pltpu.make_async_remote_copy(
        src_ref=src, dst_ref=dst, send_sem=send, recv_sem=recv, device_id=device, device_id_type=MESH
    )


def normed(v):
    c = v - jnp.mean(v, axis=1, keepdims=True)
    rs = lax.rsqrt(jnp.mean(c * c, axis=1, keepdims=True) + EPS)
    return c * rs, rs


def norm_back(xhat, rs, gain, dy):
    dxh = dy * gain
    m1 = jnp.mean(dxh, axis=1, keepdims=True)
    m2 = jnp.mean(dxh * xhat, axis=1, keepdims=True)
    return rs * (dxh - m1 - xhat * m2)


def gelu_both(u):
    k = 0.7978845608028654
    u2 = u * u
    th = jnp.tanh(k * u * (1.0 + 0.044715 * u2))
    half = 0.5 * (1.0 + th)
    grad = half + 0.5 * u * (1.0 - th * th) * (k * (1.0 + 3.0 * 0.044715 * u2))
    return u * half, grad


def layer_kernel(chips, names, *refs):
    (lens, x_in, cot_in, wqkv_in, wout_in, wcross_in, wup_in, wdown_in, gain, bias,
     y_out, dx_out, full, ng_tot) = refs[:14]
    m = dict(zip(names, refs[14:]))
    x_ext, cotm, d32, wqkv, wout, wcross, wup, wdown = (
        m[n] for n in ("x_ext", "cotm", "d32", "wqkv", "wout", "wcross", "wup", "wdown"))
    kk, vv, vt, qs, pt, ctx, mask, hmask = (m[n] for n in ("kk", "vv", "vt", "qs", "pt", "ctx", "mask", "hmask"))
    xh1, xh2, rs1, rs2, h32, hb, h1b, act, gp, dab, dr = (
        m[n] for n in ("xh1", "xh2", "rs1", "rs2", "h32", "hb", "h1b", "act", "gp", "dab", "dr"))
    dkv, halo_s, halo_r, memd_s, memd_r = (m[n] for n in ("dkv", "halo_s", "halo_r", "memd_s", "memd_r"))
    ex_o, ex_st, ex_f, ex_m, ex_h, ex_dq, qm = (
        m[n] for n in ("ex_o", "ex_st", "ex_f", "ex_m", "ex_h", "ex_dq", "qm"))
    kvm, dkvm_s, dkvm_r, kblk, vblk, cpt, cq, cctx = (
        m[n] for n in ("kvm", "dkvm_s", "dkvm_r", "kblk", "vblk", "cpt", "cq", "cctx"))
    mx1, mx2, mx3, mr1, mr2, mr3, mh, mact, mgp, mc, mm, mst, md = (
        m[n] for n in ("mx1", "mx2", "mx3", "mr1", "mr2", "mr3", "mh", "mact", "mgp", "mc", "mm", "mst", "md"))
    g, r1, r2, r3, rx, ry, ysum, ng, ny, nc, nx = (
        m[n] for n in ("g", "r1", "r2", "r3", "rx", "ry", "ysum", "ng", "ny", "nc", "nx"))
    (lsem, wsend, wrecv, xsend, xrecv, msend, mrecv, esend, erecv, ksend, krecv, dsend, drecv,
     hsend, hrecv, gsend, grecv, qsend, qrecv) = (
        m[n] for n in ("lsem", "wsend", "wrecv", "xsend", "xrecv", "msend", "mrecv", "esend", "erecv", "ksend",
                       "krecv", "dsend", "drecv", "hsend", "hrecv", "gsend", "grecv", "qsend", "qrecv"))
    s1, q1, s2, q2, s3, q3, s4, q4, s5, q5, ns, nq = (
        m[n] for n in ("s1", "q1", "s2", "q2", "s3", "q3", "s4", "q4", "s5", "q5", "ns", "nq"))

    def g_row(i):
        return gain[0, i:i + 1]

    def b_row(i):
        return bias[0, i:i + 1]

    sec = lax.axis_index("section")
    dp = lax.axis_index("dp")
    t = lax.axis_index("tensor")
    core = lax.rem(dp, 2)
    chip = lax.div(dp, 2)
    sib = dp + 1 - 2 * core
    is_enc = sec == 0
    is_dec = sec == 1
    left = lax.rem(t + 3, NT)
    right = lax.rem(t + 1, NT)
    opp = lax.rem(t + 2, NT)
    other = 1 - sec

    def chip_at(off):
        return lax.rem(chip + off, chips)

    ins = (wqkv_in, wout_in, wcross_in, wup_in, wdown_in)
    ws = (wqkv, wout, wcross, wup, wdown)

    def part(i, ref, start, n):
        if i in (QKV, CROSS):
            return ref.at[:, pl.ds(start, n), :]
        return ref.at[pl.ds(start, n), :]

    def slot(i, a, start, n):
        if i in (QKV, CROSS):
            return ws[i].at[a, :, pl.ds(start, n), :]
        return ws[i].at[a, pl.ds(start, n), :]

    barrier = pltpu.get_barrier_semaphore()
    for off in (1, 2, 3):
        pl.semaphore_signal(barrier, inc=1, device_id={"tensor": lax.rem(t + off, NT)}, device_id_type=MESH)
    pl.semaphore_signal(barrier, inc=1, device_id={"dp": sib}, device_id_type=MESH)
    for b in range(NT):
        pl.semaphore_signal(barrier, inc=1, device_id={"section": other, "tensor": b}, device_id_type=MESH)
    for off in range(1, chips):
        pl.semaphore_signal(barrier, inc=1, device_id={"dp": chip_at(off) * 2 + core}, device_id_type=MESH)

    locals_ = [
        pltpu.make_async_copy(x_in, x_ext.at[:, pl.ds(0, T), :], lsem.at[0]),
        pltpu.make_async_copy(cot_in, d32, lsem.at[1]),
    ]
    for i in range(5):
        locals_.append(pltpu.make_async_copy(ins[i], ws[i].at[t], lsem.at[2 + i]))
    for c in locals_:
        c.start()

    pl.semaphore_wait(barrier, 8 + chips - 1)

    x_right = remote(x_in.at[:, pl.ds(T - HALO, HALO), :], x_ext.at[:, pl.ds(T, HALO), :],
                     xsend.at[0], xrecv.at[0], tensor=right)
    x_left = remote(x_in.at[:, pl.ds(0, HALO), :], x_ext.at[:, pl.ds(T + HALO, HALO), :],
                    xsend.at[1], xrecv.at[1], tensor=left)
    x_right.start()

    mem_x, mem_c = [], []
    for off in (1, 2, 3):
        to = lax.rem(t + off, NT)
        mem_x.append(remote(x_in.at[:, pl.ds(0, MP), :], x_ext.at[:, pl.ds(MEM_AT, MP), :],
                            msend.at[0, off - 1], mrecv.at[0], tensor=to))
        mem_c.append(remote(cot_in.at[:, pl.ds(0, MP), :], cotm, msend.at[1, off - 1], mrecv.at[1], tensor=to))
    mem_local = [
        pltpu.make_async_copy(x_in.at[:, pl.ds(0, MP), :], x_ext.at[:, pl.ds(MEM_AT, MP), :], lsem.at[7]),
        pltpu.make_async_copy(cot_in.at[:, pl.ds(0, MP), :], cotm, lsem.at[8]),
    ]

    @pl.when(is_enc)
    def _():
        x_left.start()

        @pl.when(t == 0)
        def _():
            for c in mem_x + mem_local:
                c.start()

    def w_copies(i):
        rows = W_ROWS[i]
        hf, qt = rows // 2, rows // 4
        mine = core * hf
        y_right = remote(part(i, ins[i], mine, hf), slot(i, t, mine, hf), wsend.at[i, 0], wrecv.at[i, 0], tensor=right)
        y_left = remote(part(i, ins[i], mine, hf), slot(i, t, mine, hf), wsend.at[i, 1], wrecv.at[i, 1], tensor=left)
        on_right = remote(slot(i, left, mine, qt), slot(i, left, mine, qt), wsend.at[i, 2], wrecv.at[i, 2], tensor=right)
        on_left = remote(slot(i, right, mine + qt, qt), slot(i, right, mine + qt, qt), wsend.at[i, 3], wrecv.at[i, 3],
                         tensor=left)
        s_left = remote(slot(i, left, mine, hf), slot(i, left, mine, hf), wsend.at[i, 4], wrecv.at[i, 4], dp=sib)
        s_right = remote(slot(i, right, mine, hf), slot(i, right, mine, hf), wsend.at[i, 5], wrecv.at[i, 5], dp=sib)
        s_opp = remote(slot(i, opp, mine, hf), slot(i, opp, mine, hf), wsend.at[i, 6], wrecv.at[i, 6], dp=sib)
        return y_right, y_left, on_right, on_left, s_left, s_right, s_opp

    copies = [w_copies(i) for i in range(5)]

    def send_first(i):
        copies[i][0].start()
        copies[i][1].start()

    def send_on(i):
        y_right, y_left, on_right, on_left, s_left, s_right, s_opp = copies[i]
        y_right.wait_recv()
        on_right.start()
        s_left.start()
        y_left.wait_recv()
        on_left.start()
        s_right.start()

    def send_opp(i):
        copies[i][2].wait_recv()
        copies[i][3].wait_recv()
        copies[i][6].start()

    def ready(i, rel):
        copies[i][4 + rel].wait_recv()

    send_first(QKV)
    send_first(OUT)

    lane = lax.broadcasted_iota(jnp.int32, (T, 128), 1)
    hmask[0] = jnp.where(lane < 64, 1.0, 0.0).astype(BF)
    hmask[1] = jnp.where(lane < 64, 0.0, 1.0).astype(BF)

    def segments(pos, r):
        off = pos - MEM
        seg = jnp.where(off >= 0, 1, 0)
        end = jnp.int32(0)
        for k in range(16):
            end = end + lens[r, k]
            seg = seg + jnp.where(off >= end, 1, 0)
        return seg

    def make_masks(width, encoder):
        for r in range(R):
            i = lax.broadcasted_iota(jnp.int32, (width, 128), 0)
            pos = jnp.where(i < T, i, jnp.where(i < T + HALO, i - T - HALO, i - HALO)) + t * T
            ks = segments(pos, r)
            for half in range(2):
                qpos = lax.broadcasted_iota(jnp.int32, (8, 128), 1) + (t * T + half * 128)
                q_seg = segments(qpos, r)[0:1]
                same = ks == q_seg
                if encoder:
                    ok = jnp.logical_or(jnp.logical_and(i < MEM_AT, jnp.logical_and(same, ks > 0)),
                                        jnp.logical_and(i >= MEM_AT, i < MEM_AT + MEM))
                else:
                    ok = jnp.logical_and(same, jnp.logical_and(pos <= qpos[0:1], pos >= 0))
                mask[r, 0:width, half * 128:half * 128 + 128] = jnp.where(ok, 0.0, FILL)

    @pl.when(is_enc)
    def _():
        make_masks(W_ENC, True)

    @pl.when(is_dec)
    def _():
        make_masks(W_DEC, False)

    ex_st[t] = jnp.zeros((R * MP, 128), F32)
    ng[...] = jnp.zeros(ng.shape, F32)

    locals_[0].wait()
    locals_[2 + QKV].wait()
    x_right.wait_recv()

    @pl.when(is_enc)
    def _():
        x_left.wait_recv()

        @pl.when(t == 0)
        def _():
            mem_local[0].wait()

        @pl.when(t > 0)
        def _():
            mem_x[0].wait_recv()

    def shard_at(step):
        return lax.rem(t + jnp.where(step == 0, 0, jnp.where(step == 1, 3, step - 1)), NT)

    lane_m = lax.broadcasted_iota(jnp.int32, (MP, 128), 1)
    low_m = lane_m < 64

    def project(a, width, encoder):
        wkv = jnp.concatenate([wqkv[a, 1], wqkv[a, 2]], axis=1)
        for r in range(R):
            kv = dot(x_ext[r, 0:width], wkv)
            k32, v32 = kv[:, 0:128], kv[:, 128:256]
            kk[a, r, 0:width] = k32.astype(BF)
            vv[a, r, 0:width] = v32.astype(BF)
            vt[a, r, :, 0:width] = v32.T.astype(BF)
            q = dot(x_ext[r, 0:T], wqkv[a, 0]).astype(BF)
            qs[a, r] = (q.astype(F32) * SCALE).astype(BF)
            if encoder:
                m32 = dot(x_ext[r, MEM_AT:MEM_AT + MP], wqkv[a, 0]).astype(BF).astype(F32) * SCALE
                lhs = jnp.concatenate([jnp.where(low_m, m32, 0.0), jnp.where(low_m, 0.0, m32)], axis=0).astype(BF)
                qm[a, r] = lhs
                s = dot_nt(lhs, k32[0:T].astype(BF))
                top = jnp.max(s, axis=1, keepdims=True)
                p = jnp.exp(s - top)
                total = jnp.sum(p, axis=1, keepdims=True)
                o = dot(p.astype(BF), v32[0:T].astype(BF)) / total
                ex_o[t, a, r * MP:r * MP + MP] = jnp.where(low_m, o[0:MP], o[MP:2 * MP]).astype(BF)
                st = ex_st[t, r * MP:r * MP + MP]
                st = jnp.where(lane_m == 2 * a, top[0:MP], st)
                st = jnp.where(lane_m == 2 * a + 1, top[MP:2 * MP], st)
                st = jnp.where(lane_m == 2 * a + 8, total[0:MP], st)
                st = jnp.where(lane_m == 2 * a + 9, total[MP:2 * MP], st)
                ex_st[t, r * MP:r * MP + MP] = st

    def ex_copies(e, buf):
        out = []
        for off in (1, 2, 3):
            out.append(remote(buf.at[t], buf.at[t], esend.at[e, off - 1], erecv.at[e, off - 1],
                              tensor=lax.rem(t + off, NT)))
        return out

    exchanges = [ex_copies(e, buf) for e, buf in enumerate((ex_o, ex_st, ex_f, ex_m, ex_h))]

    def ex_start(e):
        for c in exchanges[e]:
            c.start()

    def ex_wait(e):
        for c in exchanges[e]:
            c.wait_recv()

    def wide(ref, r):
        return jnp.concatenate([ref[r, a] for a in range(NT)], axis=1)

    def w_out_full():
        return wout[...].reshape(D, D)

    def mem_combine():
        for r in range(R):
            rows = slice(r * MP, r * MP + MP)
            sts = [ex_st[s, rows] for s in range(NT)]
            top = jnp.maximum(jnp.maximum(sts[0], sts[1]), jnp.maximum(sts[2], sts[3]))
            wts = [pltpu.roll(sts[s], 120, 1) * jnp.exp(sts[s] - top) for s in range(NT)]
            total = wts[0] + wts[1] + wts[2] + wts[3]
            total = jnp.where(lane_m < 8, total, 1.0)
            inv = 1.0 / total
            mst[0, rows] = jnp.where(lane_m < 8, top + jnp.log(total), 0.0)
            for a in range(NT):
                acc = jnp.zeros((MP, 128), F32)
                for s in range(NT):
                    w = wts[s] * inv
                    wide_w = jnp.where(low_m, w[:, 2 * a:2 * a + 1], w[:, 2 * a + 1:2 * a + 2])
                    acc = acc + wide_w * ex_o[s, a, rows].astype(F32)
                mc[rows, a * 128:a * 128 + 128] = acc

    def mem_first():
        mem_combine()
        xm = jnp.concatenate([x_ext[r, MEM_AT:MEM_AT + MP] for r in range(R)], axis=0).astype(F32)
        xh, rs = normed(xm + dot(mc[...].astype(BF), w_out_full()))
        mx1[...] = xh
        mr1[...] = rs
        h = xh * g_row(0) + b_row(0)
        mh[...] = h
        av, gv = gelu_both(dot(h.astype(BF), wup[t]))
        mact[...] = av.astype(BF)
        mgp[...] = gv
        ex_f[t] = dot(av.astype(BF), wdown[t]).astype(BF)
        ex_start(2)

    kv_copies = [remote(kvm.at[t], kvm.at[t], ksend.at[b], krecv.at[t], section=other, tensor=b) for b in range(NT)]

    def mem_second():
        third = mh[...]
        for s in range(NT):
            third = third + ex_f[s].astype(F32)
        xh, rs = normed(third)
        mx2[...] = xh
        mr2[...] = rs
        y = xh * g_row(1) + b_row(1)
        md[...] = y
        xh, rs = normed(y)
        mx3[...] = xh
        mr3[...] = rs
        mv = (xh * g_row(2) + b_row(2)).astype(BF)
        mm[...] = mv
        kvm[t, 0] = dot(mv, wcross[t, 0]).astype(BF)
        kvm[t, 1] = dot(mv, wcross[t, 1]).astype(BF)
        for c in kv_copies:
            c.start()

    def attend(a, r, width):
        tops = []
        for h in range(2):
            s = dot_nt(kk[a, r, 0:width], qs[a, r] * hmask[h]) + mask[r, 0:width]
            p = jnp.exp(s - jnp.max(s, axis=0, keepdims=True))
            p = (p * (1.0 / jnp.sum(p, axis=0, keepdims=True))).astype(BF)
            pt[a, r, h, 0:width] = p
            tops.append(dot(vt[a, r, h * 64:h * 64 + 64, 0:width], p))
        ctx[r, a] = jnp.concatenate(tops, axis=0).T.astype(BF)

    @pl.loop(0, NT * R)
    def _(i):
        @pl.when(i == 1)
        def _():
            send_on(QKV)

            @pl.when(is_dec)
            def _():
                send_first(CROSS)

            send_first(UP)
            send_first(DOWN)
            ready(QKV, 0)
            ready(QKV, 1)

        @pl.when(i == 2)
        def _():
            send_opp(QKV)
            ready(QKV, 2)
            send_on(OUT)

        step_from = jnp.where(i == 0, 0, jnp.where(i == 1, 1, jnp.where(i == 2, 3, 4)))
        step_to = jnp.where(i == 0, 1, jnp.where(i == 1, 3, 4))

        @pl.loop(step_from, step_to)
        def _(step):
            @pl.when(is_enc)
            def _():
                project(shard_at(step), W_ENC, True)

            @pl.when(is_dec)
            def _():
                project(shard_at(step), W_DEC, False)

        @pl.when(i == 2)
        def _():
            @pl.when(is_enc)
            def _():
                ex_start(0)
                ex_start(1)

        @pl.when(i == 4)
        def _():
            send_opp(OUT)
            locals_[2 + OUT].wait()
            for rel in range(3):
                ready(OUT, rel)

            @pl.when(is_dec)
            def _():
                send_on(CROSS)

            @pl.when(is_enc)
            def _():
                locals_[2 + UP].wait()
                locals_[2 + DOWN].wait()
                ex_wait(0)
                ex_wait(1)
                mem_first()

        @pl.when(i == 6)
        def _():
            send_on(UP)

            @pl.when(is_enc)
            def _():
                locals_[2 + CROSS].wait()
                ex_wait(2)
                mem_second()

        a = shard_at(lax.div(i, 2))
        r = lax.rem(i, 2)

        @pl.when(is_enc)
        def _():
            attend(a, r, W_ENC)

        @pl.when(is_dec)
        def _():
            attend(a, r, W_DEC)

    @pl.when(is_dec)
    def _():
        send_opp(CROSS)
        locals_[2 + CROSS].wait()
        locals_[2 + UP].wait()
        locals_[2 + DOWN].wait()

    send_on(DOWN)

    @pl.when(jnp.logical_and(is_enc, t == 0))
    def _():
        for c in mem_c:
            c.start()

    @pl.loop(0, R)
    def _(r):
        a0 = x_ext[r, 0:T].astype(F32) + dot(wide(ctx, r), w_out_full())
        xh, rs = normed(a0)
        xh1[r] = xh
        rs1[r] = rs
        h = xh * g_row(0) + b_row(0)
        h32[r] = h
        hb[r] = h.astype(BF)

    send_opp(UP)

    pad_mask = jnp.where(
        lax.rem(lax.broadcasted_iota(jnp.int32, (256, T), 0), MP) < MEM, 0.0, FILL)

    def full_cross(j):
        return jnp.concatenate([wcross[a, j] for a in range(NT)], axis=1)

    def cross_forward():
        for rel in range(3):
            ready(CROSS, rel)
        wc0 = full_cross(0)
        wc1 = full_cross(1)
        kblk[...] = jnp.zeros(kblk.shape, BF)
        vblk[...] = jnp.zeros(vblk.shape, BF)

        @pl.loop(0, R)
        def _(r):
            h1b[r] = hb[r]
            q = dot(hb[r], wc0).astype(BF)
            cq[r] = (q.astype(F32) * SCALE).astype(BF)

        for b in range(NT):
            remote(kvm.at[b], kvm.at[b], ksend.at[b], krecv.at[b], section=other, tensor=b).wait_recv()
        for r in range(R):
            for a in range(NT):
                for h in range(2):
                    at = slice(a * 64 + h * MP, a * 64 + h * MP + MP)
                    kblk[r, at, a * 128:a * 128 + 128] = kvm[a, 0, r * MP:r * MP + MP] * hmask[h, 0:MP]
                    vblk[r, at, a * 128:a * 128 + 128] = kvm[a, 1, r * MP:r * MP + MP] * hmask[h, 0:MP]

        @pl.loop(0, R)
        def _(r):
            s = dot_nt(kblk[r], cq[r]) + pad_mask
            s = s.reshape(8, MP, T)
            p = jnp.exp(s - jnp.max(s, axis=1, keepdims=True))
            p = p * (1.0 / jnp.sum(p, axis=1, keepdims=True))
            p = p.reshape(256, T).astype(BF)
            cpt[r] = p
            c = dot_tn(p, vblk[r]).astype(BF)
            cctx[r] = c
            xh, rs = normed(h32[r] + dot_nt(c, wc1))
            xh2[r] = xh
            rs2[r] = rs
            h = xh * g_row(1) + b_row(1)
            h32[r] = h
            hb[r] = h.astype(BF)

    @pl.when(is_dec)
    def _():
        cross_forward()

    @pl.loop(0, NT * R)
    def _(i):
        for rel in range(3):
            @pl.when(i == 2 * rel + 2)
            def _():
                ready(UP, rel)

        a = shard_at(lax.div(i, 2))
        r = lax.rem(i, 2)
        av, gv = gelu_both(dot(hb[r], wup[a]))
        act[r, a] = av.astype(BF)
        gp[r, a] = gv.astype(BF)

    send_opp(DOWN)
    for rel in range(3):
        ready(DOWN, rel)
    locals_[1].wait()

    last = jnp.where(is_enc, 1, 2)
    g_last = jnp.where(is_enc, g_row(1), g_row(2))
    b_last = jnp.where(is_enc, b_row(1), b_row(2))

    def add_norm(at, xh, dy):
        ng[pl.ds(at, 1)] += jnp.sum(dy * xh, axis=0, keepdims=True)
        ng[pl.ds(at + 3, 1)] += jnp.sum(dy, axis=0, keepdims=True)

    row_i = lax.broadcasted_iota(jnp.int32, (T, D), 0)
    is_mem_row = jnp.logical_and(row_i < MEM, jnp.logical_and(is_enc, t == 0))

    @pl.loop(0, R)
    def _(r):
        third = h32[r]
        for a in range(NT):
            third = third + dot(act[r, a], wdown[a])
        xh, rs = normed(third)
        h32[r] = xh * g_last + b_last
        dy = jnp.where(is_mem_row, 0.0, d32[r])
        d3 = norm_back(xh, rs, g_last, dy)
        ng[pl.ds(last, 1)] += jnp.sum(dy * xh, axis=0, keepdims=True)
        ng[pl.ds(last + 3, 1)] += jnp.sum(dy, axis=0, keepdims=True)
        d32[r] = d3
        dab[r] = d3.astype(BF)

    @pl.when(jnp.logical_and(is_enc, t == 0))
    def _():
        for r in range(R):
            h32[r, 0:24] = jnp.where(
                lax.broadcasted_iota(jnp.int32, (24, D), 0) < MEM, md[r * MP:r * MP + 24], h32[r, 0:24])

    y_copy = pltpu.make_async_copy(h32, y_out, lsem.at[9])
    y_copy.start()

    def at(k):
        return CHUNKS[k][0], CHUNKS[k][0] // 2, CHUNKS[k][1] // 2

    def own_half(k):
        start, lo, hf = at(k)
        return start + core * hf

    def pair(k, a):
        start, lo, hf = at(k)
        return remote(g.at[a, pl.ds(start + (1 - core) * hf, hf), :], r1.at[a, pl.ds(lo, hf), :],
                      s1.at[k, a], q1.at[k, a], dp=sib)

    def pair_sum(k, a):
        start, lo, hf = at(k)
        rows = pl.ds(own_half(k), hf)
        g[a, rows] = (g[a, rows].astype(F32) + r1[a, lo:lo + hf].astype(F32)).astype(BF)

    def over_tensor(k, a):
        start, lo, hf = at(k)
        rel = lax.rem(a - t + NT, NT) - 1
        return remote(g.at[a, pl.ds(own_half(k), hf), :], r2.at[rel, pl.ds(lo - LATE, hf), :],
                      s2.at[k, rel], q2.at[k, rel], tensor=a)

    def from_tensor(k, rel):
        start, lo, hf = at(k)
        return remote(g.at[0, pl.ds(own_half(k), hf), :], r2.at[rel, pl.ds(lo - LATE, hf), :],
                      s2.at[k, rel], q2.at[k, rel], tensor=right)

    def tensor_sum(k):
        start, lo, hf = at(k)
        tot = g[t, pl.ds(own_half(k), hf)].astype(F32)
        for rel in range(3):
            tot = tot + r2[rel, lo - LATE:lo - LATE + hf].astype(F32)
        ysum[lo - LATE:lo - LATE + hf] = tot.astype(BF)

    def over_chips(k):
        start, lo, hf = at(k)
        n = hf // chips
        out = []
        for off in range(1, chips):
            to = chip_at(off)
            out.append(remote(ysum.at[pl.ds(lo - LATE + to * n, n), :],
                              r3.at[off - 1, pl.ds((lo - LATE) // chips, n), :],
                              s3.at[k, off - 1], q3.at[k, off - 1], dp=to * 2 + core))
        return out

    def chips_sum(k):
        start, lo, hf = at(k)
        n = hf // chips
        tot = ysum[pl.ds(lo - LATE + chip * n, n)].astype(F32)
        for o in range(chips - 1):
            tot = tot + r3[o, (lo - LATE) // chips:(lo - LATE) // chips + n].astype(F32)
        full[pl.ds(own_half(k) + chip * n, n)] = tot.astype(BF)

    def chips_first(k):
        start, lo, hf = at(k)
        n = hf // chips
        out = []
        for off in range(1, chips):
            to = chip_at(off)
            out.append(remote(g.at[:, pl.ds(own_half(k) + to * n, n), :],
                              rx.at[off - 1, :, pl.ds(lo // chips, n), :],
                              s3.at[k, off - 1], q3.at[k, off - 1], dp=to * 2 + core))
        return out

    def chips_first_sum(k):
        start, lo, hf = at(k)
        n = hf // chips
        rows = pl.ds(own_half(k) + chip * n, n)
        for a in range(NT):
            tot = g[a, rows].astype(F32)
            for o in range(chips - 1):
                tot = tot + rx[o, a, lo // chips:lo // chips + n].astype(F32)
            ry[3, a, lo // chips:lo // chips + n] = tot.astype(BF)

    def tensor_second(k):
        start, lo, hf = at(k)
        n = hf // chips
        out = []
        for off in (1, 2, 3):
            to = lax.rem(t + off, NT)
            out.append(remote(ry.at[3, to, pl.ds(lo // chips, n), :], ry.at[off - 1, 0, pl.ds(lo // chips, n), :],
                              s2.at[k, off - 1], q2.at[k, off - 1], tensor=to))
        return out

    def tensor_second_sum(k):
        start, lo, hf = at(k)
        n = hf // chips
        tot = ry[3, t, lo // chips:lo // chips + n].astype(F32)
        for o in range(3):
            tot = tot + ry[o, 0, lo // chips:lo // chips + n].astype(F32)
        full[pl.ds(own_half(k) + chip * n, n)] = tot.astype(BF)

    def spread(k):
        start, lo, hf = at(k)
        n = hf // chips
        mine = full.at[pl.ds(own_half(k) + chip * n, n), :]
        return [remote(mine, mine, s4.at[k, off - 1], q4.at[k, off - 1], dp=chip_at(off) * 2 + core)
                for off in range(1, chips)]

    def hand(k):
        start, lo, hf = at(k)
        mine = full.at[pl.ds(own_half(k), hf), :]
        return [remote(mine, mine, s5.at[k], q5.at[k], dp=sib)]

    def go(cs):
        for c in cs:
            c.start()

    def come(cs):
        for c in cs:
            c.wait_recv()

    def gone(cs):
        for c in cs:
            c.wait_send()

    def all_pairs(k):
        for a in range(NT):
            pair(k, a).start()

    def all_pairs_sum(k):
        for a in range(NT):
            pair(k, a).wait_recv()
            pair_sum(k, a)

    def spread_chunk(k):
        come(spread(k))
        go(hand(k))

    @pl.loop(0, NT)
    def _(a):
        for r in range(R):
            gp[r, a] = (dot_nt(dab[r], wdown[a]) * gp[r, a].astype(F32)).astype(BF)
        wd = dot_tn(act[0, a], dab[0]) + dot_tn(act[1, a], dab[1])
        wu = dot_tn(hb[0], gp[0, a]) + dot_tn(hb[1], gp[1, a])
        for j in range(4):
            g[a, G_DOWN + D * j:G_DOWN + D * (j + 1)] = wd[:, 128 * j:128 * j + 128].astype(BF)
            g[a, G_UP + D * j:G_UP + D * (j + 1)] = wu[:, 128 * j:128 * j + 128].astype(BF)

        @pl.when(jnp.logical_or(is_dec, a != t))
        def _():
            pair(C_DOWN, a).start()
            pair(C_UP, a).start()

    @pl.loop(0, R)
    def _(r):
        d = d32[r]
        for a in range(NT):
            d = d + dot_nt(gp[r, a], wup[a])
        d32[r] = d

    dkv_copies = [
        remote(dkvm_s.at[b], dkvm_r.at[t], dsend.at[b], drecv.at[t], section=other, tensor=b) for b in range(NT)
    ]

    def cross_backward():
        wc0 = full_cross(0)
        wc1 = full_cross(1)

        @pl.loop(0, R)
        def _(r):
            dy = d32[r]
            add_norm(1, xh2[r], dy)
            d2 = norm_back(xh2[r], rs2[r], g_row(1), dy)
            d32[r] = d2
            dcb = d2.astype(BF)
            dab[r] = dcb
            dc = dot(dcb, wc1).astype(BF)
            p = cpt[r].astype(F32).reshape(8, MP, T)
            dp_ = dot_nt(vblk[r], dc).reshape(8, MP, T)
            ds = p * (dp_ - jnp.sum(p * dp_, axis=1, keepdims=True))
            ds = ds.reshape(256, T).astype(BF)
            dk = dot(ds, cq[r])
            dv = dot(cpt[r], dc)
            rows = pl.ds(pl.multiple_of(r * MP, MP), MP)
            for a in range(NT):
                for j, val in ((0, dk), (1, dv)):
                    dkvm_s[a, j, rows] = jnp.where(
                        low_m, val[64 * a:64 * a + MP, 128 * a:128 * a + 128],
                        val[64 * a + MP:64 * a + 2 * MP, 128 * a:128 * a + 128])
            dq = (dot_tn(ds, kblk[r]) * SCALE).astype(BF)
            cq[r] = dq

        for c in dkv_copies:
            c.start()

        gq = dot_tn(h1b[0], cq[0]) + dot_tn(h1b[1], cq[1])
        go_ = dot_tn(dab[0], cctx[0]) + dot_tn(dab[1], cctx[1])
        for a in range(NT):
            g[a, G_CROSS:G_CROSS + D] = gq[:, 128 * a:128 * a + 128].astype(BF)
            g[a, G_CROSS + D:G_CROSS + 2 * D] = go_[:, 128 * a:128 * a + 128].astype(BF)
        all_pairs(C_CROSS)

        @pl.loop(0, R)
        def _(r):
            d32[r] += dot_nt(cq[r], wc0)

        for k in (C_DOWN, C_UP):
            all_pairs_sum(k)
            go(chips_first(k))

    @pl.when(is_dec)
    def _():
        cross_backward()

    @pl.loop(0, R)
    def _(r):
        dy = d32[r]
        add_norm(0, xh1[r], dy)
        d1 = norm_back(xh1[r], rs1[r], g_row(0), dy)
        d32[r] = d1
        db = d1.astype(BF)
        dab[r] = db
        drr = dot_nt(db, w_out_full()).astype(BF)
        for a in range(NT):
            dr[r, a] = drr[:, 128 * a:128 * a + 128]

    wo_all = dot_tn(wide(ctx, 0), dab[0]) + dot_tn(wide(ctx, 1), dab[1])
    for a in range(NT):
        for j in range(4):
            g[a, G_OUT + 128 * j:G_OUT + 128 * j + 128] = (
                wo_all[128 * a:128 * a + 128, 128 * j:128 * j + 128].astype(BF))

    def out_pairs(a):
        @pl.when(jnp.logical_or(is_dec, a != t))
        def _():
            pair(C_OUT, a).start()

    for a in range(NT):
        out_pairs(a)

    def attend_back(a, r, width, encoder):
        dk = jnp.zeros((width, 128), F32)
        dv = jnp.zeros((width, 128), F32)
        dqs = []
        kt = kk[a, r, 0:width].astype(F32).T.astype(BF)
        for h in range(2):
            q_h = qs[a, r] * hmask[h]
            dr_h = dr[r, a] * hmask[h]
            pb = pt[a, r, h, 0:width]
            p = pb.astype(F32)
            dp_ = dot_nt(vv[a, r, 0:width], dr_h)
            ds = (p * (dp_ - jnp.sum(p * dp_, axis=0, keepdims=True))).astype(BF)
            dqs.append(dot(kt[h * 64:h * 64 + 64], ds))
            dk = dk + dot(ds, q_h)
            dv = dv + dot(pb, dr_h)
        act[r, a, :, 0:128] = (jnp.concatenate(dqs, axis=0).T * SCALE).astype(BF)
        for j, val in ((0, dk), (1, dv)):
            dkv[a, r, j] = val[0:T]
            halo_s[0, a, r, j] = val[T:T + HALO].astype(BF)
            if encoder:
                halo_s[1, a, r, j] = val[T + HALO:T + 2 * HALO].astype(BF)
                memd_s[a, r, j] = val[MEM_AT:MEM_AT + MP].astype(BF)

    def halo_copies(a):
        return (remote(halo_s.at[0, a], halo_r.at[0, a], hsend.at[0, a], hrecv.at[0, a], tensor=left),
                remote(halo_s.at[1, a], halo_r.at[1, a], hsend.at[1, a], hrecv.at[1, a], tensor=right))

    first = jnp.where(t == 0, 1.0, 0.0)
    dq_copy = remote(ex_dq.at[t], ex_dq.at[t], qsend.at[0], qrecv.at[t], tensor=0)

    def add_g(start, val):
        n = val.shape[0]
        g[t, start:start + n] = (g[t, start:start + n].astype(F32) + val).astype(BF)

    def add_norm_m(at_, xh, dy):
        ng[at_:at_ + 1] += first * jnp.sum(dy * xh, axis=0, keepdims=True)
        ng[at_ + 3:at_ + 4] += first * jnp.sum(dy, axis=0, keepdims=True)

    def mem_back_first():
        for b in range(NT):
            remote(dkvm_s.at[b], dkvm_r.at[b], dsend.at[b], drecv.at[b], section=other, tensor=b).wait_recv()
        grads = []
        for j in range(2):
            tot = dkvm_r[0, j] + dkvm_r[1, j] + dkvm_r[2, j] + dkvm_r[3, j]
            grads.append(tot.astype(BF))
        ex_m[t] = (dot_nt(grads[0], wcross[t, 0]) + dot_nt(grads[1], wcross[t, 1])).astype(BF)
        ex_start(3)
        for j in range(2):
            g[t, G_CROSS + D * j:G_CROSS + D * j + D] = dot_tn(mm[...], grads[j]).astype(BF)
        pair(C_CROSS, t).start()

    def mem_back_second():
        ex_wait(3)
        dm = ex_m[0].astype(F32)
        for s in range(1, NT):
            dm = dm + ex_m[s].astype(F32)
        add_norm_m(2, mx3[...], dm)
        rows_m = lax.broadcasted_iota(jnp.int32, (R * MP, D), 0)

        @pl.when(t == 0)
        def _():
            mem_local[1].wait()

        @pl.when(t > 0)
        def _():
            mem_c[0].wait_recv()

        cm = jnp.concatenate([cotm[0], cotm[1]], axis=0)
        cm = jnp.where(lax.rem(rows_m, MP) < MEM, cm, 0.0)
        dy = cm + norm_back(mx3[...], mr3[...], g_row(2), dm)
        add_norm_m(1, mx2[...], dy)
        d3 = norm_back(mx2[...], mr2[...], g_row(1), dy)
        md[...] = d3
        d3b = d3.astype(BF)
        dum = (dot_nt(d3b, wdown[t]) * mgp[...]).astype(BF)
        ex_h[t] = dot_nt(dum, wup[t]).astype(BF)
        ex_start(4)
        wd = dot_tn(mact[...], d3b)
        wu = dot_tn(mh[...].astype(BF), dum)
        for j in range(4):
            add_g(G_DOWN + D * j, wd[:, 128 * j:128 * j + 128])
            add_g(G_UP + D * j, wu[:, 128 * j:128 * j + 128])
        pair(C_DOWN, t).start()
        pair(C_UP, t).start()

    def mem_back_third():
        ex_wait(4)
        d2 = md[...]
        for s in range(NT):
            d2 = d2 + ex_h[s].astype(F32)
        add_norm_m(0, mx1[...], d2)
        d1 = norm_back(mx1[...], mr1[...], g_row(0), d2)
        md[...] = d1
        d1b = d1.astype(BF)
        drm = dot_nt(d1b, w_out_full()).astype(BF).astype(F32)
        mh[...] = drm
        prod = drm * mc[...]
        for r in range(R):
            acc = jnp.zeros((MP, 128), F32)
            for hh in range(8):
                cols = prod[r * MP:r * MP + MP, (hh // 2) * 128:(hh // 2) * 128 + 128]
                cols = jnp.where(low_m if hh % 2 == 0 else jnp.logical_not(low_m), cols, 0.0)
                acc = jnp.where(lane_m == hh, jnp.sum(cols, axis=1, keepdims=True), acc)
            mst[1, r * MP:r * MP + MP] = acc
        for a in range(NT):
            @pl.when(t == a)
            def _():
                wo = dot_tn(mc[:, 128 * a:128 * a + 128].astype(BF), d1b)
                for j in range(4):
                    add_g(G_OUT + 128 * j, wo[:, 128 * j:128 * j + 128])
        pair(C_OUT, t).start()

    def mem_attend_back():
        for a in range(NT):
            for r in range(R):
                rows = slice(r * MP, r * MP + MP)
                lse = mst[0, rows]
                dlt = mst[1, rows]
                lse = jnp.concatenate([lse[:, 2 * a:2 * a + 1], lse[:, 2 * a + 1:2 * a + 2]], axis=0)
                dlt = jnp.concatenate([dlt[:, 2 * a:2 * a + 1], dlt[:, 2 * a + 1:2 * a + 2]], axis=0)
                lhs = qm[a, r]
                ko, vo = kk[a, r, 0:T], vv[a, r, 0:T]
                p = jnp.exp(dot_nt(lhs, ko) - lse)
                dra = mh[rows, 128 * a:128 * a + 128]
                dra = jnp.concatenate([jnp.where(low_m, dra, 0.0), jnp.where(low_m, 0.0, dra)], axis=0).astype(BF)
                ds = (p * (dot_nt(dra, vo) - dlt)).astype(BF)
                dq = dot(ds, ko)
                ex_dq[t, a, rows] = (jnp.where(low_m, dq[0:MP], dq[MP:2 * MP]) * SCALE).astype(BF)
                dkv[a, r, 0] += dot_tn(ds, lhs)
                dkv[a, r, 1] += dot_tn(p.astype(BF), dra)

        @pl.when(t > 0)
        def _():
            dq_copy.start()

    @pl.loop(0, NT * R)
    def _(i):
        a = lax.div(i, 2)
        r = lax.rem(i, 2)

        @pl.when(is_enc)
        def _():
            attend_back(a, r, W_ENC, True)

        @pl.when(is_dec)
        def _():
            attend_back(a, r, W_DEC, False)

        @pl.when(r == 1)
        def _():
            to_left, to_right = halo_copies(a)
            to_left.start()

            @pl.when(is_enc)
            def _():
                to_right.start()

        @pl.when(is_dec)
        def _():
            @pl.when(i == 1)
            def _():
                all_pairs_sum(C_CROSS)
                for off in (1, 2, 3):
                    over_tensor(C_CROSS, lax.rem(t + off, NT)).start()
                all_pairs_sum(C_OUT)
                for off in (1, 2, 3):
                    over_tensor(C_OUT, lax.rem(t + off, NT)).start()

        @pl.when(is_enc)
        def _():
            @pl.when(i == 2)
            def _():
                mem_back_first()

            @pl.when(i == 4)
            def _():
                mem_back_second()

            @pl.when(i == 6)
            def _():
                for k in (C_DOWN, C_UP):
                    all_pairs_sum(k)
                    go(chips_first(k))
                mem_back_third()

    to_first = remote(memd_s, memd_r.at[t], gsend.at[0], grecv.at[t], tensor=0)

    n1 = [remote(ny.at[t], ny.at[t], ns.at[o - 1], nq.at[o - 1], tensor=lax.rem(t + o, NT)) for o in (1, 2, 3)]
    n2 = [remote(nc.at[0], nc.at[1], ns.at[3], nq.at[3], dp=sib)]
    n3 = [remote(nx.at[chip], nx.at[chip], ns.at[3 + o], nq.at[3 + o], dp=chip_at(o) * 2 + core)
          for o in range(1, chips)]

    def mem_last():
        @pl.when(t > 0)
        def _():
            to_first.start()

        mem_attend_back()
        all_pairs_sum(C_OUT)
        for off in (1, 2, 3):
            over_tensor(C_OUT, lax.rem(t + off, NT)).start()
        pair(C_CROSS, t).wait_recv()
        pair_sum(C_CROSS, t)
        start, lo, hf = at(C_CROSS)
        ysum[lo - LATE:lo - LATE + hf] = g[t, pl.ds(own_half(C_CROSS), hf)]
        go(over_chips(C_CROSS))

        @pl.when(t == 0)
        def _():
            for r in range(R):
                d32[r, 0:MP] += md[r * MP:r * MP + MP]
            for s in range(1, NT):
                remote(memd_s, memd_r.at[s], gsend.at[0], grecv.at[s], tensor=0).wait_recv()
                remote(ex_dq.at[s], ex_dq.at[s], qsend.at[0], qrecv.at[s], tensor=0).wait_recv()
            for a in range(NT):
                for r in range(R):
                    rows = slice(r * MP, r * MP + MP)
                    for j in range(2):
                        tot = memd_s[a, r, j].astype(F32)
                        for s in range(1, NT):
                            tot = tot + memd_r[s, a, r, j].astype(F32)
                        dkv[a, r, j, 0:MP] += tot
                    tot = ex_dq[0, a, rows].astype(F32)
                    for s in range(1, NT):
                        tot = tot + ex_dq[s, a, rows].astype(F32)
                    act[r, a, 0:MP, 0:128] = (act[r, a, 0:MP, 0:128].astype(F32) + tot).astype(BF)

    ny[t] = ng[...]

    @pl.when(is_dec)
    def _():
        go(n1)

    @pl.when(is_enc)
    def _():
        go(n1)
        mem_last()

    @pl.loop(0, NT)
    def _(i):
        a = lax.rem(t + jnp.where(i == 0, 2, jnp.where(i == 1, 3, jnp.where(i == 2, 1, 0))), NT)
        to_left, to_right = halo_copies(a)
        to_left.wait_recv()

        @pl.when(is_enc)
        def _():
            to_right.wait_recv()

        for r in range(R):
            for j in range(2):
                dkv[a, r, j, T - HALO:T] += halo_r[0, a, r, j].astype(F32)

                @pl.when(is_enc)
                def _():
                    dkv[a, r, j, 0:HALO] += halo_r[1, a, r, j].astype(F32)

                act[r, a, :, 128 * (j + 1):128 * (j + 2)] = dkv[a, r, j].astype(BF)
        gw = dot_tn(x_ext[0, 0:T], act[0, a, :, 0:384]) + dot_tn(x_ext[1, 0:T], act[1, a, :, 0:384])
        for j in range(3):
            g[a, G_QKV + D * j:G_QKV + D * j + D] = gw[:, 128 * j:128 * j + 128].astype(BF)
        pair(C_QKV, a).start()
        wfull = jnp.concatenate([wqkv[a, j] for j in range(3)], axis=1)
        for r in range(R):
            d32[r] += dot_nt(act[r, a, :, 0:384], wfull)
        pair(C_QKV, a).wait_recv()
        pair_sum(C_QKV, a)

        @pl.when(a != t)
        def _():
            over_tensor(C_QKV, a).start()

    dx_copy = pltpu.make_async_copy(d32, dx_out, lsem.at[10])
    dx_copy.start()

    come(n1)
    nc[0] = ny[0] + ny[1] + ny[2] + ny[3]
    go(n2)
    for k in (C_DOWN, C_UP):
        come(chips_first(k))
        chips_first_sum(k)
        go(tensor_second(k))
    come(n2)
    nx[chip] = nc[0] + nc[1]
    go(n3)

    @pl.when(is_dec)
    def _():
        for rel in range(3):
            from_tensor(C_CROSS, rel).wait_recv()
        tensor_sum(C_CROSS)
        go(over_chips(C_CROSS))

    for rel in range(3):
        from_tensor(C_OUT, rel).wait_recv()
    tensor_sum(C_OUT)
    go(over_chips(C_OUT))
    for k in (C_DOWN, C_UP):
        come(tensor_second(k))
        tensor_second_sum(k)
        go(spread(k))
    for rel in range(3):
        from_tensor(C_QKV, rel).wait_recv()
    tensor_sum(C_QKV)
    go(over_chips(C_QKV))
    for k in (C_CROSS, C_OUT):
        come(over_chips(k))
        chips_sum(k)
        go(spread(k))
    come(n3)
    tot_n = nx[0]
    for o in range(1, chips):
        tot_n = tot_n + nx[o]
    ng_tot[...] = tot_n
    for k in (C_DOWN, C_UP):
        spread_chunk(k)
    come(over_chips(C_QKV))
    chips_sum(C_QKV)
    go(spread(C_QKV))
    for k in (C_CROSS, C_OUT, C_QKV):
        spread_chunk(k)
    for k in range(5):
        come(hand(k))

    y_copy.wait()
    dx_copy.wait()
    for i in (QKV, OUT, UP, DOWN):
        gone(copies[i])
    x_right.wait_send()
    for a in range(NT):
        halo_copies(a)[0].wait_send()
    gone(n1)
    gone(n2)
    gone(n3)
    for k in range(5):
        if k in (C_DOWN, C_UP):
            gone(chips_first(k))
            gone(tensor_second(k))
        else:
            gone(over_chips(k))
        if k != C_CROSS:
            for a in range(NT):
                pair(k, a).wait_send()
        gone(spread(k))
        gone(hand(k))
    for k in (C_OUT, C_QKV):
        for rel in range(3):
            from_tensor(k, rel).wait_send()

    @pl.when(is_dec)
    def _():
        gone(copies[CROSS])
        gone(dkv_copies)
        for a in range(NT):
            pair(C_CROSS, a).wait_send()
        for rel in range(3):
            from_tensor(C_CROSS, rel).wait_send()

    @pl.when(is_enc)
    def _():
        x_left.wait_send()
        pair(C_CROSS, t).wait_send()
        for a in range(NT):
            halo_copies(a)[1].wait_send()
        for e in range(5):
            gone(exchanges[e])
        gone(kv_copies)

        @pl.when(t == 0)
        def _():
            gone(mem_x)
            gone(mem_c)

        @pl.when(t > 0)
        def _():
            to_first.wait_send()
            dq_copy.wait_send()


def layer_call(chips, lens, x, cot, wqkv, wout, wcross, wup, wdown, gain, bias):
    any_ = pl.BlockSpec(memory_space=pl.ANY)
    vmem = pl.BlockSpec(memory_space=pltpu.VMEM)
    M = R * MP
    W = W_ENC
    S = pltpu.SemaphoreType.DMA
    C = len(CHUNKS)
    o = max(chips - 1, 1)
    late = HALF - LATE

    def V(shape, kind):
        return pltpu.VMEM(shape, kind)

    scratch = dict(
        x_ext=V((R, W, D), BF), cotm=V((R, MP, D), F32), d32=V((R, T, D), F32),
        wqkv=V((NT, 3, D, 128), BF), wout=V((NT, 128, D), BF), wcross=V((NT, 2, D, 128), BF),
        wup=V((NT, D, D), BF), wdown=V((NT, D, D), BF),
        kk=V((NT, R, W, 128), BF), vv=V((NT, R, W, 128), BF), vt=V((NT, R, 128, W), BF),
        qs=V((NT, R, T, 128), BF), pt=V((NT, R, 2, W, T), BF), ctx=V((R, NT, T, 128), BF),
        mask=V((R, W, T), F32), hmask=V((2, T, 128), BF),
        xh1=V((R, T, D), F32), xh2=V((R, T, D), F32), rs1=V((R, T, 1), F32), rs2=V((R, T, 1), F32),
        h32=V((R, T, D), F32), hb=V((R, T, D), BF), h1b=V((R, T, D), BF),
        act=V((R, NT, T, D), BF), gp=V((R, NT, T, D), BF), dab=V((R, T, D), BF), dr=V((R, NT, T, 128), BF),
        dkv=V((NT, R, 2, T, 128), F32), halo_s=V((2, NT, R, 2, HALO, 128), BF),
        halo_r=V((2, NT, R, 2, HALO, 128), BF), memd_s=V((NT, R, 2, MP, 128), BF),
        memd_r=V((NT, NT, R, 2, MP, 128), BF),
        ex_o=V((NT, NT, M, 128), BF), ex_st=V((NT, M, 128), F32), ex_f=V((NT, M, D), BF), ex_m=V((NT, M, D), BF),
        ex_h=V((NT, M, D), BF), ex_dq=V((NT, NT, M, 128), BF), qm=V((NT, R, 2 * MP, 128), BF),
        kvm=V((NT, 2, M, 128), BF), dkvm_s=V((NT, 2, M, 128), F32), dkvm_r=V((NT, 2, M, 128), F32),
        kblk=V((R, 256, D), BF), vblk=V((R, 256, D), BF), cpt=V((R, 256, T), BF), cq=V((R, T, D), BF),
        cctx=V((R, T, D), BF),
        mx1=V((M, D), F32), mx2=V((M, D), F32), mx3=V((M, D), F32), mr1=V((M, 1), F32), mr2=V((M, 1), F32),
        mr3=V((M, 1), F32), mh=V((M, D), F32), mact=V((M, D), BF), mgp=V((M, D), F32), mc=V((M, D), F32),
        mm=V((M, D), BF), mst=V((2, M, 128), F32), md=V((M, D), F32),
        g=V((NT, G_ROWS, 128), BF), r1=V((NT, HALF, 128), BF), r2=V((3, late, 128), BF),
        r3=V((o, late // chips, 128), BF), rx=V((o, NT, LATE // chips, 128), BF), ry=V((4, NT, LATE // chips, 128), BF),
        ysum=V((late, 128), BF), ng=V((8, D), F32), ny=V((NT, 8, D), F32), nc=V((2, 8, D), F32),
        nx=V((chips, 8, D), F32),
        lsem=S((11,)), wsend=S((5, 7)), wrecv=S((5, 7)), xsend=S((2,)), xrecv=S((2,)), msend=S((2, 3)), mrecv=S((2,)),
        esend=S((5, 3)), erecv=S((5, 3)), ksend=S((NT,)), krecv=S((NT,)), dsend=S((NT,)), drecv=S((NT,)),
        hsend=S((2, NT)), hrecv=S((2, NT)), gsend=S((1,)), grecv=S((NT,)), qsend=S((1,)), qrecv=S((NT,)),
        s1=S((C, NT)), q1=S((C, NT)), s2=S((C, 3)), q2=S((C, 3)), s3=S((C, o)), q3=S((C, o)),
        s4=S((C, o)), q4=S((C, o)), s5=S((C,)), q5=S((C,)), ns=S((4 + o,)), nq=S((4 + o,)),
    )
    names = tuple(scratch)

    def kernel(*refs):
        layer_kernel(chips, names, *refs)

    return pl.pallas_call(
        kernel,
        out_shape=(
            jax.ShapeDtypeStruct((R, T, D), F32),
            jax.ShapeDtypeStruct((R, T, D), F32),
            jax.ShapeDtypeStruct((G_ROWS, 128), BF),
            jax.ShapeDtypeStruct((8, D), F32),
        ),
        in_specs=[pl.BlockSpec(memory_space=pltpu.SMEM)] + [any_] * 7 + [vmem] * 2,
        out_specs=(any_, any_, vmem, vmem),
        scratch_shapes=list(scratch.values()),
        compiler_params=pltpu.CompilerParams(
            collective_id=0, has_side_effects=True, vmem_limit_bytes=VMEM_BYTES
        ),
        name="layers",
    )(lens, x, cot, wqkv, wout, wcross, wup, wdown, gain, bias)


def finish_kernel(y_in, dx_in, full, ng, y, dx, o_qkv, o_out, o_cross, o_up, o_down, o_gain, o_bias, sems):
    copies = [pltpu.make_async_copy(y_in, y.at[0], sems.at[0]), pltpu.make_async_copy(dx_in, dx.at[0], sems.at[1])]
    for c in copies:
        c.start()
    for j in range(3):
        o_qkv[0, j] = full[G_QKV + D * j:G_QKV + D * j + D].astype(F32)
    for j in range(2):
        o_cross[0, j] = full[G_CROSS + D * j:G_CROSS + D * j + D].astype(F32)
    for j in range(4):
        cols = slice(128 * j, 128 * j + 128)
        o_out[0, :, cols] = full[G_OUT + 128 * j:G_OUT + 128 * j + 128].astype(F32)
        o_up[0, :, cols] = full[G_UP + D * j:G_UP + D * j + D].astype(F32)
        o_down[0, :, cols] = full[G_DOWN + D * j:G_DOWN + D * j + D].astype(F32)
    o_gain[0] = ng[0:3]
    o_bias[0] = ng[3:6]
    for c in copies:
        c.wait()


def finish_call(y, dx, full, ng):
    any_ = pl.BlockSpec(memory_space=pl.ANY)
    vmem = pl.BlockSpec(memory_space=pltpu.VMEM)
    shapes = ((1, R, T, D), (1, R, T, D), (1, 3, D, 128), (1, 128, D), (1, 2, D, 128), (1, D, D), (1, D, D),
              (1, 3, D), (1, 3, D))
    return pl.pallas_call(
        finish_kernel,
        out_shape=tuple(jax.ShapeDtypeStruct(s, F32) for s in shapes),
        in_specs=[any_, any_, vmem, vmem],
        out_specs=(any_, any_) + (vmem,) * 7,
        scratch_shapes=[pltpu.SemaphoreType.DMA((2,))],
        compiler_params=pltpu.CompilerParams(vmem_limit_bytes=32 * 1024 * 1024),
        name="finish",
    )(y, dx, full, ng)


def solution(mesh):
    chips = mesh.shape["dp"] // 2

    def shards(inputs, lengths, w_qkv, w_out, w_cross, w_up, w_down, norm_gain, norm_bias, cotangent):
        y, dx, full, ng = layer_call(
            chips, lengths, inputs[0], cotangent[0], w_qkv[0], w_out[0], w_cross[0], w_up[0], w_down[0],
            norm_gain, norm_bias)
        return finish_call(y, dx, full, ng)

    return jax.shard_map(
        shards,
        mesh=mesh,
        in_specs=(
            P("section", "dp", "tensor", None),
            P("dp", None),
            P("section", None, None, "tensor"),
            P("section", "tensor", None),
            P("section", None, None, "tensor"),
            P("section", None, "tensor"),
            P("section", "tensor", None),
            P("section", None, None),
            P("section", None, None),
            P("section", "dp", "tensor", None),
        ),
        out_specs=(
            P("section", "dp", "tensor", None),
            P("section", "dp", "tensor", None),
            P("section", None, None, "tensor"),
            P("section", "tensor", None),
            P("section", None, None, "tensor"),
            P("section", None, "tensor"),
            P("section", "tensor", None),
            P("section", None, None),
            P("section", None, None),
        ),
        check_vma=False,
    )
```

```python
import jax
import jax.numpy as jnp
from jax import lax
from jax.experimental import pallas as pl
from jax.experimental.pallas import tpu as pltpu
from jax.sharding import PartitionSpec as P

F32 = jnp.float32
BF = jnp.bfloat16
MESH = pl.DeviceIdType.MESH
VMEM_BYTES = 62 * 1024 * 1024

MEM = 20
MP = 32
R = 2
T = 256
HALO = 160
D = 512
NT = 4
LEFT, OWN, RIGHT, MEM_2, W_ENC = 32, 192, 448, 608, 640
W_DEC = RIGHT
WIN_ENC = ((0, 480), (128, 512))
WIN_DEC = ((0, 320), (128, 320))
EPS = 1e-05
FILL = -1e30
SCALE = 0.125

G_DOWN, G_UP, G_CROSS, G_OUT, G_QKV, G_ROWS = 0, 2048, 4096, 5120, 5632, 7168
CHUNKS = ((G_DOWN, 2048), (G_UP, 2048), (G_CROSS, 1024), (G_OUT, 512), (G_QKV, 1536))
C_DOWN, C_UP, C_CROSS, C_OUT, C_QKV = range(5)
LATE = G_CROSS // 2
HALF = G_ROWS // 2
QKV, OUT, CROSS, UP, DOWN = range(5)
W_ROWS = (512, 128, 512, 512, 512)


def dot(a, b):
    return lax.dot_general(a, b, (((1,), (0,)), ((), ())), preferred_element_type=F32)


def dot_nt(a, b):
    return lax.dot_general(a, b, (((1,), (1,)), ((), ())), preferred_element_type=F32)


def dot_tn(a, b):
    return lax.dot_general(a, b, (((0,), (0,)), ((), ())), preferred_element_type=F32)


def remote(src, dst, send, recv, **device):
    return pltpu.make_async_remote_copy(
        src_ref=src, dst_ref=dst, send_sem=send, recv_sem=recv, device_id=device, device_id_type=MESH
    )


def normed(v):
    c = v - jnp.mean(v, axis=1, keepdims=True)
    rs = lax.rsqrt(jnp.mean(c * c, axis=1, keepdims=True) + EPS)
    return c * rs, rs


def norm_back(xhat, rs, gain, dy):
    dxh = dy * gain
    m1 = jnp.mean(dxh, axis=1, keepdims=True)
    m2 = jnp.mean(dxh * xhat, axis=1, keepdims=True)
    return rs * (dxh - m1 - xhat * m2)


def gelu_both(u):
    k = 0.7978845608028654
    u2 = u * u
    th = jnp.tanh(k * u * (1.0 + 0.044715 * u2))
    half = 0.5 * (1.0 + th)
    grad = half + 0.5 * u * (1.0 - th * th) * (k * (1.0 + 3.0 * 0.044715 * u2))
    return u * half, grad


def layer_kernel(chips, names, *refs):
    (lens, x_in, cot_in, wqkv_in, wout_in, wcross_in, wup_in, wdown_in, gain, bias,
     y_out, dx_out, full, ng_tot) = refs[:14]
    m = dict(zip(names, refs[14:]))
    x_ext, cotm, d32, wqkv, wout, wcross, wup, wdown = (
        m[n] for n in ("x_ext", "cotm", "d32", "wqkv", "wout", "wcross", "wup", "wdown"))
    kk, vv, qs, pt, ctx, mask, hmask = (m[n] for n in ("kk", "vv", "qs", "pt", "ctx", "mask", "hmask"))
    xh1, xh2, rs1, rs2, h32, hb, h1b, act, gp, dab, dr = (
        m[n] for n in ("xh1", "xh2", "rs1", "rs2", "h32", "hb", "h1b", "act", "gp", "dab", "dr"))
    dkv, halo_s, halo_r, mg_s, mg_r, dxm_s, dxm_r, mdu = (
        m[n] for n in ("dkv", "halo_s", "halo_r", "mg_s", "mg_r", "dxm_s", "dxm_r", "mdu"))
    ex_o, ex_st, ex_f, ex_m, qm, rq, rqs, rqr = (
        m[n] for n in ("ex_o", "ex_st", "ex_f", "ex_m", "qm", "rq", "rqs", "rqr"))
    kvm, dkvm_s, dkvm_r, kblk, vblk, cpt, cq, cctx = (
        m[n] for n in ("kvm", "dkvm_s", "dkvm_r", "kblk", "vblk", "cpt", "cq", "cctx"))
    mx1, mx2, mx3, mr1, mr2, mr3, mh, mact, mgp, mc, mm, mst, md = (
        m[n] for n in ("mx1", "mx2", "mx3", "mr1", "mr2", "mr3", "mh", "mact", "mgp", "mc", "mm", "mst", "md"))
    g, r1, r2, r3, rx, ry_s, ry_r, zz, ysum, ng, ny, nc, nx, cdb = (
        m[n] for n in ("g", "r1", "r2", "r3", "rx", "ry_s", "ry_r", "zz", "ysum", "ng", "ny", "nc", "nx", "cdb"))
    (lsem, wsend, wrecv, xsend, xrecv, msend, mrecv, esend, erecv, ksend, krecv, dsend, drecv,
     hsend, hrecv, gsend, grecv, qsend, qrecv) = (
        m[n] for n in ("lsem", "wsend", "wrecv", "xsend", "xrecv", "msend", "mrecv", "esend", "erecv", "ksend",
                       "krecv", "dsend", "drecv", "hsend", "hrecv", "gsend", "grecv", "qsend", "qrecv"))
    s1, q1, s2, q2, s3, q3, s4, q4, s5, q5, ns, nq = (
        m[n] for n in ("s1", "q1", "s2", "q2", "s3", "q3", "s4", "q4", "s5", "q5", "ns", "nq"))
    w2send, w2recv, sx, qx, sz, qz, sq, qq = (
        m[n] for n in ("w2send", "w2recv", "sx", "qx", "sz", "qz", "sq", "qq"))

    def g_row(i):
        return gain[i]

    def b_row(i):
        return bias[i]

    sec = lax.axis_index("section")
    dp = lax.axis_index("dp")
    t = lax.axis_index("tensor")
    core = lax.rem(dp, 2)
    chip = lax.div(dp, 2)
    sib = dp + 1 - 2 * core
    is_enc = sec == 0
    is_dec = sec == 1
    left = lax.rem(t + 3, NT)
    right = lax.rem(t + 1, NT)
    opp = lax.rem(t + 2, NT)
    other = 1 - sec
    xi = lax.div(dp, 4)

    def x_dev(off):
        return lax.rem(xi + off, 4) * 4 + lax.rem(dp, 4)

    z_dev = xi * 4 + lax.rem(dp + 2, 4)

    def source(off):
        return lax.rem(t + NT - off, NT)

    def chip_at(off):
        return lax.rem(chip + off, chips)

    ins = (wqkv_in, wout_in, wcross_in, wup_in, wdown_in)
    ws = (wqkv, wout, wcross, wup, wdown)

    def part(i, ref, start, n):
        if i in (QKV, CROSS):
            return ref.at[:, pl.ds(start, n), :]
        return ref.at[pl.ds(start, n), :]

    def slot(i, a, start, n):
        if i in (QKV, CROSS):
            return ws[i].at[a, :, pl.ds(start, n), :]
        return ws[i].at[a, pl.ds(start, n), :]

    barrier = pltpu.get_barrier_semaphore()
    for off in (1, 2, 3):
        pl.semaphore_signal(barrier, inc=1, device_id={"tensor": lax.rem(t + off, NT)}, device_id_type=MESH)
    pl.semaphore_signal(barrier, inc=1, device_id={"dp": sib}, device_id_type=MESH)
    for b in range(NT):
        pl.semaphore_signal(barrier, inc=1, device_id={"section": other, "tensor": b}, device_id_type=MESH)
    for off in range(1, chips):
        pl.semaphore_signal(barrier, inc=1, device_id={"dp": chip_at(off) * 2 + core}, device_id_type=MESH)

    locals_ = [
        pltpu.make_async_copy(x_in, x_ext.at[:, pl.ds(OWN, T), :], lsem.at[0]),
        pltpu.make_async_copy(cot_in, d32, lsem.at[1]),
    ]
    for i in range(5):
        locals_.append(pltpu.make_async_copy(ins[i], ws[i].at[t], lsem.at[2 + i]))
    for c in locals_:
        c.start()

    pl.semaphore_wait(barrier, 8 + chips - 1)

    x_right = remote(x_in.at[:, pl.ds(T - HALO, HALO), :], x_ext.at[:, pl.ds(LEFT, HALO), :],
                     xsend.at[0], xrecv.at[0], tensor=right)
    x_left = remote(x_in.at[:, pl.ds(0, HALO), :], x_ext.at[:, pl.ds(RIGHT, HALO), :],
                    xsend.at[1], xrecv.at[1], tensor=left)
    mem_x, mem_c = [], []
    for off in (1, 2, 3):
        to = lax.rem(t + off, NT)
        mem_x.append(remote(x_in.at[:, pl.ds(0, MP), :], x_ext.at[:, pl.ds(0, MP), :],
                            msend.at[0, off - 1], mrecv.at[0], tensor=to))
        mem_c.append(remote(cot_in.at[:, pl.ds(0, MP), :], cotm, msend.at[1, off - 1], mrecv.at[1], tensor=to))
    mem_local = [
        pltpu.make_async_copy(x_in.at[:, pl.ds(0, MP), :], x_ext.at[:, pl.ds(0, MP), :], lsem.at[7]),
        pltpu.make_async_copy(cot_in.at[:, pl.ds(0, MP), :], cotm, lsem.at[8]),
    ]

    def w_direct(i):
        hf = W_ROWS[i] // 2
        mine = core * hf
        return [remote(part(i, ins[i], mine, hf), slot(i, t, mine, hf), wsend.at[i, off - 1], wrecv.at[i, off - 1],
                       tensor=lax.rem(t + off, NT)) for off in (1, 2, 3)]

    eighth = D // 8
    at_8 = core * (D // 2) + xi * eighth

    def w_eighth(i):
        return [remote(part(i, ins[i], at_8, eighth), slot(i, t, at_8, eighth),
                       wsend.at[i, off - 1], wrecv.at[i, off - 1], tensor=lax.rem(t + off, NT)) for off in (1, 2, 3)]

    def w_along(i):
        out = []
        for off in (1, 2, 3):
            rows = slot(i, source(off), at_8, eighth)
            for xo in (1, 2, 3):
                out.append(remote(rows, rows, w2send.at[i - UP, off - 1, xo - 1], w2recv.at[i - UP, off - 1, xo - 1],
                                  dp=x_dev(xo)))
        return out

    def w_pair(i):
        hf = W_ROWS[i] // 2
        out = []
        for off in (1, 2, 3):
            rows = slot(i, source(off), core * hf, hf)
            out.append(remote(rows, rows, wsend.at[i, 2 + off], wrecv.at[i, 2 + off], dp=sib))
        return out

    def go(cs):
        for c in cs:
            c.start()

    def come(cs):
        for c in cs:
            c.wait_recv()

    def gone(cs):
        for c in cs:
            c.wait_send()

    def arrive(i):
        for c, p in zip(w_direct(i), w_pair(i)):
            c.wait_recv()
            p.start()

    def go_along(i):
        along = w_along(i)
        for off, c in enumerate(w_eighth(i)):
            c.wait_recv()
            go(along[3 * off:3 * off + 3])

    def come_along(i):
        along = w_along(i)
        for off, p in enumerate(w_pair(i)):
            come(along[3 * off:3 * off + 3])
            p.start()

    def ready(i):
        come(w_pair(i))

    @pl.when(is_enc)
    def _():
        @pl.when(t == 0)
        def _():
            go(mem_x + mem_local)

        go(w_direct(QKV))
        x_right.start()
        x_left.start()

    @pl.when(is_dec)
    def _():
        x_right.start()
        go(w_direct(QKV))
        go(w_direct(OUT))
        go(w_eighth(UP))
        go(w_eighth(DOWN))
        go(w_direct(CROSS))

    lane = lax.broadcasted_iota(jnp.int32, (T, 128), 1)
    hmask[0] = jnp.where(lane < 64, 1.0, 0.0).astype(BF)
    hmask[1] = jnp.where(lane < 64, 0.0, 1.0).astype(BF)

    def segments(pos, r):
        off = pos - MEM
        seg = jnp.where(off >= 0, 1, 0)
        end = jnp.int32(0)
        for k in range(16):
            end = end + lens[r, k]
            seg = seg + jnp.where(off >= end, 1, 0)
        return seg

    def make_masks(windows, encoder):
        for r in range(R):
            for b, (w0, wn) in enumerate(windows):
                e = lax.broadcasted_iota(jnp.int32, (wn, 128), 0) + w0
                pos = e - OWN + t * T
                ks = segments(pos, r)
                qpos = lax.broadcasted_iota(jnp.int32, (8, 128), 1) + (t * T + b * 128)
                same = ks == segments(qpos, r)[0:1]
                if encoder:
                    mem_i = jnp.where(e < LEFT, e, jnp.where(e >= MEM_2, e - MEM_2, MEM))
                    ok = jnp.logical_or(mem_i < MEM, jnp.logical_and(
                        jnp.logical_and(e >= LEFT, e < MEM_2), jnp.logical_and(same, ks > 0)))
                else:
                    ok = jnp.logical_and(jnp.logical_and(same, e >= LEFT),
                                         jnp.logical_and(pos <= qpos[0:1], pos >= 0))
                mask[r, b, 0:wn] = jnp.where(ok, 0.0, FILL)

    @pl.when(is_enc)
    def _():
        make_masks(WIN_ENC, True)

    @pl.when(is_dec)
    def _():
        make_masks(WIN_DEC, False)
        x_ext[:, 0:MP] = jnp.zeros((R, MP, D), BF)

    ex_st[t] = jnp.zeros((R * MP, 128), F32)
    ng[...] = jnp.zeros(ng.shape, F32)

    for c in locals_:
        c.wait()

    def shard_at(step):
        return lax.rem(t + jnp.where(step == 0, 0, jnp.where(step == 1, 3, step - 1)), NT)

    lane_m = lax.broadcasted_iota(jnp.int32, (MP, 128), 1)
    low_m = lane_m < 64

    def keys(a, r, lo, hi, wkv):
        kv = dot(x_ext[r, lo:hi], wkv)
        k32, v32 = kv[:, 0:128], kv[:, 128:256]
        kk[a, r, lo:hi] = k32.astype(BF)
        vv[a, r, lo:hi] = v32.astype(BF)

    def keys_weight(a):
        return jnp.concatenate([wqkv[a, 1], wqkv[a, 2]], axis=1)

    def queries(a, r):
        q = dot(x_ext[r, OWN:OWN + T], wqkv[a, 0]).astype(BF)
        q = (q.astype(F32) * SCALE).astype(BF)
        for b in range(2):
            for h in range(2):
                qs[a, r, b, h * 128:h * 128 + 128] = q[b * 128:b * 128 + 128] * hmask[h, 0:128]

    def turned(ref, a, r, hi):
        return ref[a, r, 0:hi].astype(F32).T.astype(BF)

    def project_own(a):
        wkv = keys_weight(a)
        for r in range(R):
            keys(a, r, OWN, OWN + T, wkv)
            queries(a, r)
            m32 = dot(x_ext[r, 0:MP], wqkv[a, 0]).astype(BF).astype(F32) * SCALE
            lhs = jnp.concatenate([jnp.where(low_m, m32, 0.0), jnp.where(low_m, 0.0, m32)], axis=0).astype(BF)
            qm[a, r] = lhs
            s = dot_nt(lhs, kk[a, r, OWN:OWN + T])
            top = jnp.max(s, axis=1, keepdims=True)
            p = jnp.exp(s - top)
            total = jnp.sum(p, axis=1, keepdims=True)
            o = dot(p.astype(BF), vv[a, r, OWN:OWN + T]) / total
            ex_o[t, a, r * MP:r * MP + MP] = jnp.where(low_m, o[0:MP], o[MP:2 * MP]).astype(BF)
            st = ex_st[t, r * MP:r * MP + MP]
            st = jnp.where(lane_m == 2 * a, top[0:MP], st)
            st = jnp.where(lane_m == 2 * a + 1, top[MP:2 * MP], st)
            st = jnp.where(lane_m == 2 * a + 8, total[0:MP], st)
            st = jnp.where(lane_m == 2 * a + 9, total[MP:2 * MP], st)
            ex_st[t, r * MP:r * MP + MP] = st

    def project_rest(a):
        wkv = keys_weight(a)
        for r in range(R):
            keys(a, r, 0, OWN, wkv)
            keys(a, r, RIGHT, W_ENC, wkv)

    def project_all(a):
        wkv = keys_weight(a)
        for r in range(R):
            keys(a, r, 0, W_DEC, wkv)
            queries(a, r)

    def ex_copies(e, buf):
        out = []
        for off in (1, 2, 3):
            out.append(remote(buf.at[t], buf.at[t], esend.at[e, off - 1], erecv.at[e, off - 1],
                              tensor=lax.rem(t + off, NT)))
        return out

    exchanges = [ex_copies(e, buf) for e, buf in enumerate((ex_o, ex_st, ex_f, ex_m))]

    def ex_start(e):
        for c in exchanges[e]:
            c.start()

    def ex_wait(e):
        for c in exchanges[e]:
            c.wait_recv()

    def wide(ref, r):
        return jnp.concatenate([ref[r, a] for a in range(NT)], axis=1)

    def w_out_full():
        return wout[...].reshape(D, D)

    def mem_combine():
        for r in range(R):
            rows = slice(r * MP, r * MP + MP)
            sts = [ex_st[s, rows] for s in range(NT)]
            top = jnp.maximum(jnp.maximum(sts[0], sts[1]), jnp.maximum(sts[2], sts[3]))
            wts = [pltpu.roll(sts[s], 120, 1) * jnp.exp(sts[s] - top) for s in range(NT)]
            total = wts[0] + wts[1] + wts[2] + wts[3]
            total = jnp.where(lane_m < 8, total, 1.0)
            inv = 1.0 / total
            mst[0, rows] = jnp.where(lane_m < 8, top + jnp.log(total), 0.0)
            for a in range(NT):
                acc = jnp.zeros((MP, 128), F32)
                for s in range(NT):
                    w = wts[s] * inv
                    wide_w = jnp.where(low_m, w[:, 2 * a:2 * a + 1], w[:, 2 * a + 1:2 * a + 2])
                    acc = acc + wide_w * ex_o[s, a, rows].astype(F32)
                mc[rows, a * 128:a * 128 + 128] = acc

    def x_mem():
        return jnp.concatenate([x_ext[r, 0:MP] for r in range(R)], axis=0)

    def mem_first():
        mem_combine()
        xm = x_mem().astype(F32)
        xh, rs = normed(xm + dot(mc[...].astype(BF), w_out_full()))
        mx1[...] = xh
        mr1[...] = rs
        h = xh * g_row(0) + b_row(0)
        mh[...] = h
        av, _ = gelu_both(dot(h.astype(BF), wup[t]))
        mact[...] = av.astype(BF)
        ex_f[t] = dot(av.astype(BF), wdown[t]).astype(BF)
        ex_start(2)

    kv_copies = [remote(kvm.at[t], kvm.at[t], ksend.at[b], krecv.at[t], section=other, tensor=b) for b in range(NT)]

    def mem_second():
        third = mh[...]
        for s in range(NT):
            third = third + ex_f[s].astype(F32)
        xh, rs = normed(third)
        mx2[...] = xh
        mr2[...] = rs
        y = xh * g_row(1) + b_row(1)
        md[...] = y
        xh, rs = normed(y)
        mx3[...] = xh
        mr3[...] = rs
        mv = (xh * g_row(2) + b_row(2)).astype(BF)
        mm[...] = mv
        kvm[t, 0] = dot(mv, wcross[t, 0]).astype(BF)
        kvm[t, 1] = dot(mv, wcross[t, 1]).astype(BF)
        for c in kv_copies:
            c.start()

    def attend(a, r, windows):
        v_t = turned(vv, a, r, windows[1][0] + windows[1][1])
        for b, (w0, wn) in enumerate(windows):
            mk = mask[r, b, 0:wn]
            s = dot_nt(kk[a, r, w0:w0 + wn], qs[a, r, b]) + jnp.concatenate([mk, mk], axis=1)
            p = jnp.exp(s - jnp.max(s, axis=0, keepdims=True))
            p = (p * (1.0 / jnp.sum(p, axis=0, keepdims=True))).astype(BF)
            pt[a, r, b, 0:wn] = p
            o = dot(v_t[:, w0:w0 + wn], p)
            o = jnp.concatenate([o[0:64, 0:128], o[64:128, 128:256]], axis=0)
            ctx[r, a, b * 128:b * 128 + 128] = o.T.astype(BF)

    def encoder_attention():
        @pl.when(t == 0)
        def _():
            mem_local[0].wait()

        @pl.when(t > 0)
        def _():
            mem_x[0].wait_recv()

        x_ext[:, MEM_2:MEM_2 + MP] = x_ext[:, 0:MP]

        @pl.loop(0, NT)
        def _(step):
            @pl.when(step == 1)
            def _():
                arrive(QKV)
                ready(QKV)

            project_own(shard_at(step))

        ex_start(0)
        ex_start(1)
        go(w_direct(OUT))
        go(w_eighth(UP))
        x_right.wait_recv()
        x_left.wait_recv()

        @pl.loop(0, NT)
        def _(step):
            project_rest(shard_at(step))

        @pl.loop(0, NT * R)
        def _(i):
            @pl.when(i == 2)
            def _():
                arrive(OUT)
                ex_wait(0)
                ex_wait(1)
                ready(OUT)
                mem_first()
                go(w_eighth(DOWN))
                go_along(UP)

            @pl.when(i == 6)
            def _():
                ex_wait(2)
                mem_second()
                go_along(DOWN)

                @pl.when(t == 0)
                def _():
                    go(mem_c)

            attend(shard_at(lax.div(i, 2)), lax.rem(i, 2), WIN_ENC)

    def decoder_attention():
        x_right.wait_recv()

        @pl.loop(0, NT * R)
        def _(i):
            @pl.when(i == 1)
            def _():
                arrive(QKV)

            @pl.when(i == 2)
            def _():
                ready(QKV)

            step_from = jnp.where(i == 0, 0, jnp.where(i == 2, 1, 4))
            step_to = jnp.where(i == 0, 1, 4)

            @pl.loop(step_from, step_to)
            def _(step):
                project_all(shard_at(step))

            @pl.when(i == 2)
            def _():
                arrive(OUT)
                go_along(UP)

            @pl.when(i == 5)
            def _():
                go_along(DOWN)
                ready(OUT)

            attend(shard_at(lax.div(i, 2)), lax.rem(i, 2), WIN_DEC)

        arrive(CROSS)

    @pl.when(is_enc)
    def _():
        encoder_attention()

    @pl.when(is_dec)
    def _():
        decoder_attention()

    @pl.loop(0, R)
    def _(r):
        a0 = x_ext[r, OWN:OWN + T].astype(F32) + dot(wide(ctx, r), w_out_full())
        xh, rs = normed(a0)
        xh1[r] = xh
        rs1[r] = rs
        h = xh * g_row(0) + b_row(0)
        h32[r] = h
        hb[r] = h.astype(BF)

    come_along(UP)

    pad_mask = jnp.where(
        lax.rem(lax.broadcasted_iota(jnp.int32, (256, T), 0), MP) < MEM, 0.0, FILL)

    def full_cross(j):
        return jnp.concatenate([wcross[a, j] for a in range(NT)], axis=1)

    def cross_forward():
        ready(CROSS)
        wc0 = full_cross(0)
        wc1 = full_cross(1)
        kblk[...] = jnp.zeros(kblk.shape, BF)
        vblk[...] = jnp.zeros(vblk.shape, BF)

        @pl.loop(0, R)
        def _(r):
            h1b[r] = hb[r]
            q = dot(hb[r], wc0).astype(BF)
            cq[r] = (q.astype(F32) * SCALE).astype(BF)

        for b in range(NT):
            remote(kvm.at[b], kvm.at[b], ksend.at[b], krecv.at[b], section=other, tensor=b).wait_recv()
        for r in range(R):
            for a in range(NT):
                for h in range(2):
                    at = slice(a * 64 + h * MP, a * 64 + h * MP + MP)
                    kblk[r, at, a * 128:a * 128 + 128] = kvm[a, 0, r * MP:r * MP + MP] * hmask[h, 0:MP]
                    vblk[r, at, a * 128:a * 128 + 128] = kvm[a, 1, r * MP:r * MP + MP] * hmask[h, 0:MP]

        @pl.loop(0, R)
        def _(r):
            s = dot_nt(kblk[r], cq[r]) + pad_mask
            s = s.reshape(8, MP, T)
            p = jnp.exp(s - jnp.max(s, axis=1, keepdims=True))
            p = p * (1.0 / jnp.sum(p, axis=1, keepdims=True))
            p = p.reshape(256, T).astype(BF)
            cpt[r] = p
            c = dot_tn(p, vblk[r]).astype(BF)
            cctx[r] = c
            xh, rs = normed(h32[r] + dot_nt(c, wc1))
            xh2[r] = xh
            rs2[r] = rs
            h = xh * g_row(1) + b_row(1)
            h32[r] = h
            hb[r] = h.astype(BF)

    @pl.when(is_dec)
    def _():
        cross_forward()

    @pl.loop(0, NT * R)
    def _(i):
        @pl.when(i == 2)
        def _():
            ready(UP)

        a = shard_at(lax.div(i, 2))
        r = lax.rem(i, 2)
        av, gv = gelu_both(dot(hb[r], wup[a]))
        act[r, a] = av.astype(BF)
        gp[r, a] = gv.astype(BF)

    @pl.when(is_enc)
    def _():
        for a in range(NT):
            _, gv = gelu_both(dot(mh[...].astype(BF), wup[a]))
            mgp[a] = gv

    come_along(DOWN)
    ready(DOWN)

    last = jnp.where(is_enc, 1, 2)
    g_last = jnp.where(is_enc, g_row(1), g_row(2))
    b_last = jnp.where(is_enc, b_row(1), b_row(2))

    def add_norm(at, xh, dy):
        ng[pl.ds(at, 1)] += jnp.sum(dy * xh, axis=0, keepdims=True)
        ng[pl.ds(at + 3, 1)] += jnp.sum(dy, axis=0, keepdims=True)

    row_i = lax.broadcasted_iota(jnp.int32, (T, D), 0)
    is_mem_row = jnp.logical_and(row_i < MEM, jnp.logical_and(is_enc, t == 0))

    @pl.loop(0, R)
    def _(r):
        third = h32[r]
        for a in range(NT):
            third = third + dot(act[r, a], wdown[a])
        xh, rs = normed(third)
        h32[r] = xh * g_last + b_last
        dy = jnp.where(is_mem_row, 0.0, d32[r])
        d3 = norm_back(xh, rs, g_last, dy)
        ng[pl.ds(last, 1)] += jnp.sum(dy * xh, axis=0, keepdims=True)
        ng[pl.ds(last + 3, 1)] += jnp.sum(dy, axis=0, keepdims=True)
        d32[r] = d3
        dab[r] = d3.astype(BF)

    @pl.when(jnp.logical_and(is_enc, t == 0))
    def _():
        for r in range(R):
            h32[r, 0:24] = jnp.where(
                lax.broadcasted_iota(jnp.int32, (24, D), 0) < MEM, md[r * MP:r * MP + 24], h32[r, 0:24])

    y_copy = pltpu.make_async_copy(h32, y_out, lsem.at[9])
    y_copy.start()

    def at(k):
        return CHUNKS[k][0], CHUNKS[k][0] // 2, CHUNKS[k][1] // 2

    def own_half(k):
        start, lo, hf = at(k)
        return start + core * hf

    def shard_of(q):
        return lax.rem(t + 1 + q, NT)

    def rel_of(a):
        return lax.rem(a - t + 3, NT)

    def pair(k, q):
        start, lo, hf = at(k)
        return remote(g.at[q, pl.ds(start + (1 - core) * hf, hf), :], r1.at[q, pl.ds(lo, hf), :],
                      s1.at[k, q], q1.at[k, q], dp=sib)

    def pair_sum(k, q):
        start, lo, hf = at(k)
        rows = pl.ds(own_half(k), hf)
        g[q, rows] = (g[q, rows].astype(F32) + r1[q, lo:lo + hf].astype(F32)).astype(BF)

    def over_tensor(k, q):
        start, lo, hf = at(k)
        return remote(g.at[q, pl.ds(own_half(k), hf), :], r2.at[q, pl.ds(lo - LATE, hf), :],
                      s2.at[k, q], q2.at[k, q], tensor=shard_of(q))

    def tensor_sum(k):
        start, lo, hf = at(k)
        tot = g[3, pl.ds(own_half(k), hf)].astype(F32)
        for rel in range(3):
            tot = tot + r2[rel, lo - LATE:lo - LATE + hf].astype(F32)
        ysum[lo - LATE:lo - LATE + hf] = tot.astype(BF)

    def over_chips(k):
        start, lo, hf = at(k)
        n = hf // chips
        out = []
        for off in range(1, chips):
            to = chip_at(off)
            out.append(remote(ysum.at[pl.ds(lo - LATE + to * n, n), :],
                              r3.at[off - 1, pl.ds((lo - LATE) // chips, n), :],
                              s3.at[k, off - 1], q3.at[k, off - 1], dp=to * 2 + core))
        return out

    def chips_sum(k):
        start, lo, hf = at(k)
        n = hf // chips
        tot = ysum[pl.ds(lo - LATE + chip * n, n)].astype(F32)
        for o in range(chips - 1):
            tot = tot + r3[o, (lo - LATE) // chips:(lo - LATE) // chips + n].astype(F32)
        full[pl.ds(own_half(k) + chip * n, n)] = tot.astype(BF)

    def chips_first(k, q):
        start, lo, hf = at(k)
        n = hf // chips
        out = []
        for off in range(1, chips):
            to = chip_at(off)
            out.append(remote(g.at[q, pl.ds(own_half(k) + to * n, n), :], rq.at[off - 1, q],
                              sq.at[q, off - 1], qq.at[q, off - 1], dp=to * 2 + core))
        return out

    def chips_first_sum(k, q):
        start, lo, hf = at(k)
        n = hf // chips
        tot = g[q, pl.ds(own_half(k) + chip * n, n)].astype(F32)
        for o in range(chips - 1):
            tot = tot + rq[o, q].astype(F32)
        rqs[q] = tot.astype(BF)

    def tensor_third(k):
        return [remote(rqs.at[q], rqr.at[q], s2.at[k, q], q2.at[k, q], tensor=shard_of(q)) for q in range(3)]

    def tensor_third_sum(k):
        start, lo, hf = at(k)
        n = hf // chips
        tot = rqs[3].astype(F32)
        for q in range(3):
            tot = tot + rqr[q].astype(F32)
        full[pl.ds(own_half(k) + chip * n, n)] = tot.astype(BF)

    quarter = LATE // 8

    def along_x(k, own):
        some = pl.ds(3, 1) if own else pl.ds(0, 3)
        out = []
        for off in (1, 2, 3):
            to = lax.rem(xi + off, 4)
            out.append(remote(g.at[some, pl.ds(own_half(k) + to * quarter, quarter), :],
                              rx.at[off - 1, some, pl.ds(k * quarter, quarter), :],
                              sx.at[k, int(own), off - 1], qx.at[k, int(own), off - 1], dp=x_dev(off)))
        return out

    def along_x_sum(k, q):
        rows = slice(k * quarter, (k + 1) * quarter)
        tot = g[q, pl.ds(own_half(k) + xi * quarter, quarter)].astype(F32)
        for o in range(3):
            tot = tot + rx[o, q, rows].astype(F32)
        ry_s[q, rows] = tot.astype(BF)

    def tensor_second(k):
        rows = pl.ds(k * quarter, quarter)
        return [remote(ry_s.at[q, rows, :], ry_r.at[q, rows, :], s2.at[k, q], q2.at[k, q], tensor=shard_of(q))
                for q in range(3)]

    def tensor_second_sum(k):
        rows = slice(k * quarter, (k + 1) * quarter)
        tot = ry_s[3, rows].astype(F32)
        for q in range(3):
            tot = tot + ry_r[q, rows].astype(F32)
        zz[0, rows] = tot.astype(BF)

    def over_z(k):
        rows = pl.ds(k * quarter, quarter)
        return [remote(zz.at[0, rows, :], zz.at[1, rows, :], sz.at[k], qz.at[k], dp=z_dev)]

    def over_z_sum(k):
        rows = slice(k * quarter, (k + 1) * quarter)
        full[pl.ds(own_half(k) + xi * quarter, quarter)] = (zz[0, rows].astype(F32) + zz[1, rows].astype(F32)).astype(BF)

    def spread_x(k):
        mine = full.at[pl.ds(own_half(k) + xi * quarter, quarter), :]
        return [remote(mine, mine, s4.at[k, off - 1], q4.at[k, off - 1], dp=x_dev(off)) for off in (1, 2, 3)]

    def spread(k):
        start, lo, hf = at(k)
        n = hf // chips
        mine = full.at[pl.ds(own_half(k) + chip * n, n), :]
        return [remote(mine, mine, s4.at[k, off - 1], q4.at[k, off - 1], dp=chip_at(off) * 2 + core)
                for off in range(1, chips)]

    def hand(k):
        start, lo, hf = at(k)
        mine = full.at[pl.ds(own_half(k), hf), :]
        return [remote(mine, mine, s5.at[k], q5.at[k], dp=sib)]

    def all_pairs(k):
        for q in range(NT):
            pair(k, q).start()

    def all_pairs_sum(k, some=range(NT)):
        for q in some:
            pair(k, q).wait_recv()
            pair_sum(k, q)

    def put_feed(k, q, w):
        for j in range(4):
            g[q, CHUNKS[k][0] + D * j:CHUNKS[k][0] + D * (j + 1)] = w[:, 128 * j:128 * j + 128].astype(BF)

        @pl.when(jnp.logical_or(is_dec, q < 3))
        def _():
            pair(k, q).start()

    @pl.loop(0, NT)
    def _(q):
        a = shard_of(q)
        put_feed(C_DOWN, q, dot_tn(act[0, a], dab[0]) + dot_tn(act[1, a], dab[1]))

    @pl.loop(0, R)
    def _(r):
        d = d32[r]
        for a in range(NT):
            du = (dot_nt(dab[r], wdown[a]) * gp[r, a].astype(F32)).astype(BF)
            gp[r, a] = du
            d = d + dot_nt(du, wup[a])
        d32[r] = d

    def feed_on(k):
        all_pairs_sum(k, range(3))
        go(along_x(k, False))

        @pl.when(is_dec)
        def _():
            all_pairs_sum(k, (3,))
            go(along_x(k, True))

    feed_on(C_DOWN)

    dkv_copies = [
        remote(dkvm_s.at[b], dkvm_r.at[t], dsend.at[b], drecv.at[t], section=other, tensor=b) for b in range(NT)
    ]

    def cross_backward():
        wc0 = full_cross(0)
        wc1 = full_cross(1)

        @pl.loop(0, R)
        def _(r):
            dy = d32[r]
            add_norm(1, xh2[r], dy)
            d2 = norm_back(xh2[r], rs2[r], g_row(1), dy)
            d32[r] = d2
            dcb = d2.astype(BF)
            cdb[r] = dcb
            dc = dot(dcb, wc1).astype(BF)
            p = cpt[r].astype(F32).reshape(8, MP, T)
            dp_ = dot_nt(vblk[r], dc).reshape(8, MP, T)
            ds = p * (dp_ - jnp.sum(p * dp_, axis=1, keepdims=True))
            ds = ds.reshape(256, T).astype(BF)
            dk = dot(ds, cq[r])
            dv = dot(cpt[r], dc)
            rows = pl.ds(pl.multiple_of(r * MP, MP), MP)
            for a in range(NT):
                for j, val in ((0, dk), (1, dv)):
                    dkvm_s[a, j, rows] = jnp.where(
                        low_m, val[64 * a:64 * a + MP, 128 * a:128 * a + 128],
                        val[64 * a + MP:64 * a + 2 * MP, 128 * a:128 * a + 128])
            dq = (dot_tn(ds, kblk[r]) * SCALE).astype(BF)
            cq[r] = dq

        for c in dkv_copies:
            c.start()

        gq = dot_tn(h1b[0], cq[0]) + dot_tn(h1b[1], cq[1])
        go_ = dot_tn(cdb[0], cctx[0]) + dot_tn(cdb[1], cctx[1])
        for a in range(NT):
            q = rel_of(a)
            g[q, G_CROSS:G_CROSS + D] = gq[:, 128 * a:128 * a + 128].astype(BF)
            g[q, G_CROSS + D:G_CROSS + 2 * D] = go_[:, 128 * a:128 * a + 128].astype(BF)
        all_pairs(C_CROSS)

        @pl.loop(0, R)
        def _(r):
            d32[r] += dot_nt(cq[r], wc0)

    @pl.when(is_dec)
    def _():
        cross_backward()

    @pl.loop(0, NT)
    def _(q):
        a = shard_of(q)
        put_feed(C_UP, q, dot_tn(hb[0], gp[0, a]) + dot_tn(hb[1], gp[1, a]))

    @pl.loop(0, R)
    def _(r):
        dy = d32[r]
        add_norm(0, xh1[r], dy)
        d1 = norm_back(xh1[r], rs1[r], g_row(0), dy)
        d32[r] = d1
        db = d1.astype(BF)
        dab[r] = db
        drr = dot_nt(db, w_out_full()).astype(BF)
        for a in range(NT):
            dr[r, a] = drr[:, 128 * a:128 * a + 128]

    wo_all = dot_tn(wide(ctx, 0), dab[0]) + dot_tn(wide(ctx, 1), dab[1])
    for a in range(NT):
        for j in range(4):
            g[rel_of(a), G_OUT + 128 * j:G_OUT + 128 * j + 128] = (
                wo_all[128 * a:128 * a + 128, 128 * j:128 * j + 128].astype(BF))
    for q in range(3):
        pair(C_OUT, q).start()

    @pl.when(is_dec)
    def _():
        pair(C_OUT, 3).start()

    feed_on(C_UP)

    def attend_back(a, r, windows, encoder):
        k_t = turned(kk, a, r, windows[1][0] + windows[1][1])
        dks, dvs = [], []
        for b, (w0, wn) in enumerate(windows):
            rows = slice(b * 128, b * 128 + 128)
            d_r = dr[r, a, rows]
            d_r = jnp.concatenate([d_r * hmask[0, 0:128], d_r * hmask[1, 0:128]], axis=0)
            pb = pt[a, r, b, 0:wn]
            p = pb.astype(F32)
            dp_ = dot_nt(vv[a, r, w0:w0 + wn], d_r)
            ds = (p * (dp_ - jnp.sum(p * dp_, axis=0, keepdims=True))).astype(BF)
            dq = dot(k_t[:, w0:w0 + wn], ds)
            dq = jnp.concatenate([dq[0:64, 0:128], dq[64:128, 128:256]], axis=0)
            act[r, a, rows, 0:128] = (dq.T * SCALE).astype(BF)
            dks.append(dot(ds, qs[a, r, b]))
            dvs.append(dot(pb, d_r))
        (_, n0), (w1, n1_) = windows
        for j, (lo, hi) in enumerate((dks, dvs)):
            both = lo[w1:n0] + hi[0:n0 - w1]
            val = jnp.concatenate([lo[0:w1], both, hi[n0 - w1:n1_]], axis=0)
            dkv[a, r, j] = val[OWN:OWN + T]
            halo_s[0, a, r, j] = val[LEFT:LEFT + HALO].astype(BF)
            if encoder:
                halo_s[1, a, r, j] = val[RIGHT:RIGHT + HALO].astype(BF)
                mg_s[a, r, j + 1] = (val[0:MP] + val[MEM_2:MEM_2 + MP]).astype(BF)

    def halo_copies(a):
        return (remote(halo_s.at[0, a], halo_r.at[0, a], hsend.at[0, a], hrecv.at[0, a], tensor=left),
                remote(halo_s.at[1, a], halo_r.at[1, a], hsend.at[1, a], hrecv.at[1, a], tensor=right))

    first = jnp.where(t == 0, 1.0, 0.0)
    mg_copies = [remote(mg_s.at[lax.rem(t + off, NT)], mg_r.at[off - 1], qsend.at[off - 1], qrecv.at[off - 1],
                        tensor=lax.rem(t + off, NT)) for off in (1, 2, 3)]

    def add_g(start, val):
        n = val.shape[0]
        g[3, start:start + n] = (g[3, start:start + n].astype(F32) + val).astype(BF)

    def add_norm_m(at_, xh, dy):
        ng[at_:at_ + 1] += first * jnp.sum(dy * xh, axis=0, keepdims=True)
        ng[at_ + 3:at_ + 4] += first * jnp.sum(dy, axis=0, keepdims=True)

    def mem_back_first():
        for b in range(NT):
            remote(dkvm_s.at[b], dkvm_r.at[b], dsend.at[b], drecv.at[b], section=other, tensor=b).wait_recv()
        grads = []
        for j in range(2):
            tot = dkvm_r[0, j] + dkvm_r[1, j] + dkvm_r[2, j] + dkvm_r[3, j]
            grads.append(tot.astype(BF))
        ex_m[t] = (dot_nt(grads[0], wcross[t, 0]) + dot_nt(grads[1], wcross[t, 1])).astype(BF)
        ex_start(3)
        for j in range(2):
            g[3, G_CROSS + D * j:G_CROSS + D * j + D] = dot_tn(mm[...], grads[j]).astype(BF)
        pair(C_CROSS, 3).start()

    def mem_back_second():
        ex_wait(3)
        dm = ex_m[0].astype(F32)
        for s in range(1, NT):
            dm = dm + ex_m[s].astype(F32)
        add_norm_m(2, mx3[...], dm)
        rows_m = lax.broadcasted_iota(jnp.int32, (R * MP, D), 0)

        @pl.when(t == 0)
        def _():
            mem_local[1].wait()

        @pl.when(t > 0)
        def _():
            mem_c[0].wait_recv()

        cm = jnp.concatenate([cotm[0], cotm[1]], axis=0)
        cm = jnp.where(lax.rem(rows_m, MP) < MEM, cm, 0.0)
        dy = cm + norm_back(mx3[...], mr3[...], g_row(2), dm)
        add_norm_m(1, mx2[...], dy)
        d3 = norm_back(mx2[...], mr2[...], g_row(1), dy)
        d3b = d3.astype(BF)
        d2 = d3
        for a in range(NT):
            dum = (dot_nt(d3b, wdown[a]) * mgp[a]).astype(BF)
            d2 = d2 + dot_nt(dum, wup[a])
            mdu[a] = dum
        wd = dot_tn(mact[...], d3b)
        wu = dot_tn(mh[...].astype(BF), mdu[t])
        md[...] = d2
        for j in range(4):
            add_g(G_DOWN + D * j, wd[:, 128 * j:128 * j + 128])
            add_g(G_UP + D * j, wu[:, 128 * j:128 * j + 128])
        pair(C_DOWN, 3).start()
        pair(C_UP, 3).start()

    def mem_back_third():
        d2 = md[...]
        add_norm_m(0, mx1[...], d2)
        d1 = norm_back(mx1[...], mr1[...], g_row(0), d2)
        md[...] = d1
        d1b = d1.astype(BF)
        drm = dot_nt(d1b, w_out_full()).astype(BF).astype(F32)
        mh[...] = drm
        prod = drm * mc[...]
        for r in range(R):
            acc = jnp.zeros((MP, 128), F32)
            for hh in range(8):
                cols = prod[r * MP:r * MP + MP, (hh // 2) * 128:(hh // 2) * 128 + 128]
                cols = jnp.where(low_m if hh % 2 == 0 else jnp.logical_not(low_m), cols, 0.0)
                acc = jnp.where(lane_m == hh, jnp.sum(cols, axis=1, keepdims=True), acc)
            mst[1, r * MP:r * MP + MP] = acc
        for a in range(NT):
            @pl.when(t == a)
            def _():
                wo = dot_tn(mc[:, 128 * a:128 * a + 128].astype(BF), d1b)
                for j in range(4):
                    add_g(G_OUT + 128 * j, wo[:, 128 * j:128 * j + 128])
        pair(C_OUT, 3).start()

    def mem_attend_back():
        for a in range(NT):
            for r in range(R):
                rows = slice(r * MP, r * MP + MP)
                lse = mst[0, rows]
                dlt = mst[1, rows]
                lse = jnp.concatenate([lse[:, 2 * a:2 * a + 1], lse[:, 2 * a + 1:2 * a + 2]], axis=0)
                dlt = jnp.concatenate([dlt[:, 2 * a:2 * a + 1], dlt[:, 2 * a + 1:2 * a + 2]], axis=0)
                lhs = qm[a, r]
                ko, vo = kk[a, r, OWN:OWN + T], vv[a, r, OWN:OWN + T]
                p = jnp.exp(dot_nt(lhs, ko) - lse)
                dra = mh[rows, 128 * a:128 * a + 128]
                dra = jnp.concatenate([jnp.where(low_m, dra, 0.0), jnp.where(low_m, 0.0, dra)], axis=0).astype(BF)
                ds = (p * (dot_nt(dra, vo) - dlt)).astype(BF)
                dq = dot(ds, ko)
                mg_s[a, r, 0] = (jnp.where(low_m, dq[0:MP], dq[MP:2 * MP]) * SCALE).astype(BF)
                dkv[a, r, 0] += dot_tn(ds, lhs)
                dkv[a, r, 1] += dot_tn(p.astype(BF), dra)

        go(mg_copies)

    def order(i):
        return jnp.where(i == 0, 1, jnp.where(i == 1, 0, i))

    @pl.loop(0, NT * R)
    def _(i):
        a = shard_of(order(lax.div(i, 2)))
        r = lax.rem(i, 2)

        @pl.when(is_enc)
        def _():
            attend_back(a, r, WIN_ENC, True)

        @pl.when(is_dec)
        def _():
            attend_back(a, r, WIN_DEC, False)

        @pl.when(r == 1)
        def _():
            to_left, to_right = halo_copies(a)
            to_left.start()

            @pl.when(is_enc)
            def _():
                to_right.start()

        @pl.when(is_dec)
        def _():
            @pl.when(i == 1)
            def _():
                for k in (C_CROSS, C_OUT):
                    all_pairs_sum(k)
                    go([over_tensor(k, q) for q in range(3)])

        @pl.when(is_enc)
        def _():
            @pl.when(i == 1)
            def _():
                mem_back_first()

            @pl.when(i == 5)
            def _():
                mem_back_second()

            @pl.when(i == 6)
            def _():
                mem_back_third()

    n1 = [remote(ny.at[t], ny.at[t], ns.at[o - 1], nq.at[o - 1], tensor=lax.rem(t + o, NT)) for o in (1, 2, 3)]
    n2 = [remote(nc.at[0], nc.at[1], ns.at[3], nq.at[3], dp=sib)]
    n3 = [remote(nx.at[chip], nx.at[chip], ns.at[3 + o], nq.at[3 + o], dp=chip_at(o) * 2 + core)
          for o in range(1, chips)]

    def mem_last():
        for k in (C_DOWN, C_UP):
            all_pairs_sum(k, (3,))
            go(along_x(k, True))
        mem_attend_back()
        all_pairs_sum(C_OUT)
        go([over_tensor(C_OUT, q) for q in range(3)])
        all_pairs_sum(C_CROSS, (3,))
        start, lo, hf = at(C_CROSS)
        ysum[lo - LATE:lo - LATE + hf] = g[3, pl.ds(own_half(C_CROSS), hf)]
        go(over_chips(C_CROSS))

    ny[t] = ng[...]

    @pl.when(is_dec)
    def _():
        go(n1)

    @pl.when(is_enc)
    def _():
        go(n1)
        mem_last()

    dxm_copy = remote(dxm_s, dxm_r.at[t], gsend.at[0], grecv.at[t], tensor=0)

    def qkv_on(q):
        all_pairs_sum(C_QKV, (q,))
        go(chips_first(C_QKV, q))

    def mem_own():
        come(mg_copies)
        cols = []
        for j in range(3):
            both = []
            for r in range(R):
                tot = mg_s[t, r, j].astype(F32)
                for o in range(3):
                    tot = tot + mg_r[o, r, j].astype(F32)
                both.append(tot)
            cols.append(jnp.concatenate(both, axis=0))
        dm = jnp.concatenate(cols, axis=1).astype(BF)
        gw = dot_tn(x_mem(), dm)
        for j in range(3):
            add_g(G_QKV + D * j, gw[:, 128 * j:128 * j + 128])
        return dm

    @pl.loop(0, NT)
    def _(i):
        q = order(i)
        a = shard_of(q)
        to_left, to_right = halo_copies(a)
        to_left.wait_recv()

        @pl.when(is_enc)
        def _():
            to_right.wait_recv()

        for r in range(R):
            for j in range(2):
                dkv[a, r, j, T - HALO:T] += halo_r[0, a, r, j].astype(F32)

                @pl.when(is_enc)
                def _():
                    dkv[a, r, j, 0:HALO] += halo_r[1, a, r, j].astype(F32)

                act[r, a, :, 128 * (j + 1):128 * (j + 2)] = dkv[a, r, j].astype(BF)
        gw = dot_tn(x_ext[0, OWN:OWN + T], act[0, a, :, 0:384]) + dot_tn(x_ext[1, OWN:OWN + T], act[1, a, :, 0:384])
        for j in range(3):
            g[q, G_QKV + D * j:G_QKV + D * j + D] = gw[:, 128 * j:128 * j + 128].astype(BF)

        @pl.when(q < 3)
        def _():
            pair(C_QKV, q).start()

        wfull = jnp.concatenate([wqkv[a, j] for j in range(3)], axis=1)

        @pl.when(q == 3)
        def _():
            @pl.when(is_enc)
            def _():
                dm = mem_own()
                pair(C_QKV, 3).start()
                dxm_s[...] = dot_nt(dm, wfull).astype(BF)

                @pl.when(t > 0)
                def _():
                    dxm_copy.start()

            @pl.when(is_dec)
            def _():
                pair(C_QKV, 3).start()

        for r in range(R):
            d32[r] += dot_nt(act[r, a, :, 0:384], wfull)

        @pl.when(i > 0)
        def _():
            qkv_on(order(i - 1))

    qkv_on(3)

    come(n1)
    nc[0] = ny[0] + ny[1] + ny[2] + ny[3]
    go(n2)
    for k in (C_DOWN, C_UP):
        come(along_x(k, False))
        for q in range(3):
            along_x_sum(k, q)
        go(tensor_second(k))
    come(n2)
    nx[chip] = nc[0] + nc[1]
    go(n3)

    @pl.when(is_dec)
    def _():
        come([over_tensor(C_CROSS, q) for q in range(3)])
        tensor_sum(C_CROSS)
        go(over_chips(C_CROSS))

    come([over_tensor(C_OUT, q) for q in range(3)])
    tensor_sum(C_OUT)
    go(over_chips(C_OUT))
    for q in range(NT):
        come(chips_first(C_QKV, q))
        chips_first_sum(C_QKV, q)
    go(tensor_third(C_QKV))
    for k in (C_DOWN, C_UP):
        come(along_x(k, True))
        along_x_sum(k, 3)
        come(tensor_second(k))
        tensor_second_sum(k)
        go(over_z(k))
    come(tensor_third(C_QKV))
    tensor_third_sum(C_QKV)
    go(spread(C_QKV))
    for k in (C_CROSS, C_OUT):
        come(over_chips(k))
        chips_sum(k)
        go(spread(k))
    for k in (C_DOWN, C_UP):
        come(over_z(k))
        over_z_sum(k)
        go(spread_x(k))

    @pl.when(jnp.logical_and(is_enc, t == 0))
    def _():
        tot = md[...] + dxm_s[...].astype(F32)
        for s in range(1, NT):
            remote(dxm_s, dxm_r.at[s], gsend.at[0], grecv.at[s], tensor=0).wait_recv()
            tot = tot + dxm_r[s].astype(F32)
        for r in range(R):
            d32[r, 0:MP] += tot[r * MP:r * MP + MP]

    dx_copy = pltpu.make_async_copy(d32, dx_out, lsem.at[10])
    dx_copy.start()
    come(n3)
    tot_n = nx[0]
    for o in range(1, chips):
        tot_n = tot_n + nx[o]
    ng_tot[...] = tot_n
    for k in (C_CROSS, C_OUT):
        come(spread(k))
        go(hand(k))
    for k in (C_DOWN, C_UP):
        come(spread_x(k))
        go(hand(k))
    come(spread(C_QKV))
    go(hand(C_QKV))
    for k in range(5):
        come(hand(k))

    y_copy.wait()
    dx_copy.wait()
    for i in (QKV, OUT):
        gone(w_direct(i))
        gone(w_pair(i))
    for i in (UP, DOWN):
        gone(w_eighth(i))
        gone(w_along(i))
        gone(w_pair(i))
    x_right.wait_send()
    for a in range(NT):
        halo_copies(a)[0].wait_send()
    gone(n1)
    gone(n2)
    gone(n3)
    for k in range(5):
        if k in (C_DOWN, C_UP):
            gone(along_x(k, False))
            gone(along_x(k, True))
            gone(tensor_second(k))
            gone(over_z(k))
            gone(spread_x(k))
        elif k == C_QKV:
            for q in range(NT):
                gone(chips_first(k, q))
            gone(tensor_third(k))
            gone(spread(k))
        else:
            gone(over_chips(k))
            gone(spread(k))
        if k != C_CROSS:
            gone([pair(k, q) for q in range(NT)])
        gone(hand(k))
    gone([over_tensor(C_OUT, q) for q in range(3)])

    @pl.when(is_dec)
    def _():
        gone(w_direct(CROSS))
        gone(w_pair(CROSS))
        gone(dkv_copies)
        gone([pair(C_CROSS, q) for q in range(NT)])
        gone([over_tensor(C_CROSS, q) for q in range(3)])

    @pl.when(is_enc)
    def _():
        x_left.wait_send()
        pair(C_CROSS, 3).wait_send()
        for a in range(NT):
            halo_copies(a)[1].wait_send()
        for e in range(4):
            gone(exchanges[e])
        gone(mg_copies)
        gone(kv_copies)

        @pl.when(t == 0)
        def _():
            gone(mem_x)
            gone(mem_c)

        @pl.when(t > 0)
        def _():
            dxm_copy.wait_send()


def layer_call(chips, lens, x, cot, wqkv, wout, wcross, wup, wdown, gain, bias):
    any_ = pl.BlockSpec(memory_space=pl.ANY)
    vmem = pl.BlockSpec(memory_space=pltpu.VMEM)
    M = R * MP
    W = W_ENC
    S = pltpu.SemaphoreType.DMA
    C = len(CHUNKS)
    o = max(chips - 1, 1)
    late = HALF - LATE

    def V(shape, kind):
        return pltpu.VMEM(shape, kind)

    scratch = dict(
        x_ext=V((R, W, D), BF), cotm=V((R, MP, D), F32), d32=V((R, T, D), F32),
        wqkv=V((NT, 3, D, 128), BF), wout=V((NT, 128, D), BF), wcross=V((NT, 2, D, 128), BF),
        wup=V((NT, D, D), BF), wdown=V((NT, D, D), BF),
        kk=V((NT, R, W, 128), BF), vv=V((NT, R, W, 128), BF),
        qs=V((NT, R, 2, T, 128), BF), pt=V((NT, R, 2, 512, T), BF), ctx=V((R, NT, T, 128), BF),
        mask=V((R, 2, 512, 128), F32), hmask=V((2, T, 128), BF),
        xh1=V((R, T, D), F32), xh2=V((R, T, D), F32), rs1=V((R, T, 1), F32), rs2=V((R, T, 1), F32),
        h32=V((R, T, D), F32), hb=V((R, T, D), BF), h1b=V((R, T, D), BF),
        act=V((R, NT, T, D), BF), gp=V((R, NT, T, D), BF), dab=V((R, T, D), BF), dr=V((R, NT, T, 128), BF),
        dkv=V((NT, R, 2, T, 128), F32), halo_s=V((2, NT, R, 2, HALO, 128), BF),
        halo_r=V((2, NT, R, 2, HALO, 128), BF), mg_s=V((NT, R, 3, MP, 128), BF), mg_r=V((3, R, 3, MP, 128), BF),
        dxm_s=V((M, D), BF), dxm_r=V((NT, M, D), BF), mdu=V((NT, M, D), BF),
        ex_o=V((NT, NT, M, 128), BF), ex_st=V((NT, M, 128), F32), ex_f=V((NT, M, D), BF), ex_m=V((NT, M, D), BF),
        qm=V((NT, R, 2 * MP, 128), BF),
        kvm=V((NT, 2, M, 128), BF), dkvm_s=V((NT, 2, M, 128), F32), dkvm_r=V((NT, 2, M, 128), F32),
        kblk=V((R, 256, D), BF), vblk=V((R, 256, D), BF), cpt=V((R, 256, T), BF), cq=V((R, T, D), BF),
        cctx=V((R, T, D), BF), cdb=V((R, T, D), BF),
        mx1=V((M, D), F32), mx2=V((M, D), F32), mx3=V((M, D), F32), mr1=V((M, 1), F32), mr2=V((M, 1), F32),
        mr3=V((M, 1), F32), mh=V((M, D), F32), mact=V((M, D), BF), mgp=V((NT, M, D), F32), mc=V((M, D), F32),
        mm=V((M, D), BF), mst=V((2, M, 128), F32), md=V((M, D), F32),
        g=V((NT, G_ROWS, 128), BF), r1=V((NT, HALF, 128), BF), r2=V((3, late, 128), BF),
        r3=V((o, late // chips, 128), BF), rx=V((3, NT, LATE // 4, 128), BF), ry_s=V((NT, LATE // 4, 128), BF),
        ry_r=V((3, LATE // 4, 128), BF), zz=V((2, LATE // 4, 128), BF),
        rq=V((o, NT, 768 // chips, 128), BF), rqs=V((NT, 768 // chips, 128), BF), rqr=V((3, 768 // chips, 128), BF),
        ysum=V((late, 128), BF), ng=V((8, D), F32), ny=V((NT, 8, D), F32), nc=V((2, 8, D), F32),
        nx=V((chips, 8, D), F32),
        lsem=S((11,)), wsend=S((5, 6)), wrecv=S((5, 6)), w2send=S((2, 3, 3)), w2recv=S((2, 3, 3)), xsend=S((2,)), xrecv=S((2,)), msend=S((2, 3)), mrecv=S((2,)),
        esend=S((5, 3)), erecv=S((5, 3)), ksend=S((NT,)), krecv=S((NT,)), dsend=S((NT,)), drecv=S((NT,)),
        hsend=S((2, NT)), hrecv=S((2, NT)), gsend=S((1,)), grecv=S((NT,)), qsend=S((3,)), qrecv=S((3,)), sq=S((NT, o)), qq=S((NT, o)),
        s1=S((C, NT)), q1=S((C, NT)), s2=S((C, 3)), q2=S((C, 3)), s3=S((C, o)), q3=S((C, o)),
        s4=S((C, o)), q4=S((C, o)), s5=S((C,)), q5=S((C,)), ns=S((4 + o,)), nq=S((4 + o,)),
        sx=S((2, 2, 3)), qx=S((2, 2, 3)), sz=S((2,)), qz=S((2,)),
    )
    names = tuple(scratch)

    def kernel(*refs):
        layer_kernel(chips, names, *refs)

    return pl.pallas_call(
        kernel,
        out_shape=(
            jax.ShapeDtypeStruct((R, T, D), F32),
            jax.ShapeDtypeStruct((R, T, D), F32),
            jax.ShapeDtypeStruct((G_ROWS, 128), BF),
            jax.ShapeDtypeStruct((8, D), F32),
        ),
        in_specs=[pl.BlockSpec(memory_space=pltpu.SMEM)] + [any_] * 7 + [vmem] * 2,
        out_specs=(any_, any_, vmem, vmem),
        scratch_shapes=list(scratch.values()),
        compiler_params=pltpu.CompilerParams(
            collective_id=0, has_side_effects=True, vmem_limit_bytes=VMEM_BYTES
        ),
        name="layers",
    )(lens, x, cot, wqkv, wout, wcross, wup, wdown, gain, bias)


def finish_kernel(y_in, dx_in, full, ng, y, dx, o_qkv, o_out, o_cross, o_up, o_down, o_gain, o_bias, sems):
    copies = [pltpu.make_async_copy(y_in, y.at[0], sems.at[0]), pltpu.make_async_copy(dx_in, dx.at[0], sems.at[1])]
    for c in copies:
        c.start()
    for j in range(3):
        o_qkv[0, j] = full[G_QKV + D * j:G_QKV + D * j + D].astype(F32)
    for j in range(2):
        o_cross[0, j] = full[G_CROSS + D * j:G_CROSS + D * j + D].astype(F32)
    for j in range(4):
        cols = slice(128 * j, 128 * j + 128)
        o_out[0, :, cols] = full[G_OUT + 128 * j:G_OUT + 128 * j + 128].astype(F32)
        o_up[0, :, cols] = full[G_UP + D * j:G_UP + D * j + D].astype(F32)
        o_down[0, :, cols] = full[G_DOWN + D * j:G_DOWN + D * j + D].astype(F32)
    for i in range(3):
        o_gain[i] = ng[i:i + 1]
        o_bias[i] = ng[i + 3:i + 4]
    for c in copies:
        c.wait()


def finish_call(y, dx, full, ng):
    any_ = pl.BlockSpec(memory_space=pl.ANY)
    vmem = pl.BlockSpec(memory_space=pltpu.VMEM)
    shapes = ((1, R, T, D), (1, R, T, D), (1, 3, D, 128), (1, 128, D), (1, 2, D, 128), (1, D, D), (1, D, D),
              (3, 1, D), (3, 1, D))
    return pl.pallas_call(
        finish_kernel,
        out_shape=tuple(jax.ShapeDtypeStruct(s, F32) for s in shapes),
        in_specs=[vmem] * 4,
        out_specs=(any_, any_) + (vmem,) * 7,
        scratch_shapes=[pltpu.SemaphoreType.DMA((2,))],
        compiler_params=pltpu.CompilerParams(vmem_limit_bytes=VMEM_BYTES),
        name="finish",
    )(y, dx, full, ng)


def solution(mesh):
    chips = mesh.shape["dp"] // 2

    def shards(inputs, lengths, w_qkv, w_out, w_cross, w_up, w_down, norm_gain, norm_bias, cotangent):
        y, dx, full, ng = layer_call(
            chips, lengths, inputs[0], cotangent[0], w_qkv[0], w_out[0], w_cross[0], w_up[0], w_down[0],
            jnp.transpose(norm_gain, (1, 0, 2)), jnp.transpose(norm_bias, (1, 0, 2)))
        outs = finish_call(y, dx, full, ng)
        return outs[:7] + tuple(jnp.transpose(v, (1, 0, 2)) for v in outs[7:])

    return jax.shard_map(
        shards,
        mesh=mesh,
        in_specs=(
            P("section", "dp", "tensor", None),
            P("dp", None),
            P("section", None, None, "tensor"),
            P("section", "tensor", None),
            P("section", None, None, "tensor"),
            P("section", None, "tensor"),
            P("section", "tensor", None),
            P("section", None, None),
            P("section", None, None),
            P("section", "dp", "tensor", None),
        ),
        out_specs=(
            P("section", "dp", "tensor", None),
            P("section", "dp", "tensor", None),
            P("section", None, None, "tensor"),
            P("section", "tensor", None),
            P("section", None, None, "tensor"),
            P("section", None, "tensor"),
            P("section", "tensor", None),
            P("section", None, None),
            P("section", None, None),
        ),
        check_vma=False,
    )
```

```python
import jax
import jax.numpy as jnp
from jax import lax
from jax.experimental import pallas as pl
from jax.experimental.pallas import tpu as pltpu
from jax.sharding import PartitionSpec as P

F32 = jnp.float32
BF = jnp.bfloat16
MESH = pl.DeviceIdType.MESH
VMEM_BYTES = 62 * 1024 * 1024

MEM = 20
MP = 32
R = 2
M = R * MP
T = 256
HALO = 160
D = 512
NT = 4
LEFT, OWN, RIGHT, MEM_2, W_ENC = 32, 192, 448, 608, 640
W_DEC = RIGHT
WIN_ENC = ((0, 480), (128, 512))
WIN_DEC = ((0, 320), (128, 320))
EPS = 1e-05
FILL = -1e30
SCALE = 0.125

G_DOWN, G_UP, G_CROSS, G_OUT, G_QKV, G_ROWS = 0, 2048, 4096, 5120, 5632, 7168
G_KV = G_QKV + 512
CHUNKS = ((G_DOWN, 2048), (G_UP, 2048), (G_CROSS, 1024), (G_OUT, 512), (G_QKV, 512), (G_KV, 1024))
CN = len(CHUNKS)
C_DOWN, C_UP, C_CROSS, C_OUT, C_Q, C_KV = range(CN)
LATE = G_CROSS // 2
HALF = G_ROWS // 2
QKV, OUT, CROSS, UP, DOWN = range(5)
ALONG = {QKV: 0, UP: 1, DOWN: 2}
W_ROWS = (512, 128, 512, 512, 512)


def dot(a, b):
    return lax.dot_general(a, b, (((1,), (0,)), ((), ())), preferred_element_type=F32)


def dot_nt(a, b):
    return lax.dot_general(a, b, (((1,), (1,)), ((), ())), preferred_element_type=F32)


def dot_tn(a, b):
    return lax.dot_general(a, b, (((0,), (0,)), ((), ())), preferred_element_type=F32)


def remote(src, dst, send, recv, **device):
    return pltpu.make_async_remote_copy(
        src_ref=src, dst_ref=dst, send_sem=send, recv_sem=recv, device_id=device, device_id_type=MESH
    )


def normed(v):
    c = v - jnp.mean(v, axis=1, keepdims=True)
    rs = lax.rsqrt(jnp.mean(c * c, axis=1, keepdims=True) + EPS)
    return c * rs, rs


def norm_back(xhat, rs, gain, dy):
    dxh = dy * gain
    m1 = jnp.mean(dxh, axis=1, keepdims=True)
    m2 = jnp.mean(dxh * xhat, axis=1, keepdims=True)
    return rs * (dxh - m1 - xhat * m2)


def gelu_both(u):
    k = 0.7978845608028654
    u2 = u * u
    th = jnp.tanh(k * u * (1.0 + 0.044715 * u2))
    half = 0.5 * (1.0 + th)
    grad = half + 0.5 * u * (1.0 - th * th) * (k * (1.0 + 3.0 * 0.044715 * u2))
    return u * half, grad


def layer_kernel(chips, names, *refs):
    (lens, x_in, cot_in, wqkv_in, wout_in, wcross_in, wup_in, wdown_in, gain, bias,
     y_out, dx_out, full, ng_tot) = refs[:14]
    m = dict(zip(names, refs[14:]))
    x_ext, cotm, d32, wqkv, wout, wcross, wup, wdown = (
        m[n] for n in ("x_ext", "cotm", "d32", "wqkv", "wout", "wcross", "wup", "wdown"))
    kk, vv, qs, pt, ctx, mask, hmask = (m[n] for n in ("kk", "vv", "qs", "pt", "ctx", "mask", "hmask"))
    xh1, xh2, rs1, rs2, h32, hb, h1b, act, gp, dab, dr = (
        m[n] for n in ("xh1", "xh2", "rs1", "rs2", "h32", "hb", "h1b", "act", "gp", "dab", "dr"))
    dkv, halo_s, halo_r, mg_s, mg_r, dxm_s, dxm_r, mdu = (
        m[n] for n in ("dkv", "halo_s", "halo_r", "mg_s", "mg_r", "dxm_s", "dxm_r", "mdu"))
    ex_o, ex_st, ex_f, ex_m, qm, rq, rqs, rqr = (
        m[n] for n in ("ex_o", "ex_st", "ex_f", "ex_m", "qm", "rq", "rqs", "rqr"))
    kvm, dkvm_s, dkvm_r, kblk, vblk, cpt, cq, cctx = (
        m[n] for n in ("kvm", "dkvm_s", "dkvm_r", "kblk", "vblk", "cpt", "cq", "cctx"))
    mx1, mx2, mx3, mr1, mr2, mr3, mh, mact, mc, mm, mst, md = (
        m[n] for n in ("mx1", "mx2", "mx3", "mr1", "mr2", "mr3", "mh", "mact", "mc", "mm", "mst", "md"))
    g, r1, rx, ry_s, ry_r, zz, ng, ny, nc, nx, cdb, dmb = (
        m[n] for n in ("g", "r1", "rx", "ry_s", "ry_r", "zz", "ng", "ny", "nc", "nx", "cdb", "dmb"))
    (lsem, wsend, wrecv, xsend, xrecv, msend, mrecv, esend, erecv, ksend, krecv, dsend, drecv,
     hsend, hrecv, gsend, grecv, qsend, qrecv) = (
        m[n] for n in ("lsem", "wsend", "wrecv", "xsend", "xrecv", "msend", "mrecv", "esend", "erecv", "ksend",
                       "krecv", "dsend", "drecv", "hsend", "hrecv", "gsend", "grecv", "qsend", "qrecv"))
    s1, q1, s2, q2, s4, q4, s5, q5, ns, nq = (
        m[n] for n in ("s1", "q1", "s2", "q2", "s4", "q4", "s5", "q5", "ns", "nq"))
    w2send, w2recv, sx, qx, sz, qz, sq, qq = (
        m[n] for n in ("w2send", "w2recv", "sx", "qx", "sz", "qz", "sq", "qq"))

    def g_row(i):
        return gain[i]

    def b_row(i):
        return bias[i]

    sec = lax.axis_index("section")
    dp = lax.axis_index("dp")
    t = lax.axis_index("tensor")
    core = lax.rem(dp, 2)
    chip = lax.div(dp, 2)
    sib = dp + 1 - 2 * core
    is_enc = sec == 0
    is_dec = sec == 1
    left = lax.rem(t + 3, NT)
    right = lax.rem(t + 1, NT)
    opp = lax.rem(t + 2, NT)
    other = 1 - sec
    xi = lax.div(dp, 4)

    def x_dev(off):
        return lax.rem(xi + off, 4) * 4 + lax.rem(dp, 4)

    z_dev = xi * 4 + lax.rem(dp + 2, 4)

    def source(off):
        return lax.rem(t + NT - off, NT)

    def chip_at(off):
        return lax.rem(chip + off, chips)

    ins = (wqkv_in, wout_in, wcross_in, wup_in, wdown_in)
    ws = (wqkv, wout, wcross, wup, wdown)

    def part(i, ref, start, n):
        if i in (QKV, CROSS):
            return ref.at[:, pl.ds(start, n), :]
        return ref.at[pl.ds(start, n), :]

    def slot(i, a, start, n):
        if i in (QKV, CROSS):
            return ws[i].at[a, :, pl.ds(start, n), :]
        return ws[i].at[a, pl.ds(start, n), :]

    barrier = pltpu.get_barrier_semaphore()
    for off in (1, 2, 3):
        pl.semaphore_signal(barrier, inc=1, device_id={"tensor": lax.rem(t + off, NT)}, device_id_type=MESH)
    pl.semaphore_signal(barrier, inc=1, device_id={"dp": sib}, device_id_type=MESH)
    for b in range(NT):
        pl.semaphore_signal(barrier, inc=1, device_id={"section": other, "tensor": b}, device_id_type=MESH)
    for off in range(1, chips):
        pl.semaphore_signal(barrier, inc=1, device_id={"dp": chip_at(off) * 2 + core}, device_id_type=MESH)

    locals_ = [
        pltpu.make_async_copy(x_in, x_ext.at[:, pl.ds(OWN, T), :], lsem.at[0]),
        pltpu.make_async_copy(cot_in, d32, lsem.at[1]),
    ]
    for i in range(5):
        locals_.append(pltpu.make_async_copy(ins[i], ws[i].at[t], lsem.at[2 + i]))
    for c in locals_:
        c.start()

    pl.semaphore_wait(barrier, 8 + chips - 1)

    x_right = remote(x_in.at[:, pl.ds(T - HALO, HALO), :], x_ext.at[:, pl.ds(LEFT, HALO), :],
                     xsend.at[0], xrecv.at[0], tensor=right)
    x_left = remote(x_in.at[:, pl.ds(0, HALO), :], x_ext.at[:, pl.ds(RIGHT, HALO), :],
                    xsend.at[1], xrecv.at[1], tensor=left)
    mem_x, mem_c = [], []
    for off in (1, 2, 3):
        to = lax.rem(t + off, NT)
        mem_x.append(remote(x_in.at[:, pl.ds(0, MP), :], x_ext.at[:, pl.ds(0, MP), :],
                            msend.at[0, off - 1], mrecv.at[0], tensor=to))
        mem_c.append(remote(cot_in.at[:, pl.ds(0, MP), :], cotm, msend.at[1, off - 1], mrecv.at[1], tensor=to))
    mem_local = [
        pltpu.make_async_copy(x_in.at[:, pl.ds(0, MP), :], x_ext.at[:, pl.ds(0, MP), :], lsem.at[7]),
        pltpu.make_async_copy(cot_in.at[:, pl.ds(0, MP), :], cotm, lsem.at[8]),
    ]

    def w_direct(i):
        hf = W_ROWS[i] // 2
        mine = core * hf
        return [remote(part(i, ins[i], mine, hf), slot(i, t, mine, hf), wsend.at[i, off - 1], wrecv.at[i, off - 1],
                       tensor=lax.rem(t + off, NT)) for off in (1, 2, 3)]

    eighth = D // 8
    at_8 = core * (D // 2) + xi * eighth

    def w_eighth(i):
        return [remote(part(i, ins[i], at_8, eighth), slot(i, t, at_8, eighth),
                       wsend.at[i, off - 1], wrecv.at[i, off - 1], tensor=lax.rem(t + off, NT)) for off in (1, 2, 3)]

    def w_along(i):
        out = []
        for off in (1, 2, 3):
            rows = slot(i, source(off), at_8, eighth)
            for xo in (1, 2, 3):
                out.append(remote(rows, rows, w2send.at[ALONG[i], off - 1, xo - 1], w2recv.at[ALONG[i], off - 1, xo - 1],
                                  dp=x_dev(xo)))
        return out

    def w_pair(i):
        hf = W_ROWS[i] // 2
        out = []
        for off in (1, 2, 3):
            rows = slot(i, source(off), core * hf, hf)
            out.append(remote(rows, rows, wsend.at[i, 2 + off], wrecv.at[i, 2 + off], dp=sib))
        return out

    def go(cs):
        for c in cs:
            c.start()

    def come(cs):
        for c in cs:
            c.wait_recv()

    def gone(cs):
        for c in cs:
            c.wait_send()

    def arrive(i):
        for c, p in zip(w_direct(i), w_pair(i)):
            c.wait_recv()
            p.start()

    def go_along(i):
        along = w_along(i)
        for off, c in enumerate(w_eighth(i)):
            c.wait_recv()
            go(along[3 * off:3 * off + 3])

    def come_along(i):
        along = w_along(i)
        for off, p in enumerate(w_pair(i)):
            come(along[3 * off:3 * off + 3])
            p.start()

    def ready(i):
        come(w_pair(i))

    go(w_eighth(QKV))

    @pl.when(is_enc)
    def _():
        @pl.when(t == 0)
        def _():
            go(mem_x + mem_local)

        x_right.start()
        x_left.start()
        go(w_eighth(UP))
        go(w_direct(OUT))

    @pl.when(is_dec)
    def _():
        x_right.start()
        go(w_eighth(UP))
        go(w_direct(OUT))
        go(w_eighth(DOWN))
        go(w_direct(CROSS))

    lane = lax.broadcasted_iota(jnp.int32, (T, 128), 1)
    hmask[0] = jnp.where(lane < 64, 1.0, 0.0).astype(BF)
    hmask[1] = jnp.where(lane < 64, 0.0, 1.0).astype(BF)

    def bounds(pos, r):
        end = jnp.int32(MEM)
        first = jnp.where(pos >= MEM, MEM, 0)
        after = jnp.full(pos.shape, MEM, jnp.int32)
        for k in range(16):
            after = jnp.where(pos >= end, end + lens[r, k], after)
            first = jnp.where(pos >= end, end, first)
            end = end + lens[r, k]
        return first, after

    def make_masks(windows, encoder):
        for r in range(R):
            for b, (w0, wn) in enumerate(windows):
                e = lax.broadcasted_iota(jnp.int32, (wn, 128), 0) + w0
                pos = e - OWN + t * T
                qpos = lax.broadcasted_iota(jnp.int32, (8, 128), 1) + (t * T + b * 128)
                first, after = bounds(qpos, r)
                ok = jnp.logical_and(pos >= first[0:1], pos < after[0:1])
                if encoder:
                    mem_i = jnp.where(e < LEFT, e, jnp.where(e >= MEM_2, e - MEM_2, MEM))
                    ok = jnp.logical_or(mem_i < MEM, jnp.logical_and(
                        jnp.logical_and(e >= LEFT, e < MEM_2), jnp.logical_and(ok, pos >= MEM)))
                else:
                    ok = jnp.logical_and(jnp.logical_and(ok, e >= LEFT), pos <= qpos[0:1])
                mask[r, b, 0:wn] = jnp.where(ok, 0.0, FILL)

    @pl.when(is_enc)
    def _():
        make_masks(WIN_ENC, True)

    @pl.when(is_dec)
    def _():
        make_masks(WIN_DEC, False)
        x_ext[:, 0:MP] = jnp.zeros((R, MP, D), BF)

    ex_st[t] = jnp.zeros((R * MP, 128), F32)
    ng[...] = jnp.zeros(ng.shape, F32)

    go_along(QKV)
    for c in locals_:
        c.wait()

    def shard_at(step):
        return lax.rem(t + jnp.where(step == 0, 0, jnp.where(step == 1, 3, step - 1)), NT)

    lane_m = lax.broadcasted_iota(jnp.int32, (MP, 128), 1)
    low_m = lane_m < 64

    def keys(a, r, lo, hi, wkv):
        kv = dot(x_ext[r, lo:hi], wkv)
        k32, v32 = kv[:, 0:128], kv[:, 128:256]
        kk[a, r, lo:hi] = k32.astype(BF)
        vv[a, r, lo:hi] = v32.astype(BF)

    def keys_weight(a):
        return jnp.concatenate([wqkv[a, 1], wqkv[a, 2]], axis=1)

    def queries(a, r):
        q = dot(x_ext[r, OWN:OWN + T], wqkv[a, 0]).astype(BF)
        q = (q.astype(F32) * SCALE).astype(BF)
        for b in range(2):
            for h in range(2):
                qs[a, r, b, h * 128:h * 128 + 128] = q[b * 128:b * 128 + 128] * hmask[h, 0:128]

    def turned(ref, a, r, hi):
        return ref[a, r, 0:hi].astype(F32).T.astype(BF)

    def project_own(shards_):
        jobs = [(a, r) for a in shards_ for r in range(R)]
        for a in shards_:
            wkv = keys_weight(a)
            for r in range(R):
                keys(a, r, OWN, OWN + T, wkv)
                queries(a, r)
        lhs = []
        for a, r in jobs:
            m32 = dot(x_ext[r, 0:MP], wqkv[a, 0]).astype(BF).astype(F32) * SCALE
            lhs.append(jnp.concatenate([jnp.where(low_m, m32, 0.0), jnp.where(low_m, 0.0, m32)], axis=0).astype(BF))
        ss = [dot_nt(v, kk[a, r, OWN:OWN + T]) for v, (a, r) in zip(lhs, jobs)]
        tops = [jnp.max(s, axis=1, keepdims=True) for s in ss]
        ps = [jnp.exp(s - top) for s, top in zip(ss, tops)]
        totals = [jnp.sum(p, axis=1, keepdims=True) for p in ps]
        os_ = [dot(p.astype(BF), vv[a, r, OWN:OWN + T]) / total for p, total, (a, r) in zip(ps, totals, jobs)]
        for (a, r), v, o in zip(jobs, lhs, os_):
            qm[a, r] = v
            ex_o[t, a, r * MP:r * MP + MP] = jnp.where(low_m, o[0:MP], o[MP:2 * MP]).astype(BF)
        for r in range(R):
            st = ex_st[t, r * MP:r * MP + MP]
            for (a, r_), top, total in zip(jobs, tops, totals):
                if r_ == r:
                    st = jnp.where(lane_m == 2 * a, top[0:MP], st)
                    st = jnp.where(lane_m == 2 * a + 1, top[MP:2 * MP], st)
                    st = jnp.where(lane_m == 2 * a + 8, total[0:MP], st)
                    st = jnp.where(lane_m == 2 * a + 9, total[MP:2 * MP], st)
            ex_st[t, r * MP:r * MP + MP] = st

    def project_rest(a):
        wkv = keys_weight(a)
        for r in range(R):
            keys(a, r, 0, OWN, wkv)
            keys(a, r, RIGHT, W_ENC, wkv)

    def project_all(a):
        wkv = keys_weight(a)
        for r in range(R):
            keys(a, r, 0, W_DEC, wkv)
            queries(a, r)

    def ex_copies(e, buf):
        out = []
        for off in (1, 2, 3):
            out.append(remote(buf.at[t], buf.at[t], esend.at[e, off - 1], erecv.at[e, off - 1],
                              tensor=lax.rem(t + off, NT)))
        return out

    exchanges = [ex_copies(e, buf) for e, buf in enumerate((ex_o, ex_st, ex_f, ex_m))]

    def ex_start(e):
        for c in exchanges[e]:
            c.start()

    def ex_wait(e):
        for c in exchanges[e]:
            c.wait_recv()

    def wide(ref, r):
        return jnp.concatenate([ref[r, a] for a in range(NT)], axis=1)

    def w_out_full():
        return wout[...].reshape(D, D)

    def mem_combine():
        for r in range(R):
            rows = slice(r * MP, r * MP + MP)
            sts = [ex_st[s, rows] for s in range(NT)]
            top = jnp.maximum(jnp.maximum(sts[0], sts[1]), jnp.maximum(sts[2], sts[3]))
            wts = [pltpu.roll(sts[s], 120, 1) * jnp.exp(sts[s] - top) for s in range(NT)]
            total = wts[0] + wts[1] + wts[2] + wts[3]
            total = jnp.where(lane_m < 8, total, 1.0)
            inv = 1.0 / total
            mst[0, rows] = jnp.where(lane_m < 8, top + jnp.log(total), 0.0)
            for a in range(NT):
                acc = jnp.zeros((MP, 128), F32)
                for s in range(NT):
                    w = wts[s] * inv
                    wide_w = jnp.where(low_m, w[:, 2 * a:2 * a + 1], w[:, 2 * a + 1:2 * a + 2])
                    acc = acc + wide_w * ex_o[s, a, rows].astype(F32)
                mc[rows, a * 128:a * 128 + 128] = acc

    def x_mem():
        return jnp.concatenate([x_ext[r, 0:MP] for r in range(R)], axis=0)

    def mem_first():
        mem_combine()
        xm = x_mem().astype(F32)
        xh, rs = normed(xm + dot(mc[...].astype(BF), w_out_full()))
        mx1[...] = xh
        mr1[...] = rs
        h = xh * g_row(0) + b_row(0)
        mh[...] = h
        av, _ = gelu_both(dot(h.astype(BF), wup[t]))
        mact[...] = av.astype(BF)
        ex_f[t] = dot(av.astype(BF), wdown[t]).astype(BF)
        ex_start(2)

    kv_copies = [remote(kvm.at[t], kvm.at[t], ksend.at[b], krecv.at[t], section=other, tensor=b) for b in range(NT)]

    def mem_second():
        third = mh[...]
        for s in range(NT):
            third = third + ex_f[s].astype(F32)
        xh, rs = normed(third)
        mx2[...] = xh
        mr2[...] = rs
        y = xh * g_row(1) + b_row(1)
        md[...] = y
        xh, rs = normed(y)
        mx3[...] = xh
        mr3[...] = rs
        mv = (xh * g_row(2) + b_row(2)).astype(BF)
        mm[...] = mv
        kvm[t, 0] = dot(mv, wcross[t, 0]).astype(BF)
        kvm[t, 1] = dot(mv, wcross[t, 1]).astype(BF)
        for c in kv_copies:
            c.start()

    def attend(a, windows):
        jobs = [(r, b, w0, wn) for r in range(R) for b, (w0, wn) in enumerate(windows)]
        v_t = [turned(vv, a, r, windows[1][0] + windows[1][1]) for r in range(R)]
        scores = []
        for r, b, w0, wn in jobs:
            mk = mask[r, b, 0:wn]
            scores.append(dot_nt(kk[a, r, w0:w0 + wn], qs[a, r, b]) + jnp.concatenate([mk, mk], axis=1))
        ps = []
        for s in scores:
            p = jnp.exp(s - jnp.max(s, axis=0, keepdims=True))
            ps.append((p * (1.0 / jnp.sum(p, axis=0, keepdims=True))).astype(BF))
        for (r, b, w0, wn), p in zip(jobs, ps):
            pt[a, r, b, 0:wn] = p
            o = dot(v_t[r][:, w0:w0 + wn], p)
            o = jnp.concatenate([o[0:64, 0:128], o[64:128, 128:256]], axis=0)
            ctx[r, a, b * 128:b * 128 + 128] = o.T.astype(BF)

    def encoder_attention():
        @pl.when(t == 0)
        def _():
            mem_local[0].wait()

        @pl.when(t > 0)
        def _():
            mem_x[0].wait_recv()

        x_ext[:, MEM_2:MEM_2 + MP] = x_ext[:, 0:MP]

        project_own([t])
        come_along(QKV)
        ready(QKV)
        project_own([left, right, opp])
        ex_start(0)
        ex_start(1)
        go(w_eighth(DOWN))
        x_right.wait_recv()
        x_left.wait_recv()
        go_along(UP)
        arrive(OUT)

        @pl.loop(0, NT)
        def _(step):
            project_rest(shard_at(step))

        @pl.loop(0, NT)
        def _(i):
            @pl.when(i == 2)
            def _():
                ex_wait(0)
                ex_wait(1)
                ready(OUT)
                mem_first()
                go_along(DOWN)

            @pl.when(i == 3)
            def _():
                ex_wait(2)
                mem_second()

                @pl.when(t == 0)
                def _():
                    go(mem_c)

            attend(shard_at(i), WIN_ENC)

    def decoder_attention():
        x_right.wait_recv()

        project_all(t)

        @pl.loop(0, NT)
        def _(i):
            @pl.when(i == 1)
            def _():
                come_along(QKV)
                go_along(UP)
                ready(QKV)

                @pl.loop(1, NT)
                def _(step):
                    project_all(shard_at(step))

            @pl.when(i == 2)
            def _():
                arrive(OUT)

            @pl.when(i == 3)
            def _():
                go_along(DOWN)
                ready(OUT)

            attend(shard_at(i), WIN_DEC)

    @pl.when(is_enc)
    def _():
        encoder_attention()

    @pl.when(is_dec)
    def _():
        decoder_attention()

    both = range(R)
    a0s = [x_ext[r, OWN:OWN + T].astype(F32) + dot(wide(ctx, r), w_out_full()) for r in both]
    for r, (xh, rs) in enumerate([normed(v) for v in a0s]):
        xh1[r] = xh
        rs1[r] = rs
        h = xh * g_row(0) + b_row(0)
        h32[r] = h
        hb[r] = h.astype(BF)

    pad_mask = jnp.where(
        lax.rem(lax.broadcasted_iota(jnp.int32, (256, T), 0), MP) < MEM, 0.0, FILL)

    def full_cross(j):
        return jnp.concatenate([wcross[a, j] for a in range(NT)], axis=1)

    def cross_forward():
        arrive(CROSS)
        come_along(UP)
        ready(CROSS)
        wc0 = full_cross(0)
        wc1 = full_cross(1)
        kblk[...] = jnp.zeros(kblk.shape, BF)
        vblk[...] = jnp.zeros(vblk.shape, BF)

        @pl.loop(0, R)
        def _(r):
            h1b[r] = hb[r]
            q = dot(hb[r], wc0).astype(BF)
            cq[r] = (q.astype(F32) * SCALE).astype(BF)

        for b in range(NT):
            remote(kvm.at[b], kvm.at[b], ksend.at[b], krecv.at[b], section=other, tensor=b).wait_recv()
        for r in range(R):
            for a in range(NT):
                for h in range(2):
                    at = slice(a * 64 + h * MP, a * 64 + h * MP + MP)
                    kblk[r, at, a * 128:a * 128 + 128] = kvm[a, 0, r * MP:r * MP + MP] * hmask[h, 0:MP]
                    vblk[r, at, a * 128:a * 128 + 128] = kvm[a, 1, r * MP:r * MP + MP] * hmask[h, 0:MP]

        ss = [(dot_nt(kblk[r], cq[r]) + pad_mask).reshape(8, MP, T) for r in both]
        ps = []
        for s in ss:
            p = jnp.exp(s - jnp.max(s, axis=1, keepdims=True))
            ps.append((p * (1.0 / jnp.sum(p, axis=1, keepdims=True))).reshape(256, T).astype(BF))
        cs = [dot_tn(p, vblk[r]).astype(BF) for r, p in enumerate(ps)]
        sums = [h32[r] + dot_nt(c, wc1) for r, c in enumerate(cs)]
        for r, (xh, rs) in enumerate([normed(v) for v in sums]):
            cpt[r] = ps[r]
            cctx[r] = cs[r]
            xh2[r] = xh
            rs2[r] = rs
            h = xh * g_row(1) + b_row(1)
            h32[r] = h
            hb[r] = h.astype(BF)

    @pl.when(is_dec)
    def _():
        cross_forward()

    @pl.when(is_enc)
    def _():
        come_along(UP)

    @pl.loop(0, NT)
    def _(i):
        @pl.when(i == 1)
        def _():
            ready(UP)

        a = shard_at(i)
        us = [dot(hb[r], wup[a]) for r in both]
        for r, (av, gv) in enumerate([gelu_both(u) for u in us]):
            act[r, a] = av.astype(BF)
            gp[r, a] = gv.astype(BF)

    @pl.when(is_enc)
    def _():
        for a in range(NT):
            _, gv = gelu_both(dot(mh[...].astype(BF), wup[a]))
            xh2[a // 2, (a % 2) * M:(a % 2) * M + M] = gv

    come_along(DOWN)
    ready(DOWN)

    last = jnp.where(is_enc, 1, 2)
    g_last = jnp.where(is_enc, g_row(1), g_row(2))
    b_last = jnp.where(is_enc, b_row(1), b_row(2))

    def add_norm(at, xh, dy):
        ng[pl.ds(at, 1)] += jnp.sum(dy * xh, axis=0, keepdims=True)
        ng[pl.ds(at + 3, 1)] += jnp.sum(dy, axis=0, keepdims=True)

    row_i = lax.broadcasted_iota(jnp.int32, (T, D), 0)
    is_mem_row = jnp.logical_and(row_i < MEM, jnp.logical_and(is_enc, t == 0))

    thirds = [h32[r] + dot(wide(act, r), wdown[...].reshape(NT * D, D)) for r in both]
    nrms = [normed(v) for v in thirds]
    dys = [jnp.where(is_mem_row, 0.0, d32[r]) for r in both]
    d3s = [norm_back(xh, rs, g_last, dy) for (xh, rs), dy in zip(nrms, dys)]
    for r in both:
        xh, dy = nrms[r][0], dys[r]
        h32[r] = xh * g_last + b_last
        ng[pl.ds(last, 1)] += jnp.sum(dy * xh, axis=0, keepdims=True)
        ng[pl.ds(last + 3, 1)] += jnp.sum(dy, axis=0, keepdims=True)
        d32[r] = d3s[r]
        dab[r] = d3s[r].astype(BF)

    @pl.when(jnp.logical_and(is_enc, t == 0))
    def _():
        for r in range(R):
            h32[r, 0:24] = jnp.where(
                lax.broadcasted_iota(jnp.int32, (24, D), 0) < MEM, md[r * MP:r * MP + 24], h32[r, 0:24])

    y_copy = pltpu.make_async_copy(h32, y_out, lsem.at[9])
    y_copy.start()

    def at(k):
        return CHUNKS[k][0], CHUNKS[k][0] // 2, CHUNKS[k][1] // 2

    def own_half(k):
        start, lo, hf = at(k)
        return start + core * hf

    def shard_of(q):
        return lax.rem(t + 1 + q, NT)

    def rel_of(a):
        return lax.rem(a - t + 3, NT)

    def pair(k, q):
        start, lo, hf = at(k)
        return remote(g.at[q, pl.ds(start + (1 - core) * hf, hf), :], r1.at[q, pl.ds(lo, hf), :],
                      s1.at[k, q], q1.at[k, q], dp=sib)

    def pair_sum(k, q):
        start, lo, hf = at(k)
        rows = pl.ds(own_half(k), hf)
        g[q, rows] = (g[q, rows].astype(F32) + r1[q, lo:lo + hf].astype(F32)).astype(BF)

    def chips_first(k, q):
        start, lo, hf = at(k)
        n = hf // chips
        out = []
        for off in range(1, chips):
            to = chip_at(off)
            out.append(remote(g.at[q, pl.ds(own_half(k) + to * n, n), :],
                              rq.at[off - 1, q, pl.ds((lo - LATE) // chips, n), :],
                              sq.at[k, q, off - 1], qq.at[k, q, off - 1], dp=to * 2 + core))
        return out

    def chips_on(k, some):
        all_pairs_sum(k, some)
        for q in some:
            go(chips_first(k, q))

    def chips_done(k, some):
        start, lo, hf = at(k)
        n = hf // chips
        base = (lo - LATE) // chips
        for q in some:
            come(chips_first(k, q))
            tot = g[q, pl.ds(own_half(k) + chip * n, n)].astype(F32)
            for o in range(chips - 1):
                tot = tot + rq[o, q, base:base + n].astype(F32)
            rqs[q, base:base + n] = tot.astype(BF)

    def tensor_third(k):
        start, lo, hf = at(k)
        rows = pl.ds((lo - LATE) // chips, hf // chips)
        return [remote(rqs.at[q, rows, :], rqr.at[q, rows, :], s2.at[k, q], q2.at[k, q], tensor=shard_of(q))
                for q in range(3)]

    def tensor_third_sum(k, only_own=False):
        start, lo, hf = at(k)
        n = hf // chips
        base = (lo - LATE) // chips
        tot = rqs[3, base:base + n].astype(F32)
        if not only_own:
            for q in range(3):
                tot = tot + rqr[q, base:base + n].astype(F32)
        full[pl.ds(own_half(k) + chip * n, n)] = tot.astype(BF)

    quarter = LATE // 8

    def along_x(k, own):
        some = pl.ds(3, 1) if own else pl.ds(0, 3)
        out = []
        for off in (1, 2, 3):
            to = lax.rem(xi + off, 4)
            out.append(remote(g.at[some, pl.ds(own_half(k) + to * quarter, quarter), :],
                              rx.at[off - 1, some, pl.ds(k * quarter, quarter), :],
                              sx.at[k, int(own), off - 1], qx.at[k, int(own), off - 1], dp=x_dev(off)))
        return out

    def along_x_sum(k, q):
        rows = slice(k * quarter, (k + 1) * quarter)
        tot = g[q, pl.ds(own_half(k) + xi * quarter, quarter)].astype(F32)
        for o in range(3):
            tot = tot + rx[o, q, rows].astype(F32)
        ry_s[q, rows] = tot.astype(BF)

    def tensor_second(k):
        rows = pl.ds(k * quarter, quarter)
        return [remote(ry_s.at[q, rows, :], ry_r.at[q, rows, :], s2.at[k, q], q2.at[k, q], tensor=shard_of(q))
                for q in range(3)]

    def tensor_second_sum(k):
        rows = slice(k * quarter, (k + 1) * quarter)
        tot = ry_s[3, rows].astype(F32)
        for q in range(3):
            tot = tot + ry_r[q, rows].astype(F32)
        zz[0, rows] = tot.astype(BF)

    def over_z(k):
        rows = pl.ds(k * quarter, quarter)
        return [remote(zz.at[0, rows, :], zz.at[1, rows, :], sz.at[k], qz.at[k], dp=z_dev)]

    def over_z_sum(k):
        rows = slice(k * quarter, (k + 1) * quarter)
        full[pl.ds(own_half(k) + xi * quarter, quarter)] = (zz[0, rows].astype(F32) + zz[1, rows].astype(F32)).astype(BF)

    def spread_x(k):
        mine = full.at[pl.ds(own_half(k) + xi * quarter, quarter), :]
        return [remote(mine, mine, s4.at[k, off - 1], q4.at[k, off - 1], dp=x_dev(off)) for off in (1, 2, 3)]

    def spread(k):
        start, lo, hf = at(k)
        n = hf // chips
        mine = full.at[pl.ds(own_half(k) + chip * n, n), :]
        return [remote(mine, mine, s4.at[k, off - 1], q4.at[k, off - 1], dp=chip_at(off) * 2 + core)
                for off in range(1, chips)]

    def hand(k):
        start, lo, hf = at(k)
        mine = full.at[pl.ds(own_half(k), hf), :]
        return [remote(mine, mine, s5.at[k], q5.at[k], dp=sib)]

    def all_pairs(k):
        for q in range(NT):
            pair(k, q).start()

    def all_pairs_sum(k, some=range(NT)):
        for q in some:
            pair(k, q).wait_recv()
            pair_sum(k, q)

    def put_feed(k, q, w):
        for j in range(4):
            g[q, CHUNKS[k][0] + D * j:CHUNKS[k][0] + D * (j + 1)] = w[:, 128 * j:128 * j + 128].astype(BF)

        @pl.when(jnp.logical_or(is_dec, q < 3))
        def _():
            pair(k, q).start()

    @pl.loop(0, NT)
    def _(q):
        a = shard_of(q)
        put_feed(C_DOWN, q, dot_tn(act[0, a], dab[0]) + dot_tn(act[1, a], dab[1]))

    @pl.loop(0, NT)
    def _(a):
        dacts = [dot_nt(dab[r], wdown[a]) for r in both]
        for r in both:
            gp[r, a] = (dacts[r] * gp[r, a].astype(F32)).astype(BF)

    w_up_all = jnp.concatenate([wup[a] for a in range(NT)], axis=1)
    for r in both:
        d32[r] += dot_nt(wide(gp, r), w_up_all)

    def feed_on(k):
        all_pairs_sum(k, range(3))
        go(along_x(k, False))

        @pl.when(is_dec)
        def _():
            all_pairs_sum(k, (3,))
            go(along_x(k, True))

    feed_on(C_DOWN)

    dkv_copies = [
        remote(dkvm_s.at[b], dkvm_r.at[t], dsend.at[b], drecv.at[t], section=other, tensor=b) for b in range(NT)
    ]

    def cross_backward():
        wc0 = full_cross(0)
        wc1 = full_cross(1)

        dys = [d32[r] for r in both]
        d2s = [norm_back(xh2[r], rs2[r], g_row(1), dys[r]) for r in both]
        dcs = []
        for r in both:
            d32[r] = d2s[r]
            cdb[r] = d2s[r].astype(BF)
        for r in both:
            dcs.append(dot(cdb[r], wc1).astype(BF))
        dps = [dot_nt(vblk[r], dcs[r]).reshape(8, MP, T) for r in both]
        dss = []
        for r in both:
            p = cpt[r].astype(F32).reshape(8, MP, T)
            ds = p * (dps[r] - jnp.sum(p * dps[r], axis=1, keepdims=True))
            dss.append(ds.reshape(256, T).astype(BF))
        dks = [dot(dss[r], cq[r]) for r in both]
        dvs = [dot(cpt[r], dcs[r]) for r in both]
        for r in both:
            rows = slice(r * MP, r * MP + MP)
            for a in range(NT):
                for j, val in ((0, dks[r]), (1, dvs[r])):
                    dkvm_s[a, j, rows] = jnp.where(
                        low_m, val[64 * a:64 * a + MP, 128 * a:128 * a + 128],
                        val[64 * a + MP:64 * a + 2 * MP, 128 * a:128 * a + 128])
        go(dkv_copies)
        dqs = [(dot_tn(dss[r], kblk[r]) * SCALE).astype(BF) for r in both]
        for r in both:
            add_norm(1, xh2[r], dys[r])
            cq[r] = dqs[r]
        for r in both:
            d32[r] += dot_nt(dqs[r], wc0)

    def cross_grads():
        gq = dot_tn(h1b[0], cq[0]) + dot_tn(h1b[1], cq[1])
        go_ = dot_tn(cdb[0], cctx[0]) + dot_tn(cdb[1], cctx[1])
        for a in range(NT):
            q = rel_of(a)
            g[q, G_CROSS:G_CROSS + D] = gq[:, 128 * a:128 * a + 128].astype(BF)
            g[q, G_CROSS + D:G_CROSS + 2 * D] = go_[:, 128 * a:128 * a + 128].astype(BF)
        all_pairs(C_CROSS)

    @pl.when(is_dec)
    def _():
        cross_backward()

    @pl.loop(0, NT)
    def _(q):
        a = shard_of(q)
        put_feed(C_UP, q, dot_tn(hb[0], gp[0, a]) + dot_tn(hb[1], gp[1, a]))

    dys1 = [d32[r] for r in both]
    d1s = [norm_back(xh1[r], rs1[r], g_row(0), dys1[r]) for r in both]
    for r in both:
        d32[r] = d1s[r]
        dab[r] = d1s[r].astype(BF)
    for r in both:
        drr = dot_nt(dab[r], w_out_full()).astype(BF)
        for a in range(NT):
            dr[r, a] = drr[:, 128 * a:128 * a + 128]
    for r in both:
        add_norm(0, xh1[r], dys1[r])

    def out_grads():
        wo_all = dot_tn(wide(ctx, 0), dab[0]) + dot_tn(wide(ctx, 1), dab[1])
        for a in range(NT):
            for j in range(4):
                g[rel_of(a), G_OUT + 128 * j:G_OUT + 128 * j + 128] = (
                    wo_all[128 * a:128 * a + 128, 128 * j:128 * j + 128].astype(BF))
        for q in range(3):
            pair(C_OUT, q).start()

        @pl.when(is_dec)
        def _():
            pair(C_OUT, 3).start()

    feed_on(C_UP)

    def attend_back(a, windows, encoder):
        jobs = [(r, b, w0, wn) for r in range(R) for b, (w0, wn) in enumerate(windows)]
        k_t = [turned(kk, a, r, windows[1][0] + windows[1][1]) for r in range(R)]
        drs, dps, dss = [], [], []
        for r, b, w0, wn in jobs:
            d_r = dr[r, a, b * 128:b * 128 + 128]
            d_r = jnp.concatenate([d_r * hmask[0, 0:128], d_r * hmask[1, 0:128]], axis=0)
            drs.append(d_r)
            dps.append(dot_nt(vv[a, r, w0:w0 + wn], d_r))
        for (r, b, w0, wn), dp_ in zip(jobs, dps):
            p = pt[a, r, b, 0:wn].astype(F32)
            dss.append((p * (dp_ - jnp.sum(p * dp_, axis=0, keepdims=True))).astype(BF))
        dks, dvs = [], []
        for (r, b, w0, wn), ds, d_r in zip(jobs, dss, drs):
            dq = dot(k_t[r][:, w0:w0 + wn], ds)
            dq = jnp.concatenate([dq[0:64, 0:128], dq[64:128, 128:256]], axis=0)
            act[r, a, b * 128:b * 128 + 128, 0:128] = (dq.T * SCALE).astype(BF)
            dks.append(dot(ds, qs[a, r, b]))
            dvs.append(dot(pt[a, r, b, 0:wn], d_r))
        (_, n0), (w1, n1_) = windows
        for r in range(R):
            for j, parts in enumerate((dks, dvs)):
                lo, hi = parts[2 * r], parts[2 * r + 1]
                both = lo[w1:n0] + hi[0:n0 - w1]
                val = jnp.concatenate([lo[0:w1], both, hi[n0 - w1:n1_]], axis=0)
                dkv[a, r, j] = val[OWN:OWN + T]
                halo_s[0, a, r, j] = val[LEFT:LEFT + HALO].astype(BF)
                if encoder:
                    halo_s[1, a, r, j] = val[RIGHT:RIGHT + HALO].astype(BF)
                    mg_s[a, r, j + 1] = (val[0:MP] + val[MEM_2:MEM_2 + MP]).astype(BF)

    def halo_copies(a):
        return (remote(halo_s.at[0, a], halo_r.at[0, a], hsend.at[0, a], hrecv.at[0, a], tensor=left),
                remote(halo_s.at[1, a], halo_r.at[1, a], hsend.at[1, a], hrecv.at[1, a], tensor=right))

    first = jnp.where(t == 0, 1.0, 0.0)
    mg_copies = [remote(mg_s.at[lax.rem(t + off, NT)], mg_r.at[off - 1], qsend.at[off - 1], qrecv.at[off - 1],
                        tensor=lax.rem(t + off, NT)) for off in (1, 2, 3)]

    def add_g(start, val):
        n = val.shape[0]
        g[3, start:start + n] = (g[3, start:start + n].astype(F32) + val).astype(BF)

    def add_norm_m(at_, xh, dy):
        ng[at_:at_ + 1] += first * jnp.sum(dy * xh, axis=0, keepdims=True)
        ng[at_ + 3:at_ + 4] += first * jnp.sum(dy, axis=0, keepdims=True)

    def mem_back_first():
        for b in range(NT):
            remote(dkvm_s.at[b], dkvm_r.at[b], dsend.at[b], drecv.at[b], section=other, tensor=b).wait_recv()
        grads = []
        for j in range(2):
            tot = dkvm_r[0, j] + dkvm_r[1, j] + dkvm_r[2, j] + dkvm_r[3, j]
            grads.append(tot.astype(BF))
        ex_m[t] = (dot_nt(grads[0], wcross[t, 0]) + dot_nt(grads[1], wcross[t, 1])).astype(BF)
        ex_start(3)
        for j in range(2):
            g[3, G_CROSS + D * j:G_CROSS + D * j + D] = dot_tn(mm[...], grads[j]).astype(BF)
        pair(C_CROSS, 3).start()

    def mem_back_second():
        ex_wait(3)
        dm = ex_m[0].astype(F32)
        for s in range(1, NT):
            dm = dm + ex_m[s].astype(F32)
        add_norm_m(2, mx3[...], dm)
        rows_m = lax.broadcasted_iota(jnp.int32, (R * MP, D), 0)

        @pl.when(t == 0)
        def _():
            mem_local[1].wait()

        @pl.when(t > 0)
        def _():
            mem_c[0].wait_recv()

        cm = jnp.concatenate([cotm[0], cotm[1]], axis=0)
        cm = jnp.where(lax.rem(rows_m, MP) < MEM, cm, 0.0)
        dy = cm + norm_back(mx3[...], mr3[...], g_row(2), dm)
        add_norm_m(1, mx2[...], dy)
        d3 = norm_back(mx2[...], mr2[...], g_row(1), dy)
        d3b = d3.astype(BF)
        d2 = d3
        for a in range(NT):
            dum = (dot_nt(d3b, wdown[a]) * xh2[a // 2, (a % 2) * M:(a % 2) * M + M]).astype(BF)
            d2 = d2 + dot_nt(dum, wup[a])
            mdu[a] = dum
        wd = dot_tn(mact[...], d3b)
        wu = dot_tn(mh[...].astype(BF), mdu[t])
        md[...] = d2
        for j in range(4):
            add_g(G_DOWN + D * j, wd[:, 128 * j:128 * j + 128])
            add_g(G_UP + D * j, wu[:, 128 * j:128 * j + 128])
        pair(C_DOWN, 3).start()
        pair(C_UP, 3).start()

    def mem_back_third():
        d2 = md[...]
        add_norm_m(0, mx1[...], d2)
        d1 = norm_back(mx1[...], mr1[...], g_row(0), d2)
        md[...] = d1
        d1b = d1.astype(BF)
        dmb[...] = d1b
        drm = dot_nt(d1b, w_out_full()).astype(BF).astype(F32)
        mh[...] = drm
        prod = drm * mc[...]
        for r in range(R):
            acc = jnp.zeros((MP, 128), F32)
            for hh in range(8):
                cols = prod[r * MP:r * MP + MP, (hh // 2) * 128:(hh // 2) * 128 + 128]
                cols = jnp.where(low_m if hh % 2 == 0 else jnp.logical_not(low_m), cols, 0.0)
                acc = jnp.where(lane_m == hh, jnp.sum(cols, axis=1, keepdims=True), acc)
            mst[1, r * MP:r * MP + MP] = acc
    def mem_out():
        for a in range(NT):
            @pl.when(t == a)
            def _():
                wo = dot_tn(mc[:, 128 * a:128 * a + 128].astype(BF), dmb[...])
                for j in range(4):
                    add_g(G_OUT + 128 * j, wo[:, 128 * j:128 * j + 128])
        pair(C_OUT, 3).start()

    def mem_attend_back():
        jobs = [(a, r) for a in range(NT) for r in range(R)]
        ss = [dot_nt(qm[a, r], kk[a, r, OWN:OWN + T]) for a, r in jobs]
        dras, dlts, ps = [], [], []
        for (a, r), s in zip(jobs, ss):
            rows = slice(r * MP, r * MP + MP)
            lse = mst[0, rows]
            dlt = mst[1, rows]
            lse = jnp.concatenate([lse[:, 2 * a:2 * a + 1], lse[:, 2 * a + 1:2 * a + 2]], axis=0)
            dlts.append(jnp.concatenate([dlt[:, 2 * a:2 * a + 1], dlt[:, 2 * a + 1:2 * a + 2]], axis=0))
            ps.append(jnp.exp(s - lse))
            dra = mh[rows, 128 * a:128 * a + 128]
            dras.append(
                jnp.concatenate([jnp.where(low_m, dra, 0.0), jnp.where(low_m, 0.0, dra)], axis=0).astype(BF))
        dps = [dot_nt(d, vv[a, r, OWN:OWN + T]) for d, (a, r) in zip(dras, jobs)]
        dss = [(p * (dp_ - dlt)).astype(BF) for p, dp_, dlt in zip(ps, dps, dlts)]
        dqs = [dot(ds, kk[a, r, OWN:OWN + T]) for ds, (a, r) in zip(dss, jobs)]
        for (a, r), dq in zip(jobs, dqs):
            mg_s[a, r, 0] = (jnp.where(low_m, dq[0:MP], dq[MP:2 * MP]) * SCALE).astype(BF)
        go(mg_copies)
        for (a, r), ds, p, dra in zip(jobs, dss, ps, dras):
            dkv[a, r, 0] += dot_tn(ds, qm[a, r])
            dkv[a, r, 1] += dot_tn(p.astype(BF), dra)

    def x_done(k, own):
        come(along_x(k, own))
        if own:
            along_x_sum(k, 3)
            return
        for q in range(3):
            along_x_sum(k, q)
        go(tensor_second(k))

    def order(i):
        return jnp.where(i == 0, 1, jnp.where(i == 1, 0, i))

    @pl.loop(0, NT)
    def _(i):
        a = shard_of(order(i))

        @pl.when(is_enc)
        def _():
            attend_back(a, WIN_ENC, True)

        @pl.when(is_dec)
        def _():
            attend_back(a, WIN_DEC, False)

        to_left, to_right = halo_copies(a)
        to_left.start()

        @pl.when(is_enc)
        def _():
            to_right.start()

        @pl.when(is_dec)
        def _():
            @pl.when(i == 3)
            def _():
                cross_grads()
                x_done(C_DOWN, False)
                x_done(C_DOWN, True)

        @pl.when(is_enc)
        def _():
            @pl.when(i == 0)
            def _():
                mem_back_first()

            @pl.when(i == 2)
            def _():
                mem_back_second()

            @pl.when(i == 3)
            def _():
                mem_back_third()

    n1 = [remote(ny.at[t], ny.at[t], ns.at[o - 1], nq.at[o - 1], tensor=lax.rem(t + o, NT)) for o in (1, 2, 3)]
    n2 = [remote(nc.at[0], nc.at[1], ns.at[3], nq.at[3], dp=sib)]
    n3 = [remote(nx.at[chip], nx.at[chip], ns.at[3 + o], nq.at[3 + o], dp=chip_at(o) * 2 + core)
          for o in range(1, chips)]

    def query_grads(q):
        a = shard_of(q)
        gw = dot_tn(x_ext[0, OWN:OWN + T], act[0, a, :, 0:128]) + dot_tn(x_ext[1, OWN:OWN + T], act[1, a, :, 0:128])
        g[q, G_QKV:G_QKV + D] = gw.astype(BF)

    def mem_last():
        mem_attend_back()
        for k in (C_DOWN, C_UP):
            all_pairs_sum(k, (3,))
            go(along_x(k, True))
        out_grads()
        mem_out()
        chips_on(C_CROSS, (3,))
        for q in range(NT):
            query_grads(q)
        for q in range(3):
            pair(C_Q, q).start()
        chips_on(C_OUT, range(NT))
        chips_on(C_Q, range(3))

    def decoder_last():
        out_grads()
        for q in range(NT):
            query_grads(q)
            pair(C_Q, q).start()
        chips_on(C_CROSS, range(NT))
        chips_on(C_OUT, range(NT))
        chips_on(C_Q, range(NT))

    ny[t] = ng[...]
    go(n1)

    @pl.when(is_dec)
    def _():
        decoder_last()

    @pl.when(is_enc)
    def _():
        mem_last()

    dxm_copy = remote(dxm_s, dxm_r.at[t], gsend.at[0], grecv.at[t], tensor=0)

    def mem_own():
        come(mg_copies)
        cols = []
        for j in range(3):
            both = []
            for r in range(R):
                tot = mg_s[t, r, j].astype(F32)
                for o in range(3):
                    tot = tot + mg_r[o, r, j].astype(F32)
                both.append(tot)
            cols.append(jnp.concatenate(both, axis=0))
        dm = jnp.concatenate(cols, axis=1).astype(BF)
        gw = dot_tn(x_mem(), dm)
        for j in range(3):
            add_g(G_QKV + D * j, gw[:, 128 * j:128 * j + 128])
        pair(C_Q, 3).start()
        pair(C_KV, 3).start()
        return dm

    def qkv_full(a):
        return jnp.concatenate([wqkv[a, j] for j in range(3)], axis=1)

    @pl.when(is_dec)
    def _():
        come(tensor_second(C_DOWN))
        tensor_second_sum(C_DOWN)
        go(over_z(C_DOWN))

    @pl.loop(0, NT)
    def _(i):
        q = order(i)
        a = shard_of(q)
        to_left, to_right = halo_copies(a)
        to_left.wait_recv()

        @pl.when(is_enc)
        def _():
            to_right.wait_recv()

        for r in range(R):
            for j in range(2):
                dkv[a, r, j, T - HALO:T] += halo_r[0, a, r, j].astype(F32)

                @pl.when(is_enc)
                def _():
                    dkv[a, r, j, 0:HALO] += halo_r[1, a, r, j].astype(F32)

                act[r, a, :, 128 * (j + 1):128 * (j + 2)] = dkv[a, r, j].astype(BF)
        gw = (dot_tn(x_ext[0, OWN:OWN + T], act[0, a, :, 128:384])
              + dot_tn(x_ext[1, OWN:OWN + T], act[1, a, :, 128:384]))
        for j in range(2):
            g[q, G_KV + D * j:G_KV + D * j + D] = gw[:, 128 * j:128 * j + 128].astype(BF)

        @pl.when(jnp.logical_or(is_dec, q < 3))
        def _():
            pair(C_KV, q).start()

        @pl.when(jnp.logical_and(is_enc, q == 3))
        def _():
            dm = mem_own()
            dxm_s[...] = dot_nt(dm, qkv_full(t)).astype(BF)

            @pl.when(t > 0)
            def _():
                dxm_copy.start()

        @pl.when(i > 0)
        def _():
            q_before = order(i - 1)
            pair(C_KV, q_before).wait_recv()
            pair_sum(C_KV, q_before)
            go(chips_first(C_KV, q_before))

    chips_on(C_KV, (3,))

    @pl.when(is_enc)
    def _():
        chips_on(C_Q, (3,))

    come(n1)
    nc[0] = ny[0] + ny[1] + ny[2] + ny[3]
    go(n2)

    @pl.when(is_enc)
    def _():
        x_done(C_DOWN, False)
        x_done(C_UP, False)

    @pl.when(is_dec)
    def _():
        x_done(C_UP, False)
        x_done(C_UP, True)
        chips_done(C_CROSS, range(NT))
        go(tensor_third(C_CROSS))

    w_qkv_all = jnp.concatenate([qkv_full(a) for a in range(NT)], axis=1)
    for r in both:
        d_all = jnp.concatenate([act[r, a, :, 0:384] for a in range(NT)], axis=1)
        d32[r] += dot_nt(d_all, w_qkv_all)

    come(n2)
    nx[chip] = nc[0] + nc[1]
    go(n3)

    @pl.when(is_dec)
    def _():
        come(over_z(C_DOWN))
        over_z_sum(C_DOWN)
        go(spread_x(C_DOWN))

    @pl.when(is_enc)
    def _():
        x_done(C_DOWN, True)
        x_done(C_UP, True)
        chips_done(C_CROSS, (3,))
        tensor_third_sum(C_CROSS, True)
        go(spread(C_CROSS))

    for k in (C_OUT, C_Q, C_KV):
        chips_done(k, range(NT))
        go(tensor_third(k))

    @pl.when(is_enc)
    def _():
        come(tensor_second(C_DOWN))
        tensor_second_sum(C_DOWN)
        go(over_z(C_DOWN))

    @pl.when(is_dec)
    def _():
        come(tensor_third(C_CROSS))
        tensor_third_sum(C_CROSS)
        go(spread(C_CROSS))

    come(tensor_second(C_UP))
    tensor_second_sum(C_UP)
    go(over_z(C_UP))
    for k in (C_OUT, C_Q, C_KV):
        come(tensor_third(k))
        tensor_third_sum(k)
        go(spread(k))

    @pl.when(is_enc)
    def _():
        come(over_z(C_DOWN))
        over_z_sum(C_DOWN)
        go(spread_x(C_DOWN))

    come(over_z(C_UP))
    over_z_sum(C_UP)
    go(spread_x(C_UP))

    @pl.when(jnp.logical_and(is_enc, t == 0))
    def _():
        tot = md[...] + dxm_s[...].astype(F32)
        for s in range(1, NT):
            remote(dxm_s, dxm_r.at[s], gsend.at[0], grecv.at[s], tensor=0).wait_recv()
            tot = tot + dxm_r[s].astype(F32)
        for r in range(R):
            d32[r, 0:MP] += tot[r * MP:r * MP + MP]

    dx_copy = pltpu.make_async_copy(d32, dx_out, lsem.at[10])
    dx_copy.start()
    come(n3)
    tot_n = nx[0]
    for o in range(1, chips):
        tot_n = tot_n + nx[o]
    ng_tot[...] = tot_n
    come(spread(C_CROSS))
    go(hand(C_CROSS))
    come(spread_x(C_DOWN))
    go(hand(C_DOWN))
    for k in (C_OUT, C_Q, C_KV):
        come(spread(k))
        go(hand(k))
    come(spread_x(C_UP))
    go(hand(C_UP))
    for k in range(CN):
        come(hand(k))

    y_copy.wait()
    dx_copy.wait()
    gone(w_direct(OUT))
    gone(w_pair(OUT))
    for i in (QKV, UP, DOWN):
        gone(w_eighth(i))
        gone(w_along(i))
        gone(w_pair(i))
    x_right.wait_send()
    for a in range(NT):
        halo_copies(a)[0].wait_send()
    gone(n1)
    gone(n2)
    gone(n3)
    for k in range(CN):
        if k in (C_DOWN, C_UP):
            gone(along_x(k, False))
            gone(along_x(k, True))
            gone(tensor_second(k))
            gone(over_z(k))
            gone(spread_x(k))
        else:
            gone(spread(k))
        if k in (C_OUT, C_Q, C_KV):
            for q in range(NT):
                gone(chips_first(k, q))
            gone(tensor_third(k))
        if k != C_CROSS:
            gone([pair(k, q) for q in range(NT)])
        gone(hand(k))

    @pl.when(is_dec)
    def _():
        gone(w_direct(CROSS))
        gone(w_pair(CROSS))
        gone(dkv_copies)
        gone([pair(C_CROSS, q) for q in range(NT)])
        for q in range(NT):
            gone(chips_first(C_CROSS, q))
        gone(tensor_third(C_CROSS))

    @pl.when(is_enc)
    def _():
        x_left.wait_send()
        pair(C_CROSS, 3).wait_send()
        gone(chips_first(C_CROSS, 3))
        for a in range(NT):
            halo_copies(a)[1].wait_send()
        for e in range(4):
            gone(exchanges[e])
        gone(mg_copies)
        gone(kv_copies)

        @pl.when(t == 0)
        def _():
            gone(mem_x)
            gone(mem_c)

        @pl.when(t > 0)
        def _():
            dxm_copy.wait_send()


def layer_call(chips, lens, x, cot, wqkv, wout, wcross, wup, wdown, gain, bias):
    any_ = pl.BlockSpec(memory_space=pl.ANY)
    vmem = pl.BlockSpec(memory_space=pltpu.VMEM)
    W = W_ENC
    S = pltpu.SemaphoreType.DMA
    C = len(CHUNKS)
    o = max(chips - 1, 1)
    late = HALF - LATE

    def V(shape, kind):
        return pltpu.VMEM(shape, kind)

    scratch = dict(
        x_ext=V((R, W, D), BF), cotm=V((R, MP, D), F32), d32=V((R, T, D), F32),
        wqkv=V((NT, 3, D, 128), BF), wout=V((NT, 128, D), BF), wcross=V((NT, 2, D, 128), BF),
        wup=V((NT, D, D), BF), wdown=V((NT, D, D), BF),
        kk=V((NT, R, W, 128), BF), vv=V((NT, R, W, 128), BF),
        qs=V((NT, R, 2, T, 128), BF), pt=V((NT, R, 2, 512, T), BF), ctx=V((R, NT, T, 128), BF),
        mask=V((R, 2, 512, 128), F32), hmask=V((2, T, 128), BF),
        xh1=V((R, T, D), F32), xh2=V((R, T, D), F32), rs1=V((R, T, 1), F32), rs2=V((R, T, 1), F32),
        h32=V((R, T, D), F32), hb=V((R, T, D), BF), h1b=V((R, T, D), BF),
        act=V((R, NT, T, D), BF), gp=V((R, NT, T, D), BF), dab=V((R, T, D), BF), dr=V((R, NT, T, 128), BF),
        dkv=V((NT, R, 2, T, 128), F32), halo_s=V((2, NT, R, 2, HALO, 128), BF),
        halo_r=V((2, NT, R, 2, HALO, 128), BF), mg_s=V((NT, R, 3, MP, 128), BF), mg_r=V((3, R, 3, MP, 128), BF),
        dxm_s=V((M, D), BF), dxm_r=V((NT, M, D), BF), mdu=V((NT, M, D), BF),
        ex_o=V((NT, NT, M, 128), BF), ex_st=V((NT, M, 128), F32), ex_f=V((NT, M, D), BF), ex_m=V((NT, M, D), BF),
        qm=V((NT, R, 2 * MP, 128), BF),
        kvm=V((NT, 2, M, 128), BF), dkvm_s=V((NT, 2, M, 128), F32), dkvm_r=V((NT, 2, M, 128), F32),
        kblk=V((R, 256, D), BF), vblk=V((R, 256, D), BF), cpt=V((R, 256, T), BF), cq=V((R, T, D), BF),
        cctx=V((R, T, D), BF), cdb=V((R, T, D), BF),
        mx1=V((M, D), F32), mx2=V((M, D), F32), mx3=V((M, D), F32), mr1=V((M, 1), F32), mr2=V((M, 1), F32),
        mr3=V((M, 1), F32), mh=V((M, D), F32), mact=V((M, D), BF), mc=V((M, D), F32),
        mm=V((M, D), BF), mst=V((2, M, 128), F32), md=V((M, D), F32), dmb=V((M, D), BF),
        g=V((NT, G_ROWS, 128), BF), r1=V((NT, HALF, 128), BF),
        rx=V((3, NT, LATE // 4, 128), BF), ry_s=V((NT, LATE // 4, 128), BF),
        ry_r=V((3, LATE // 4, 128), BF), zz=V((2, LATE // 4, 128), BF),
        rq=V((o, NT, late // chips, 128), BF), rqs=V((NT, late // chips, 128), BF), rqr=V((3, late // chips, 128), BF),
        ng=V((8, D), F32), ny=V((NT, 8, D), F32), nc=V((2, 8, D), F32),
        nx=V((chips, 8, D), F32),
        lsem=S((11,)), wsend=S((5, 6)), wrecv=S((5, 6)), w2send=S((3, 3, 3)), w2recv=S((3, 3, 3)), xsend=S((2,)), xrecv=S((2,)), msend=S((2, 3)), mrecv=S((2,)),
        esend=S((5, 3)), erecv=S((5, 3)), ksend=S((NT,)), krecv=S((NT,)), dsend=S((NT,)), drecv=S((NT,)),
        hsend=S((2, NT)), hrecv=S((2, NT)), gsend=S((1,)), grecv=S((NT,)), qsend=S((3,)), qrecv=S((3,)), sq=S((C, NT, o)), qq=S((C, NT, o)),
        s1=S((C, NT)), q1=S((C, NT)), s2=S((C, 3)), q2=S((C, 3)),
        s4=S((C, o)), q4=S((C, o)), s5=S((C,)), q5=S((C,)), ns=S((4 + o,)), nq=S((4 + o,)),
        sx=S((2, 2, 3)), qx=S((2, 2, 3)), sz=S((2,)), qz=S((2,)),
    )
    names = tuple(scratch)

    def kernel(*refs):
        layer_kernel(chips, names, *refs)

    return pl.pallas_call(
        kernel,
        out_shape=(
            jax.ShapeDtypeStruct((R, T, D), F32),
            jax.ShapeDtypeStruct((R, T, D), F32),
            jax.ShapeDtypeStruct((G_ROWS, 128), BF),
            jax.ShapeDtypeStruct((8, D), F32),
        ),
        in_specs=[pl.BlockSpec(memory_space=pltpu.SMEM)] + [any_] * 7 + [vmem] * 2,
        out_specs=(any_, any_, vmem, vmem),
        scratch_shapes=list(scratch.values()),
        compiler_params=pltpu.CompilerParams(
            collective_id=0, has_side_effects=True, vmem_limit_bytes=VMEM_BYTES
        ),
        name="layers",
    )(lens, x, cot, wqkv, wout, wcross, wup, wdown, gain, bias)


def finish_kernel(y_in, dx_in, full, ng, y, dx, o_qkv, o_out, o_cross, o_up, o_down, o_gain, o_bias, sems):
    copies = [pltpu.make_async_copy(y_in, y.at[0], sems.at[0]), pltpu.make_async_copy(dx_in, dx.at[0], sems.at[1])]
    for c in copies:
        c.start()
    for j in range(3):
        o_qkv[0, j] = full[G_QKV + D * j:G_QKV + D * j + D].astype(F32)
    for j in range(2):
        o_cross[0, j] = full[G_CROSS + D * j:G_CROSS + D * j + D].astype(F32)
    for j in range(4):
        cols = slice(128 * j, 128 * j + 128)
        o_out[0, :, cols] = full[G_OUT + 128 * j:G_OUT + 128 * j + 128].astype(F32)
        o_up[0, :, cols] = full[G_UP + D * j:G_UP + D * j + D].astype(F32)
        o_down[0, :, cols] = full[G_DOWN + D * j:G_DOWN + D * j + D].astype(F32)
    for i in range(3):
        o_gain[i] = ng[i:i + 1]
        o_bias[i] = ng[i + 3:i + 4]
    for c in copies:
        c.wait()


def finish_call(y, dx, full, ng):
    any_ = pl.BlockSpec(memory_space=pl.ANY)
    vmem = pl.BlockSpec(memory_space=pltpu.VMEM)
    shapes = ((1, R, T, D), (1, R, T, D), (1, 3, D, 128), (1, 128, D), (1, 2, D, 128), (1, D, D), (1, D, D),
              (3, 1, D), (3, 1, D))
    return pl.pallas_call(
        finish_kernel,
        out_shape=tuple(jax.ShapeDtypeStruct(s, F32) for s in shapes),
        in_specs=[vmem] * 4,
        out_specs=(any_, any_) + (vmem,) * 7,
        scratch_shapes=[pltpu.SemaphoreType.DMA((2,))],
        compiler_params=pltpu.CompilerParams(vmem_limit_bytes=VMEM_BYTES),
        name="finish",
    )(y, dx, full, ng)


def solution(mesh):
    chips = mesh.shape["dp"] // 2

    def shards(inputs, lengths, w_qkv, w_out, w_cross, w_up, w_down, norm_gain, norm_bias, cotangent):
        y, dx, full, ng = layer_call(
            chips, lengths, inputs[0], cotangent[0], w_qkv[0], w_out[0], w_cross[0], w_up[0], w_down[0],
            jnp.transpose(norm_gain, (1, 0, 2)), jnp.transpose(norm_bias, (1, 0, 2)))
        outs = finish_call(y, dx, full, ng)
        return outs[:7] + tuple(jnp.transpose(v, (1, 0, 2)) for v in outs[7:])

    return jax.shard_map(
        shards,
        mesh=mesh,
        in_specs=(
            P("section", "dp", "tensor", None),
            P("dp", None),
            P("section", None, None, "tensor"),
            P("section", "tensor", None),
            P("section", None, None, "tensor"),
            P("section", None, "tensor"),
            P("section", "tensor", None),
            P("section", None, None),
            P("section", None, None),
            P("section", "dp", "tensor", None),
        ),
        out_specs=(
            P("section", "dp", "tensor", None),
            P("section", "dp", "tensor", None),
            P("section", None, None, "tensor"),
            P("section", "tensor", None),
            P("section", None, None, "tensor"),
            P("section", None, "tensor"),
            P("section", "tensor", None),
            P("section", None, None),
            P("section", None, None),
        ),
        check_vma=False,
    )
```

```python
import jax
import jax.numpy as jnp
from jax import lax
from jax.experimental import pallas as pl
from jax.experimental.pallas import tpu as pltpu
from jax.sharding import PartitionSpec as P

F32 = jnp.float32
BF = jnp.bfloat16
MESH = pl.DeviceIdType.MESH
VMEM_BYTES = 62 * 1024 * 1024

MEM = 20
MP = 32
R = 2
M = R * MP
T = 256
HALO = 160
D = 512
NT = 4
LEFT, OWN, RIGHT, MEM_2, W_ENC = 32, 192, 448, 608, 640
W_DEC = RIGHT
WIN_ENC = ((0, 480), (128, 512))
WIN_DEC = ((0, 320), (128, 320))
EPS = 1e-05
FILL = -1e30
SCALE = 0.125

G_DOWN, G_UP, G_CROSS, G_OUT, G_QKV, G_ROWS = 0, 2048, 4096, 5120, 5632, 7168
G_KV = G_QKV + 512
CHUNKS = ((G_DOWN, 2048), (G_UP, 2048), (G_CROSS, 1024), (G_OUT, 512), (G_QKV, 512), (G_KV, 1024))
CN = len(CHUNKS)
C_DOWN, C_UP, C_CROSS, C_OUT, C_Q, C_KV = range(CN)
LATE = G_CROSS // 2
LAST = G_OUT // 2
HALF = G_ROWS // 2
QKV, OUT, CROSS, UP, DOWN = range(5)
ALONG = {QKV: 0, UP: 1, DOWN: 2}
W_ROWS = (512, 128, 512, 512, 512)


def dot(a, b):
    return lax.dot_general(a, b, (((1,), (0,)), ((), ())), preferred_element_type=F32)


def dot_nt(a, b):
    return lax.dot_general(a, b, (((1,), (1,)), ((), ())), preferred_element_type=F32)


def dot_tn(a, b):
    return lax.dot_general(a, b, (((0,), (0,)), ((), ())), preferred_element_type=F32)


def remote(src, dst, send, recv, **device):
    return pltpu.make_async_remote_copy(
        src_ref=src, dst_ref=dst, send_sem=send, recv_sem=recv, device_id=device, device_id_type=MESH
    )


def normed(v):
    c = v - jnp.mean(v, axis=1, keepdims=True)
    rs = lax.rsqrt(jnp.mean(c * c, axis=1, keepdims=True) + EPS)
    return c * rs, rs


def norm_back(xhat, rs, gain, dy):
    dxh = dy * gain
    m1 = jnp.mean(dxh, axis=1, keepdims=True)
    m2 = jnp.mean(dxh * xhat, axis=1, keepdims=True)
    return rs * (dxh - m1 - xhat * m2)


def gelu_both(u):
    k = 0.7978845608028654
    u2 = u * u
    th = jnp.tanh(k * u * (1.0 + 0.044715 * u2))
    half = 0.5 * (1.0 + th)
    grad = half + 0.5 * u * (1.0 - th * th) * (k * (1.0 + 3.0 * 0.044715 * u2))
    return u * half, grad


def layer_kernel(chips, names, *refs):
    (lens, x_in, cot_in, wqkv_in, wout_in, wcross_in, wup_in, wdown_in, gain, bias,
     y_out, dx_out, full, ng_tot) = refs[:14]
    m = dict(zip(names, refs[14:]))
    x_ext, cotm, d32, wqkv, wout, wcross, wup, wdown = (
        m[n] for n in ("x_ext", "cotm", "d32", "wqkv", "wout", "wcross", "wup", "wdown"))
    kk, vv, qs, pt, ctx, mask, hmask = (m[n] for n in ("kk", "vv", "qs", "pt", "ctx", "mask", "hmask"))
    xh1, xh2, rs1, rs2, h32, hb, h1b, act, gp, dab, dr = (
        m[n] for n in ("xh1", "xh2", "rs1", "rs2", "h32", "hb", "h1b", "act", "gp", "dab", "dr"))
    dkv, halo_s, halo_r, mg_s, mg_r, dxm_s, dxm_r, mdu = (
        m[n] for n in ("dkv", "halo_s", "halo_r", "mg_s", "mg_r", "dxm_s", "dxm_r", "mdu"))
    ex_o, ex_st, ex_f, ex_m, qm, rq, rqs, rqr, r2, r3, ysum = (
        m[n] for n in ("ex_o", "ex_st", "ex_f", "ex_m", "qm", "rq", "rqs", "rqr", "r2", "r3", "ysum"))
    kvm, dkvm_s, dkvm_r, kblk, vblk, cpt, cq, cctx = (
        m[n] for n in ("kvm", "dkvm_s", "dkvm_r", "kblk", "vblk", "cpt", "cq", "cctx"))
    mx1, mx2, mx3, mr1, mr2, mr3, mh, mact, mc, mm, mst, md = (
        m[n] for n in ("mx1", "mx2", "mx3", "mr1", "mr2", "mr3", "mh", "mact", "mc", "mm", "mst", "md"))
    g, r1, rx, ry_s, ry_r, zz, ng, ny, nc, nx, cdb, dmb = (
        m[n] for n in ("g", "r1", "rx", "ry_s", "ry_r", "zz", "ng", "ny", "nc", "nx", "cdb", "dmb"))
    (lsem, wsend, wrecv, xsend, xrecv, msend, mrecv, esend, erecv, ksend, krecv, dsend, drecv,
     hsend, hrecv, gsend, grecv, qsend, qrecv) = (
        m[n] for n in ("lsem", "wsend", "wrecv", "xsend", "xrecv", "msend", "mrecv", "esend", "erecv", "ksend",
                       "krecv", "dsend", "drecv", "hsend", "hrecv", "gsend", "grecv", "qsend", "qrecv"))
    s1, q1, s2, q2, s4, q4, s5, q5, ns, nq = (
        m[n] for n in ("s1", "q1", "s2", "q2", "s4", "q4", "s5", "q5", "ns", "nq"))
    w2send, w2recv, sx, qx, sz, qz, sq, qq, s3, q3 = (
        m[n] for n in ("w2send", "w2recv", "sx", "qx", "sz", "qz", "sq", "qq", "s3", "q3"))

    def g_row(i):
        return gain[i]

    def b_row(i):
        return bias[i]

    sec = lax.axis_index("section")
    dp = lax.axis_index("dp")
    t = lax.axis_index("tensor")
    core = lax.rem(dp, 2)
    chip = lax.div(dp, 2)
    sib = dp + 1 - 2 * core
    is_enc = sec == 0
    is_dec = sec == 1
    left = lax.rem(t + 3, NT)
    right = lax.rem(t + 1, NT)
    opp = lax.rem(t + 2, NT)
    other = 1 - sec
    xi = lax.div(dp, 4)

    def x_dev(off):
        return lax.rem(xi + off, 4) * 4 + lax.rem(dp, 4)

    z_dev = xi * 4 + lax.rem(dp + 2, 4)

    def source(off):
        return lax.rem(t + NT - off, NT)

    def chip_at(off):
        return lax.rem(chip + off, chips)

    ins = (wqkv_in, wout_in, wcross_in, wup_in, wdown_in)
    ws = (wqkv, wout, wcross, wup, wdown)

    def part(i, ref, start, n):
        if i in (QKV, CROSS):
            return ref.at[:, pl.ds(start, n), :]
        return ref.at[pl.ds(start, n), :]

    def slot(i, a, start, n):
        if i in (QKV, CROSS):
            return ws[i].at[a, :, pl.ds(start, n), :]
        return ws[i].at[a, pl.ds(start, n), :]

    barrier = pltpu.get_barrier_semaphore()
    for off in (1, 2, 3):
        pl.semaphore_signal(barrier, inc=1, device_id={"tensor": lax.rem(t + off, NT)}, device_id_type=MESH)
    pl.semaphore_signal(barrier, inc=1, device_id={"dp": sib}, device_id_type=MESH)
    for b in range(NT):
        pl.semaphore_signal(barrier, inc=1, device_id={"section": other, "tensor": b}, device_id_type=MESH)
    for off in range(1, chips):
        pl.semaphore_signal(barrier, inc=1, device_id={"dp": chip_at(off) * 2 + core}, device_id_type=MESH)

    locals_ = [
        pltpu.make_async_copy(x_in, x_ext.at[:, pl.ds(OWN, T), :], lsem.at[0]),
        pltpu.make_async_copy(cot_in, d32, lsem.at[1]),
    ]
    for i in range(5):
        locals_.append(pltpu.make_async_copy(ins[i], ws[i].at[t], lsem.at[2 + i]))
    for c in locals_:
        c.start()

    pl.semaphore_wait(barrier, 8 + chips - 1)

    x_right = remote(x_in.at[:, pl.ds(T - HALO, HALO), :], x_ext.at[:, pl.ds(LEFT, HALO), :],
                     xsend.at[0], xrecv.at[0], tensor=right)
    x_left = remote(x_in.at[:, pl.ds(0, HALO), :], x_ext.at[:, pl.ds(RIGHT, HALO), :],
                    xsend.at[1], xrecv.at[1], tensor=left)
    mem_x, mem_c = [], []
    for off in (1, 2, 3):
        to = lax.rem(t + off, NT)
        mem_x.append(remote(x_in.at[:, pl.ds(0, MP), :], x_ext.at[:, pl.ds(0, MP), :],
                            msend.at[0, off - 1], mrecv.at[0], tensor=to))
        mem_c.append(remote(cot_in.at[:, pl.ds(0, MP), :], cotm, msend.at[1, off - 1], mrecv.at[1], tensor=to))
    mem_local = [
        pltpu.make_async_copy(x_in.at[:, pl.ds(0, MP), :], x_ext.at[:, pl.ds(0, MP), :], lsem.at[7]),
        pltpu.make_async_copy(cot_in.at[:, pl.ds(0, MP), :], cotm, lsem.at[8]),
    ]

    def w_direct(i):
        hf = W_ROWS[i] // 2
        mine = core * hf
        return [remote(part(i, ins[i], mine, hf), slot(i, t, mine, hf), wsend.at[i, off - 1], wrecv.at[i, off - 1],
                       tensor=lax.rem(t + off, NT)) for off in (1, 2, 3)]

    eighth = D // 8
    at_8 = core * (D // 2) + xi * eighth

    def w_eighth(i):
        return [remote(part(i, ins[i], at_8, eighth), slot(i, t, at_8, eighth),
                       wsend.at[i, off - 1], wrecv.at[i, off - 1], tensor=lax.rem(t + off, NT)) for off in (1, 2, 3)]

    def w_along(i):
        out = []
        for off in (1, 2, 3):
            rows = slot(i, source(off), at_8, eighth)
            for xo in (1, 2, 3):
                out.append(remote(rows, rows, w2send.at[ALONG[i], off - 1, xo - 1], w2recv.at[ALONG[i], off - 1, xo - 1],
                                  dp=x_dev(xo)))
        return out

    def w_pair(i):
        hf = W_ROWS[i] // 2
        out = []
        for off in (1, 2, 3):
            rows = slot(i, source(off), core * hf, hf)
            out.append(remote(rows, rows, wsend.at[i, 2 + off], wrecv.at[i, 2 + off], dp=sib))
        return out

    def go(cs):
        for c in cs:
            c.start()

    def come(cs):
        for c in cs:
            c.wait_recv()

    def gone(cs):
        for c in cs:
            c.wait_send()

    def arrive(i):
        for c, p in zip(w_direct(i), w_pair(i)):
            c.wait_recv()
            p.start()

    def go_along(i):
        along = w_along(i)
        for off, c in enumerate(w_eighth(i)):
            c.wait_recv()
            go(along[3 * off:3 * off + 3])

    def come_along(i):
        along = w_along(i)
        for off, p in enumerate(w_pair(i)):
            come(along[3 * off:3 * off + 3])
            p.start()

    def ready(i):
        come(w_pair(i))

    go(w_eighth(QKV))

    @pl.when(is_enc)
    def _():
        @pl.when(t == 0)
        def _():
            go(mem_x + mem_local)

        x_right.start()
        x_left.start()
        go(w_eighth(UP))
        go(w_direct(OUT))

    @pl.when(is_dec)
    def _():
        x_right.start()
        go(w_eighth(UP))
        go(w_direct(OUT))
        go(w_eighth(DOWN))
        go(w_direct(CROSS))

    lane = lax.broadcasted_iota(jnp.int32, (T, 128), 1)
    hmask[0] = jnp.where(lane < 64, 1.0, 0.0).astype(BF)
    hmask[1] = jnp.where(lane < 64, 0.0, 1.0).astype(BF)

    def bounds(pos, r):
        end = jnp.int32(MEM)
        first = jnp.where(pos >= MEM, MEM, 0)
        after = jnp.full(pos.shape, MEM, jnp.int32)
        for k in range(16):
            after = jnp.where(pos >= end, end + lens[r, k], after)
            first = jnp.where(pos >= end, end, first)
            end = end + lens[r, k]
        return first, after

    def make_masks(windows, encoder):
        for r in range(R):
            for b, (w0, wn) in enumerate(windows):
                e = lax.broadcasted_iota(jnp.int32, (wn, 128), 0) + w0
                pos = e - OWN + t * T
                qpos = lax.broadcasted_iota(jnp.int32, (8, 128), 1) + (t * T + b * 128)
                first, after = bounds(qpos, r)
                ok = jnp.logical_and(pos >= first[0:1], pos < after[0:1])
                if encoder:
                    mem_i = jnp.where(e < LEFT, e, jnp.where(e >= MEM_2, e - MEM_2, MEM))
                    ok = jnp.logical_or(mem_i < MEM, jnp.logical_and(
                        jnp.logical_and(e >= LEFT, e < MEM_2), jnp.logical_and(ok, pos >= MEM)))
                else:
                    ok = jnp.logical_and(jnp.logical_and(ok, e >= LEFT), pos <= qpos[0:1])
                mask[r, b, 0:wn] = jnp.where(ok, 0.0, FILL)

    @pl.when(is_enc)
    def _():
        make_masks(WIN_ENC, True)

    @pl.when(is_dec)
    def _():
        make_masks(WIN_DEC, False)
        x_ext[:, 0:MP] = jnp.zeros((R, MP, D), BF)

    ex_st[t] = jnp.zeros((R * MP, 128), F32)
    ng[...] = jnp.zeros(ng.shape, F32)

    go_along(QKV)
    for c in locals_:
        c.wait()

    def shard_at(step):
        return lax.rem(t + jnp.where(step == 0, 0, jnp.where(step == 1, 3, step - 1)), NT)

    lane_m = lax.broadcasted_iota(jnp.int32, (MP, 128), 1)
    low_m = lane_m < 64

    def keys(a, r, lo, hi, wkv):
        kv = dot(x_ext[r, lo:hi], wkv)
        k32, v32 = kv[:, 0:128], kv[:, 128:256]
        kk[a, r, lo:hi] = k32.astype(BF)
        vv[a, r, lo:hi] = v32.astype(BF)

    def keys_weight(a):
        return jnp.concatenate([wqkv[a, 1], wqkv[a, 2]], axis=1)

    def queries(a, r):
        q = dot(x_ext[r, OWN:OWN + T], wqkv[a, 0]).astype(BF)
        q = (q.astype(F32) * SCALE).astype(BF)
        for b in range(2):
            for h in range(2):
                qs[a, r, b, h * 128:h * 128 + 128] = q[b * 128:b * 128 + 128] * hmask[h, 0:128]

    def turned(ref, a, r, hi):
        return ref[a, r, 0:hi].astype(F32).T.astype(BF)

    def project_own(shards_):
        jobs = [(a, r) for a in shards_ for r in range(R)]
        for a in shards_:
            wkv = keys_weight(a)
            for r in range(R):
                keys(a, r, OWN, OWN + T, wkv)
                queries(a, r)
        lhs = []
        for a, r in jobs:
            m32 = dot(x_ext[r, 0:MP], wqkv[a, 0]).astype(BF).astype(F32) * SCALE
            lhs.append(jnp.concatenate([jnp.where(low_m, m32, 0.0), jnp.where(low_m, 0.0, m32)], axis=0).astype(BF))
        ss = [dot_nt(v, kk[a, r, OWN:OWN + T]) for v, (a, r) in zip(lhs, jobs)]
        tops = [jnp.max(s, axis=1, keepdims=True) for s in ss]
        ps = [jnp.exp(s - top) for s, top in zip(ss, tops)]
        totals = [jnp.sum(p, axis=1, keepdims=True) for p in ps]
        os_ = [dot(p.astype(BF), vv[a, r, OWN:OWN + T]) / total for p, total, (a, r) in zip(ps, totals, jobs)]
        for (a, r), v, o in zip(jobs, lhs, os_):
            qm[a, r] = v
            ex_o[t, a, r * MP:r * MP + MP] = jnp.where(low_m, o[0:MP], o[MP:2 * MP]).astype(BF)
        for r in range(R):
            st = ex_st[t, r * MP:r * MP + MP]
            for (a, r_), top, total in zip(jobs, tops, totals):
                if r_ == r:
                    st = jnp.where(lane_m == 2 * a, top[0:MP], st)
                    st = jnp.where(lane_m == 2 * a + 1, top[MP:2 * MP], st)
                    st = jnp.where(lane_m == 2 * a + 8, total[0:MP], st)
                    st = jnp.where(lane_m == 2 * a + 9, total[MP:2 * MP], st)
            ex_st[t, r * MP:r * MP + MP] = st

    def project_rest(a):
        wkv = keys_weight(a)
        for r in range(R):
            keys(a, r, 0, OWN, wkv)
            keys(a, r, RIGHT, W_ENC, wkv)

    def project_all(a):
        wkv = keys_weight(a)
        for r in range(R):
            keys(a, r, 0, W_DEC, wkv)
            queries(a, r)

    def ex_copies(e, buf):
        out = []
        for off in (1, 2, 3):
            out.append(remote(buf.at[t], buf.at[t], esend.at[e, off - 1], erecv.at[e, off - 1],
                              tensor=lax.rem(t + off, NT)))
        return out

    exchanges = [ex_copies(e, buf) for e, buf in enumerate((ex_o, ex_st, ex_f, ex_m))]

    def ex_start(e):
        for c in exchanges[e]:
            c.start()

    def ex_wait(e):
        for c in exchanges[e]:
            c.wait_recv()

    def wide(ref, r):
        return jnp.concatenate([ref[r, a] for a in range(NT)], axis=1)

    def w_out_full():
        return wout[...].reshape(D, D)

    def mem_combine():
        for r in range(R):
            rows = slice(r * MP, r * MP + MP)
            sts = [ex_st[s, rows] for s in range(NT)]
            top = jnp.maximum(jnp.maximum(sts[0], sts[1]), jnp.maximum(sts[2], sts[3]))
            wts = [pltpu.roll(sts[s], 120, 1) * jnp.exp(sts[s] - top) for s in range(NT)]
            total = wts[0] + wts[1] + wts[2] + wts[3]
            total = jnp.where(lane_m < 8, total, 1.0)
            inv = 1.0 / total
            mst[0, rows] = jnp.where(lane_m < 8, top + jnp.log(total), 0.0)
            for a in range(NT):
                acc = jnp.zeros((MP, 128), F32)
                for s in range(NT):
                    w = wts[s] * inv
                    wide_w = jnp.where(low_m, w[:, 2 * a:2 * a + 1], w[:, 2 * a + 1:2 * a + 2])
                    acc = acc + wide_w * ex_o[s, a, rows].astype(F32)
                mc[rows, a * 128:a * 128 + 128] = acc

    def x_mem():
        return jnp.concatenate([x_ext[r, 0:MP] for r in range(R)], axis=0)

    def mem_first():
        mem_combine()
        xm = x_mem().astype(F32)
        xh, rs = normed(xm + dot(mc[...].astype(BF), w_out_full()))
        mx1[...] = xh
        mr1[...] = rs
        h = xh * g_row(0) + b_row(0)
        mh[...] = h
        av, _ = gelu_both(dot(h.astype(BF), wup[t]))
        mact[...] = av.astype(BF)
        ex_f[t] = dot(av.astype(BF), wdown[t]).astype(BF)
        ex_start(2)

    kv_copies = [remote(kvm.at[t], kvm.at[t], ksend.at[b], krecv.at[t], section=other, tensor=b) for b in range(NT)]

    def mem_second():
        third = mh[...]
        for s in range(NT):
            third = third + ex_f[s].astype(F32)
        xh, rs = normed(third)
        mx2[...] = xh
        mr2[...] = rs
        y = xh * g_row(1) + b_row(1)
        md[...] = y
        xh, rs = normed(y)
        mx3[...] = xh
        mr3[...] = rs
        mv = (xh * g_row(2) + b_row(2)).astype(BF)
        mm[...] = mv
        kvm[t, 0] = dot(mv, wcross[t, 0]).astype(BF)
        kvm[t, 1] = dot(mv, wcross[t, 1]).astype(BF)
        for c in kv_copies:
            c.start()

    def attend(a, windows):
        jobs = [(r, b, w0, wn) for r in range(R) for b, (w0, wn) in enumerate(windows)]
        v_t = [turned(vv, a, r, windows[1][0] + windows[1][1]) for r in range(R)]
        scores = []
        for r, b, w0, wn in jobs:
            mk = mask[r, b, 0:wn]
            scores.append(dot_nt(kk[a, r, w0:w0 + wn], qs[a, r, b]) + jnp.concatenate([mk, mk], axis=1))
        ps = []
        for s in scores:
            p = jnp.exp(s - jnp.max(s, axis=0, keepdims=True))
            ps.append((p * (1.0 / jnp.sum(p, axis=0, keepdims=True))).astype(BF))
        for (r, b, w0, wn), p in zip(jobs, ps):
            pt[a, r, b, 0:wn] = p
            o = dot(v_t[r][:, w0:w0 + wn], p)
            o = jnp.concatenate([o[0:64, 0:128], o[64:128, 128:256]], axis=0)
            ctx[r, a, b * 128:b * 128 + 128] = o.T.astype(BF)

    def encoder_attention():
        @pl.when(t == 0)
        def _():
            mem_local[0].wait()

        @pl.when(t > 0)
        def _():
            mem_x[0].wait_recv()

        x_ext[:, MEM_2:MEM_2 + MP] = x_ext[:, 0:MP]

        project_own([t])
        come_along(QKV)
        ready(QKV)
        project_own([left, right, opp])
        ex_start(0)
        ex_start(1)
        go(w_eighth(DOWN))
        x_right.wait_recv()
        x_left.wait_recv()
        go_along(UP)
        arrive(OUT)

        @pl.loop(0, NT)
        def _(step):
            project_rest(shard_at(step))

        @pl.loop(0, NT)
        def _(i):
            @pl.when(i == 2)
            def _():
                ex_wait(0)
                ex_wait(1)
                ready(OUT)
                mem_first()
                go_along(DOWN)

            @pl.when(i == 3)
            def _():
                ex_wait(2)
                mem_second()

                @pl.when(t == 0)
                def _():
                    go(mem_c)

            attend(shard_at(i), WIN_ENC)

    def decoder_attention():
        x_right.wait_recv()

        project_all(t)

        @pl.loop(0, NT)
        def _(i):
            @pl.when(i == 1)
            def _():
                come_along(QKV)
                go_along(UP)
                ready(QKV)

                @pl.loop(1, NT)
                def _(step):
                    project_all(shard_at(step))

            @pl.when(i == 2)
            def _():
                arrive(OUT)

            @pl.when(i == 3)
            def _():
                go_along(DOWN)
                ready(OUT)

            attend(shard_at(i), WIN_DEC)

    @pl.when(is_enc)
    def _():
        encoder_attention()

    @pl.when(is_dec)
    def _():
        decoder_attention()

    both = range(R)
    a0s = [x_ext[r, OWN:OWN + T].astype(F32) + dot(wide(ctx, r), w_out_full()) for r in both]
    for r, (xh, rs) in enumerate([normed(v) for v in a0s]):
        xh1[r] = xh
        rs1[r] = rs
        h = xh * g_row(0) + b_row(0)
        h32[r] = h
        hb[r] = h.astype(BF)

    pad_mask = jnp.where(
        lax.rem(lax.broadcasted_iota(jnp.int32, (256, T), 0), MP) < MEM, 0.0, FILL)

    def full_cross(j):
        return jnp.concatenate([wcross[a, j] for a in range(NT)], axis=1)

    def cross_forward():
        arrive(CROSS)
        come_along(UP)
        ready(CROSS)
        wc0 = full_cross(0)
        wc1 = full_cross(1)
        kblk[...] = jnp.zeros(kblk.shape, BF)
        vblk[...] = jnp.zeros(vblk.shape, BF)

        @pl.loop(0, R)
        def _(r):
            h1b[r] = hb[r]
            q = dot(hb[r], wc0).astype(BF)
            cq[r] = (q.astype(F32) * SCALE).astype(BF)

        for b in range(NT):
            remote(kvm.at[b], kvm.at[b], ksend.at[b], krecv.at[b], section=other, tensor=b).wait_recv()
        for r in range(R):
            for a in range(NT):
                for h in range(2):
                    at = slice(a * 64 + h * MP, a * 64 + h * MP + MP)
                    kblk[r, at, a * 128:a * 128 + 128] = kvm[a, 0, r * MP:r * MP + MP] * hmask[h, 0:MP]
                    vblk[r, at, a * 128:a * 128 + 128] = kvm[a, 1, r * MP:r * MP + MP] * hmask[h, 0:MP]

        ss = [(dot_nt(kblk[r], cq[r]) + pad_mask).reshape(8, MP, T) for r in both]
        ps = []
        for s in ss:
            p = jnp.exp(s - jnp.max(s, axis=1, keepdims=True))
            ps.append((p * (1.0 / jnp.sum(p, axis=1, keepdims=True))).reshape(256, T).astype(BF))
        cs = [dot_tn(p, vblk[r]).astype(BF) for r, p in enumerate(ps)]
        sums = [h32[r] + dot_nt(c, wc1) for r, c in enumerate(cs)]
        for r, (xh, rs) in enumerate([normed(v) for v in sums]):
            cpt[r] = ps[r]
            cctx[r] = cs[r]
            xh2[r] = xh
            rs2[r] = rs
            h = xh * g_row(1) + b_row(1)
            h32[r] = h
            hb[r] = h.astype(BF)

    @pl.when(is_dec)
    def _():
        cross_forward()

    @pl.when(is_enc)
    def _():
        come_along(UP)

    @pl.loop(0, NT)
    def _(i):
        @pl.when(i == 1)
        def _():
            ready(UP)

        a = shard_at(i)
        us = [dot(hb[r], wup[a]) for r in both]
        for r, (av, gv) in enumerate([gelu_both(u) for u in us]):
            act[r, a] = av.astype(BF)
            gp[r, a] = gv.astype(BF)

    @pl.when(is_enc)
    def _():
        for a in range(NT):
            _, gv = gelu_both(dot(mh[...].astype(BF), wup[a]))
            xh2[a // 2, (a % 2) * M:(a % 2) * M + M] = gv

    come_along(DOWN)
    ready(DOWN)

    last = jnp.where(is_enc, 1, 2)
    g_last = jnp.where(is_enc, g_row(1), g_row(2))
    b_last = jnp.where(is_enc, b_row(1), b_row(2))

    def add_norm(at, xh, dy):
        ng[pl.ds(at, 1)] += jnp.sum(dy * xh, axis=0, keepdims=True)
        ng[pl.ds(at + 3, 1)] += jnp.sum(dy, axis=0, keepdims=True)

    row_i = lax.broadcasted_iota(jnp.int32, (T, D), 0)
    is_mem_row = jnp.logical_and(row_i < MEM, jnp.logical_and(is_enc, t == 0))

    thirds = [h32[r] + dot(wide(act, r), wdown[...].reshape(NT * D, D)) for r in both]
    nrms = [normed(v) for v in thirds]
    dys = [jnp.where(is_mem_row, 0.0, d32[r]) for r in both]
    d3s = [norm_back(xh, rs, g_last, dy) for (xh, rs), dy in zip(nrms, dys)]
    for r in both:
        xh, dy = nrms[r][0], dys[r]
        h32[r] = xh * g_last + b_last
        ng[pl.ds(last, 1)] += jnp.sum(dy * xh, axis=0, keepdims=True)
        ng[pl.ds(last + 3, 1)] += jnp.sum(dy, axis=0, keepdims=True)
        d32[r] = d3s[r]
        dab[r] = d3s[r].astype(BF)

    @pl.when(jnp.logical_and(is_enc, t == 0))
    def _():
        for r in range(R):
            h32[r, 0:24] = jnp.where(
                lax.broadcasted_iota(jnp.int32, (24, D), 0) < MEM, md[r * MP:r * MP + 24], h32[r, 0:24])

    y_copy = pltpu.make_async_copy(h32, y_out, lsem.at[9])
    y_copy.start()

    def at(k):
        return CHUNKS[k][0], CHUNKS[k][0] // 2, CHUNKS[k][1] // 2

    def own_half(k):
        start, lo, hf = at(k)
        return start + core * hf

    def shard_of(q):
        return lax.rem(t + 1 + q, NT)

    def rel_of(a):
        return lax.rem(a - t + 3, NT)

    def pair(k, q):
        start, lo, hf = at(k)
        return remote(g.at[q, pl.ds(start + (1 - core) * hf, hf), :], r1.at[q, pl.ds(lo, hf), :],
                      s1.at[k, q], q1.at[k, q], dp=sib)

    def pair_sum(k, q):
        start, lo, hf = at(k)
        rows = pl.ds(own_half(k), hf)
        g[q, rows] = (g[q, rows].astype(F32) + r1[q, lo:lo + hf].astype(F32)).astype(BF)

    def x_row(k):
        return 0 if k == C_CROSS else 512 // chips

    def chips_first(k, q, some=1):
        start, lo, hf = at(k)
        n = hf // chips
        out = []
        for off in range(1, chips):
            to = chip_at(off)
            out.append(remote(g.at[pl.ds(q, some), pl.ds(own_half(k) + to * n, n), :],
                              rq.at[off - 1, pl.ds(q, some), pl.ds(x_row(k), n), :],
                              sq.at[k, q, off - 1], qq.at[k, q, off - 1], dp=to * 2 + core))
        return out

    def chips_on(k, q, some):
        all_pairs_sum(k, range(q, q + some))
        go(chips_first(k, q, some))

    def chips_done(k, groups):
        start, lo, hf = at(k)
        n = hf // chips
        base = x_row(k)
        for first_q, some in groups:
            come(chips_first(k, first_q, some))
            for q in range(first_q, first_q + some):
                tot = g[q, pl.ds(own_half(k) + chip * n, n)].astype(F32)
                for o in range(chips - 1):
                    tot = tot + rq[o, q, base:base + n].astype(F32)
                rqs[q, base:base + n] = tot.astype(BF)

    def tensor_third(k):
        start, lo, hf = at(k)
        rows = pl.ds(x_row(k), hf // chips)
        return [remote(rqs.at[q, rows, :], rqr.at[q, rows, :], s2.at[k, q], q2.at[k, q], tensor=shard_of(q))
                for q in range(3)]

    def tensor_third_sum(k, only_own=False):
        start, lo, hf = at(k)
        n = hf // chips
        base = x_row(k)
        tot = rqs[3, base:base + n].astype(F32)
        if not only_own:
            for q in range(3):
                tot = tot + rqr[q, base:base + n].astype(F32)
        full[pl.ds(own_half(k) + chip * n, n)] = tot.astype(BF)

    def over_tensor(k, q):
        start, lo, hf = at(k)
        return remote(g.at[q, pl.ds(own_half(k), hf), :], r2.at[q, pl.ds(lo - LAST, hf), :],
                      s2.at[k, q], q2.at[k, q], tensor=shard_of(q))

    def tensor_on(k, some):
        all_pairs_sum(k, some)
        go([over_tensor(k, q) for q in some if q < 3])

    def tensor_sum(k, only_own=False):
        start, lo, hf = at(k)
        tot = g[3, pl.ds(own_half(k), hf)].astype(F32)
        if not only_own:
            come([over_tensor(k, q) for q in range(3)])
            for q in range(3):
                tot = tot + r2[q, lo - LAST:lo - LAST + hf].astype(F32)
        ysum[lo - LAST:lo - LAST + hf] = tot.astype(BF)
        go(over_chips(k))

    def over_chips(k):
        start, lo, hf = at(k)
        n = hf // chips
        out = []
        for off in range(1, chips):
            to = chip_at(off)
            out.append(remote(ysum.at[pl.ds(lo - LAST + to * n, n), :],
                              r3.at[off - 1, pl.ds((lo - LAST) // chips, n), :],
                              s3.at[k, off - 1], q3.at[k, off - 1], dp=to * 2 + core))
        return out

    def chips_sum(k):
        start, lo, hf = at(k)
        n = hf // chips
        come(over_chips(k))
        tot = ysum[pl.ds(lo - LAST + chip * n, n)].astype(F32)
        for o in range(chips - 1):
            tot = tot + r3[o, (lo - LAST) // chips:(lo - LAST) // chips + n].astype(F32)
        full[pl.ds(own_half(k) + chip * n, n)] = tot.astype(BF)
        go(spread(k))

    quarter = LATE // 8

    def along_x(k, own):
        some = pl.ds(3, 1) if own else pl.ds(0, 3)
        out = []
        for off in (1, 2, 3):
            to = lax.rem(xi + off, 4)
            out.append(remote(g.at[some, pl.ds(own_half(k) + to * quarter, quarter), :],
                              rx.at[off - 1, some, pl.ds(k * quarter, quarter), :],
                              sx.at[k, int(own), off - 1], qx.at[k, int(own), off - 1], dp=x_dev(off)))
        return out

    def along_x_sum(k, q):
        rows = slice(k * quarter, (k + 1) * quarter)
        tot = g[q, pl.ds(own_half(k) + xi * quarter, quarter)].astype(F32)
        for o in range(3):
            tot = tot + rx[o, q, rows].astype(F32)
        ry_s[q, rows] = tot.astype(BF)

    def tensor_second(k):
        rows = pl.ds(k * quarter, quarter)
        return [remote(ry_s.at[q, rows, :], ry_r.at[q, rows, :], s2.at[k, q], q2.at[k, q], tensor=shard_of(q))
                for q in range(3)]

    def tensor_second_sum(k):
        rows = slice(k * quarter, (k + 1) * quarter)
        tot = ry_s[3, rows].astype(F32)
        for q in range(3):
            tot = tot + ry_r[q, rows].astype(F32)
        zz[0, rows] = tot.astype(BF)

    def over_z(k):
        rows = pl.ds(k * quarter, quarter)
        return [remote(zz.at[0, rows, :], zz.at[1, rows, :], sz.at[k], qz.at[k], dp=z_dev)]

    def over_z_sum(k):
        rows = slice(k * quarter, (k + 1) * quarter)
        full[pl.ds(own_half(k) + xi * quarter, quarter)] = (zz[0, rows].astype(F32) + zz[1, rows].astype(F32)).astype(BF)

    def spread_x(k):
        mine = full.at[pl.ds(own_half(k) + xi * quarter, quarter), :]
        return [remote(mine, mine, s4.at[k, off - 1], q4.at[k, off - 1], dp=x_dev(off)) for off in (1, 2, 3)]

    def spread(k):
        start, lo, hf = at(k)
        n = hf // chips
        mine = full.at[pl.ds(own_half(k) + chip * n, n), :]
        return [remote(mine, mine, s4.at[k, off - 1], q4.at[k, off - 1], dp=chip_at(off) * 2 + core)
                for off in range(1, chips)]

    def hand(k):
        start, lo, hf = at(k)
        mine = full.at[pl.ds(own_half(k), hf), :]
        return [remote(mine, mine, s5.at[k], q5.at[k], dp=sib)]

    def all_pairs(k):
        for q in range(NT):
            pair(k, q).start()

    def all_pairs_sum(k, some=range(NT)):
        for q in some:
            pair(k, q).wait_recv()
            pair_sum(k, q)

    def put_feed(k, q, w):
        for j in range(4):
            g[q, CHUNKS[k][0] + D * j:CHUNKS[k][0] + D * (j + 1)] = w[:, 128 * j:128 * j + 128].astype(BF)

        @pl.when(jnp.logical_or(is_dec, q < 3))
        def _():
            pair(k, q).start()

    @pl.loop(0, NT)
    def _(q):
        a = shard_of(q)
        put_feed(C_DOWN, q, dot_tn(act[0, a], dab[0]) + dot_tn(act[1, a], dab[1]))

    @pl.loop(0, NT)
    def _(a):
        dacts = [dot_nt(dab[r], wdown[a]) for r in both]
        for r in both:
            gp[r, a] = (dacts[r] * gp[r, a].astype(F32)).astype(BF)

    w_up_all = jnp.concatenate([wup[a] for a in range(NT)], axis=1)
    for r in both:
        d32[r] += dot_nt(wide(gp, r), w_up_all)

    def feed_on(k):
        all_pairs_sum(k, range(3))
        go(along_x(k, False))

        @pl.when(is_dec)
        def _():
            all_pairs_sum(k, (3,))
            go(along_x(k, True))

    feed_on(C_DOWN)

    dkv_copies = [
        remote(dkvm_s.at[b], dkvm_r.at[t], dsend.at[b], drecv.at[t], section=other, tensor=b) for b in range(NT)
    ]

    def cross_backward():
        wc0 = full_cross(0)
        wc1 = full_cross(1)

        dys = [d32[r] for r in both]
        d2s = [norm_back(xh2[r], rs2[r], g_row(1), dys[r]) for r in both]
        dcs = []
        for r in both:
            d32[r] = d2s[r]
            cdb[r] = d2s[r].astype(BF)
        for r in both:
            dcs.append(dot(cdb[r], wc1).astype(BF))
        dps = [dot_nt(vblk[r], dcs[r]).reshape(8, MP, T) for r in both]
        dss = []
        for r in both:
            p = cpt[r].astype(F32).reshape(8, MP, T)
            ds = p * (dps[r] - jnp.sum(p * dps[r], axis=1, keepdims=True))
            dss.append(ds.reshape(256, T).astype(BF))
        dks = [dot(dss[r], cq[r]) for r in both]
        dvs = [dot(cpt[r], dcs[r]) for r in both]
        for r in both:
            rows = slice(r * MP, r * MP + MP)
            for a in range(NT):
                for j, val in ((0, dks[r]), (1, dvs[r])):
                    dkvm_s[a, j, rows] = jnp.where(
                        low_m, val[64 * a:64 * a + MP, 128 * a:128 * a + 128],
                        val[64 * a + MP:64 * a + 2 * MP, 128 * a:128 * a + 128])
        go(dkv_copies)
        dqs = [(dot_tn(dss[r], kblk[r]) * SCALE).astype(BF) for r in both]
        for r in both:
            add_norm(1, xh2[r], dys[r])
            cq[r] = dqs[r]
        for r in both:
            d32[r] += dot_nt(dqs[r], wc0)

    def cross_grads():
        gq = dot_tn(h1b[0], cq[0]) + dot_tn(h1b[1], cq[1])
        go_ = dot_tn(cdb[0], cctx[0]) + dot_tn(cdb[1], cctx[1])
        for a in range(NT):
            q = rel_of(a)
            g[q, G_CROSS:G_CROSS + D] = gq[:, 128 * a:128 * a + 128].astype(BF)
            g[q, G_CROSS + D:G_CROSS + 2 * D] = go_[:, 128 * a:128 * a + 128].astype(BF)
        all_pairs(C_CROSS)

    @pl.when(is_dec)
    def _():
        cross_backward()

    @pl.loop(0, NT)
    def _(q):
        a = shard_of(q)
        put_feed(C_UP, q, dot_tn(hb[0], gp[0, a]) + dot_tn(hb[1], gp[1, a]))

    dys1 = [d32[r] for r in both]
    d1s = [norm_back(xh1[r], rs1[r], g_row(0), dys1[r]) for r in both]
    for r in both:
        d32[r] = d1s[r]
        dab[r] = d1s[r].astype(BF)
    for r in both:
        drr = dot_nt(dab[r], w_out_full()).astype(BF)
        for a in range(NT):
            dr[r, a] = drr[:, 128 * a:128 * a + 128]
    for r in both:
        add_norm(0, xh1[r], dys1[r])

    def out_grads():
        wo_all = dot_tn(wide(ctx, 0), dab[0]) + dot_tn(wide(ctx, 1), dab[1])
        for a in range(NT):
            for j in range(4):
                g[rel_of(a), G_OUT + 128 * j:G_OUT + 128 * j + 128] = (
                    wo_all[128 * a:128 * a + 128, 128 * j:128 * j + 128].astype(BF))
        for q in range(3):
            pair(C_OUT, q).start()

        @pl.when(is_dec)
        def _():
            pair(C_OUT, 3).start()

    feed_on(C_UP)

    def attend_back(a, windows, encoder):
        jobs = [(r, b, w0, wn) for r in range(R) for b, (w0, wn) in enumerate(windows)]
        k_t = [turned(kk, a, r, windows[1][0] + windows[1][1]) for r in range(R)]
        drs, dps, dss = [], [], []
        for r, b, w0, wn in jobs:
            d_r = dr[r, a, b * 128:b * 128 + 128]
            d_r = jnp.concatenate([d_r * hmask[0, 0:128], d_r * hmask[1, 0:128]], axis=0)
            drs.append(d_r)
            dps.append(dot_nt(vv[a, r, w0:w0 + wn], d_r))
        for (r, b, w0, wn), dp_ in zip(jobs, dps):
            p = pt[a, r, b, 0:wn].astype(F32)
            dss.append((p * (dp_ - jnp.sum(p * dp_, axis=0, keepdims=True))).astype(BF))
        dks, dvs = [], []
        for (r, b, w0, wn), ds, d_r in zip(jobs, dss, drs):
            dq = dot(k_t[r][:, w0:w0 + wn], ds)
            dq = jnp.concatenate([dq[0:64, 0:128], dq[64:128, 128:256]], axis=0)
            act[r, a, b * 128:b * 128 + 128, 0:128] = (dq.T * SCALE).astype(BF)
            dks.append(dot(ds, qs[a, r, b]))
            dvs.append(dot(pt[a, r, b, 0:wn], d_r))
        (_, n0), (w1, n1_) = windows
        for r in range(R):
            for j, parts in enumerate((dks, dvs)):
                lo, hi = parts[2 * r], parts[2 * r + 1]
                both = lo[w1:n0] + hi[0:n0 - w1]
                val = jnp.concatenate([lo[0:w1], both, hi[n0 - w1:n1_]], axis=0)
                dkv[a, r, j] = val[OWN:OWN + T]
                halo_s[0, a, r, j] = val[LEFT:LEFT + HALO].astype(BF)
                if encoder:
                    halo_s[1, a, r, j] = val[RIGHT:RIGHT + HALO].astype(BF)
                    mg_s[a, r, j + 1] = (val[0:MP] + val[MEM_2:MEM_2 + MP]).astype(BF)

    def halo_copies(a):
        return (remote(halo_s.at[0, a], halo_r.at[0, a], hsend.at[0, a], hrecv.at[0, a], tensor=left),
                remote(halo_s.at[1, a], halo_r.at[1, a], hsend.at[1, a], hrecv.at[1, a], tensor=right))

    first = jnp.where(t == 0, 1.0, 0.0)
    mg_copies = [remote(mg_s.at[lax.rem(t + off, NT)], mg_r.at[off - 1], qsend.at[off - 1], qrecv.at[off - 1],
                        tensor=lax.rem(t + off, NT)) for off in (1, 2, 3)]

    def add_g(start, val):
        n = val.shape[0]
        g[3, start:start + n] = (g[3, start:start + n].astype(F32) + val).astype(BF)

    def add_norm_m(at_, xh, dy):
        ng[at_:at_ + 1] += first * jnp.sum(dy * xh, axis=0, keepdims=True)
        ng[at_ + 3:at_ + 4] += first * jnp.sum(dy, axis=0, keepdims=True)

    def mem_back_first():
        for b in range(NT):
            remote(dkvm_s.at[b], dkvm_r.at[b], dsend.at[b], drecv.at[b], section=other, tensor=b).wait_recv()
        grads = []
        for j in range(2):
            tot = dkvm_r[0, j] + dkvm_r[1, j] + dkvm_r[2, j] + dkvm_r[3, j]
            grads.append(tot.astype(BF))
        ex_m[t] = (dot_nt(grads[0], wcross[t, 0]) + dot_nt(grads[1], wcross[t, 1])).astype(BF)
        ex_start(3)
        for j in range(2):
            g[3, G_CROSS + D * j:G_CROSS + D * j + D] = dot_tn(mm[...], grads[j]).astype(BF)
        pair(C_CROSS, 3).start()

    def mem_back_second():
        ex_wait(3)
        dm = ex_m[0].astype(F32)
        for s in range(1, NT):
            dm = dm + ex_m[s].astype(F32)
        add_norm_m(2, mx3[...], dm)
        rows_m = lax.broadcasted_iota(jnp.int32, (R * MP, D), 0)

        @pl.when(t == 0)
        def _():
            mem_local[1].wait()

        @pl.when(t > 0)
        def _():
            mem_c[0].wait_recv()

        cm = jnp.concatenate([cotm[0], cotm[1]], axis=0)
        cm = jnp.where(lax.rem(rows_m, MP) < MEM, cm, 0.0)
        dy = cm + norm_back(mx3[...], mr3[...], g_row(2), dm)
        add_norm_m(1, mx2[...], dy)
        d3 = norm_back(mx2[...], mr2[...], g_row(1), dy)
        d3b = d3.astype(BF)
        d2 = d3
        for a in range(NT):
            dum = (dot_nt(d3b, wdown[a]) * xh2[a // 2, (a % 2) * M:(a % 2) * M + M]).astype(BF)
            d2 = d2 + dot_nt(dum, wup[a])
            mdu[a] = dum
        wd = dot_tn(mact[...], d3b)
        wu = dot_tn(mh[...].astype(BF), mdu[t])
        md[...] = d2
        for j in range(4):
            add_g(G_DOWN + D * j, wd[:, 128 * j:128 * j + 128])
            add_g(G_UP + D * j, wu[:, 128 * j:128 * j + 128])
        pair(C_DOWN, 3).start()
        pair(C_UP, 3).start()

    def mem_back_third():
        d2 = md[...]
        add_norm_m(0, mx1[...], d2)
        d1 = norm_back(mx1[...], mr1[...], g_row(0), d2)
        md[...] = d1
        d1b = d1.astype(BF)
        dmb[...] = d1b
        drm = dot_nt(d1b, w_out_full()).astype(BF).astype(F32)
        mh[...] = drm
        prod = drm * mc[...]
        for r in range(R):
            acc = jnp.zeros((MP, 128), F32)
            for hh in range(8):
                cols = prod[r * MP:r * MP + MP, (hh // 2) * 128:(hh // 2) * 128 + 128]
                cols = jnp.where(low_m if hh % 2 == 0 else jnp.logical_not(low_m), cols, 0.0)
                acc = jnp.where(lane_m == hh, jnp.sum(cols, axis=1, keepdims=True), acc)
            mst[1, r * MP:r * MP + MP] = acc
    def mem_out():
        for a in range(NT):
            @pl.when(t == a)
            def _():
                wo = dot_tn(mc[:, 128 * a:128 * a + 128].astype(BF), dmb[...])
                for j in range(4):
                    add_g(G_OUT + 128 * j, wo[:, 128 * j:128 * j + 128])
        pair(C_OUT, 3).start()

    def mem_attend_back():
        jobs = [(a, r) for a in range(NT) for r in range(R)]
        ss = [dot_nt(qm[a, r], kk[a, r, OWN:OWN + T]) for a, r in jobs]
        dras, dlts, ps = [], [], []
        for (a, r), s in zip(jobs, ss):
            rows = slice(r * MP, r * MP + MP)
            lse = mst[0, rows]
            dlt = mst[1, rows]
            lse = jnp.concatenate([lse[:, 2 * a:2 * a + 1], lse[:, 2 * a + 1:2 * a + 2]], axis=0)
            dlts.append(jnp.concatenate([dlt[:, 2 * a:2 * a + 1], dlt[:, 2 * a + 1:2 * a + 2]], axis=0))
            ps.append(jnp.exp(s - lse))
            dra = mh[rows, 128 * a:128 * a + 128]
            dras.append(
                jnp.concatenate([jnp.where(low_m, dra, 0.0), jnp.where(low_m, 0.0, dra)], axis=0).astype(BF))
        dps = [dot_nt(d, vv[a, r, OWN:OWN + T]) for d, (a, r) in zip(dras, jobs)]
        dss = [(p * (dp_ - dlt)).astype(BF) for p, dp_, dlt in zip(ps, dps, dlts)]
        dqs = [dot(ds, kk[a, r, OWN:OWN + T]) for ds, (a, r) in zip(dss, jobs)]
        for (a, r), dq in zip(jobs, dqs):
            mg_s[a, r, 0] = (jnp.where(low_m, dq[0:MP], dq[MP:2 * MP]) * SCALE).astype(BF)
        go(mg_copies)
        for (a, r), ds, p, dra in zip(jobs, dss, ps, dras):
            dkv[a, r, 0] += dot_tn(ds, qm[a, r])
            dkv[a, r, 1] += dot_tn(p.astype(BF), dra)

    def x_done(k, own):
        come(along_x(k, own))
        if own:
            along_x_sum(k, 3)
            return
        for q in range(3):
            along_x_sum(k, q)
        go(tensor_second(k))

    def order(i):
        return jnp.where(i == 0, 1, jnp.where(i == 1, 0, i))

    @pl.loop(0, NT)
    def _(i):
        a = shard_of(order(i))

        @pl.when(is_enc)
        def _():
            attend_back(a, WIN_ENC, True)

        @pl.when(is_dec)
        def _():
            attend_back(a, WIN_DEC, False)

        to_left, to_right = halo_copies(a)
        to_left.start()

        @pl.when(is_enc)
        def _():
            to_right.start()

        @pl.when(is_dec)
        def _():
            @pl.when(i == 3)
            def _():
                cross_grads()

        @pl.when(is_enc)
        def _():
            @pl.when(i == 0)
            def _():
                mem_back_first()

            @pl.when(i == 2)
            def _():
                mem_back_second()

            @pl.when(i == 3)
            def _():
                mem_back_third()

    n1 = [remote(ny.at[t], ny.at[t], ns.at[o - 1], nq.at[o - 1], tensor=lax.rem(t + o, NT)) for o in (1, 2, 3)]
    n2 = [remote(nc.at[0], nc.at[1], ns.at[3], nq.at[3], dp=sib)]
    n3 = [remote(nx.at[chip], nx.at[chip], ns.at[3 + o], nq.at[3 + o], dp=chip_at(o) * 2 + core)
          for o in range(1, chips)]

    def query_grads(q):
        a = shard_of(q)
        gw = dot_tn(x_ext[0, OWN:OWN + T], act[0, a, :, 0:128]) + dot_tn(x_ext[1, OWN:OWN + T], act[1, a, :, 0:128])
        g[q, G_QKV:G_QKV + D] = gw.astype(BF)

    def mem_last():
        mem_attend_back()
        for k in (C_DOWN, C_UP):
            all_pairs_sum(k, (3,))
            go(along_x(k, True))
        out_grads()
        mem_out()
        chips_on(C_CROSS, 3, 1)
        for q in range(NT):
            query_grads(q)
        for q in range(3):
            pair(C_Q, q).start()
        tensor_on(C_Q, range(3))
        tensor_on(C_OUT, range(NT))
        x_done(C_DOWN, False)

    def decoder_last():
        out_grads()
        for q in range(NT):
            query_grads(q)
            pair(C_Q, q).start()
        tensor_on(C_Q, range(NT))
        chips_on(C_CROSS, 0, NT)
        tensor_on(C_OUT, range(NT))
        x_done(C_DOWN, False)
        x_done(C_DOWN, True)

    ny[t] = ng[...]
    go(n1)

    @pl.when(is_dec)
    def _():
        decoder_last()

    @pl.when(is_enc)
    def _():
        mem_last()

    dxm_copy = remote(dxm_s, dxm_r.at[t], gsend.at[0], grecv.at[t], tensor=0)

    def mem_own():
        come(mg_copies)
        cols = []
        for j in range(3):
            both = []
            for r in range(R):
                tot = mg_s[t, r, j].astype(F32)
                for o in range(3):
                    tot = tot + mg_r[o, r, j].astype(F32)
                both.append(tot)
            cols.append(jnp.concatenate(both, axis=0))
        dm = jnp.concatenate(cols, axis=1).astype(BF)
        gw = dot_tn(x_mem(), dm)
        for j in range(3):
            add_g(G_QKV + D * j, gw[:, 128 * j:128 * j + 128])
        pair(C_Q, 3).start()
        pair(C_KV, 3).start()
        return dm

    def qkv_full(a):
        return jnp.concatenate([wqkv[a, j] for j in range(3)], axis=1)

    @pl.loop(0, NT)
    def _(i):
        q = order(i)
        a = shard_of(q)
        to_left, to_right = halo_copies(a)
        to_left.wait_recv()

        @pl.when(is_enc)
        def _():
            to_right.wait_recv()

        for r in range(R):
            for j in range(2):
                dkv[a, r, j, T - HALO:T] += halo_r[0, a, r, j].astype(F32)

                @pl.when(is_enc)
                def _():
                    dkv[a, r, j, 0:HALO] += halo_r[1, a, r, j].astype(F32)

                act[r, a, :, 128 * (j + 1):128 * (j + 2)] = dkv[a, r, j].astype(BF)
        gw = (dot_tn(x_ext[0, OWN:OWN + T], act[0, a, :, 128:384])
              + dot_tn(x_ext[1, OWN:OWN + T], act[1, a, :, 128:384]))
        for j in range(2):
            g[q, G_KV + D * j:G_KV + D * j + D] = gw[:, 128 * j:128 * j + 128].astype(BF)

        @pl.when(jnp.logical_or(is_dec, q < 3))
        def _():
            pair(C_KV, q).start()

        @pl.when(jnp.logical_and(is_enc, q == 3))
        def _():
            dm = mem_own()
            dxm_s[...] = dot_nt(dm, qkv_full(t)).astype(BF)

        @pl.when(i > 0)
        def _():
            q_before = order(i - 1)
            pair(C_KV, q_before).wait_recv()
            pair_sum(C_KV, q_before)

            @pl.when(i == 2)
            def _():
                go(chips_first(C_KV, 0, 2))

    all_pairs_sum(C_KV, (3,))
    go(chips_first(C_KV, 2, 2))

    @pl.when(is_enc)
    def _():
        all_pairs_sum(C_Q, (3,))

    for i in (QKV, UP, DOWN):
        gone(w_eighth(i))
        gone(w_along(i))
        gone(w_pair(i))
    gone(w_direct(OUT))
    gone(w_pair(OUT))
    x_right.wait_send()
    y_copy.wait()

    @pl.when(is_dec)
    def _():
        gone(w_direct(CROSS))
        gone(w_pair(CROSS))
        gone(dkv_copies)

    @pl.when(is_enc)
    def _():
        x_left.wait_send()
        for e in range(4):
            gone(exchanges[e])
        gone(kv_copies)
        gone(mg_copies)

        @pl.when(t == 0)
        def _():
            gone(mem_x)
            gone(mem_c)

    @pl.when(is_dec)
    def _():
        x_done(C_UP, False)
        x_done(C_UP, True)

    @pl.when(is_enc)
    def _():
        x_done(C_UP, False)
        for k in (C_DOWN, C_UP):
            x_done(k, True)

    come(n1)
    nc[0] = ny[0] + ny[1] + ny[2] + ny[3]
    go(n2)

    @pl.when(is_dec)
    def _():
        chips_done(C_CROSS, ((0, NT),))
        go(tensor_third(C_CROSS))

    @pl.when(is_enc)
    def _():
        chips_done(C_CROSS, ((3, 1),))
        tensor_third_sum(C_CROSS, True)
        go(spread(C_CROSS))

    tensor_sum(C_OUT)
    tensor_sum(C_Q)
    come(tensor_second(C_DOWN))
    tensor_second_sum(C_DOWN)
    go(over_z(C_DOWN))
    chips_done(C_KV, ((0, 2), (2, 2)))
    go(tensor_third(C_KV))

    @pl.when(jnp.logical_and(is_enc, t > 0))
    def _():
        dxm_copy.start()

    come(tensor_second(C_UP))
    tensor_second_sum(C_UP)
    go(over_z(C_UP))

    w_qkv_all = jnp.concatenate([qkv_full(a) for a in range(NT)], axis=1)
    for r in both:
        d_all = jnp.concatenate([act[r, a, :, 0:384] for a in range(NT)], axis=1)
        d32[r] += dot_nt(d_all, w_qkv_all)

    come(n2)
    nx[chip] = nc[0] + nc[1]
    go(n3)

    @pl.when(is_dec)
    def _():
        come(tensor_third(C_CROSS))
        tensor_third_sum(C_CROSS)
        go(spread(C_CROSS))

    chips_sum(C_OUT)
    chips_sum(C_Q)
    come(over_z(C_DOWN))
    over_z_sum(C_DOWN)
    go(spread_x(C_DOWN))
    come(tensor_third(C_KV))
    tensor_third_sum(C_KV)
    go(spread(C_KV))
    come(over_z(C_UP))
    over_z_sum(C_UP)
    go(spread_x(C_UP))
    for a in range(NT):
        halo_copies(a)[0].wait_send()
    for k in range(CN):
        if k in (C_DOWN, C_UP):
            gone(along_x(k, False))
            gone(along_x(k, True))
            gone(tensor_second(k))
        if k != C_CROSS:
            gone([pair(k, q) for q in range(NT)])
    gone(n1)
    gone(n2)
    gone(chips_first(C_KV, 0, 2))
    gone(chips_first(C_KV, 2, 2))

    @pl.when(is_dec)
    def _():
        gone([pair(C_CROSS, q) for q in range(NT)])
        gone(chips_first(C_CROSS, 0, NT))

    @pl.when(is_enc)
    def _():
        pair(C_CROSS, 3).wait_send()
        for a in range(NT):
            halo_copies(a)[1].wait_send()
        gone(chips_first(C_CROSS, 3))

    come(n3)
    tot_n = nx[0]
    for o in range(1, chips):
        tot_n = tot_n + nx[o]
    ng_tot[...] = tot_n
    come(spread(C_CROSS))
    go(hand(C_CROSS))
    come(spread_x(C_DOWN))
    go(hand(C_DOWN))
    for k in (C_OUT, C_Q, C_KV):
        come(spread(k))
        go(hand(k))
    come(spread_x(C_UP))
    go(hand(C_UP))
    @pl.when(jnp.logical_and(is_enc, t == 0))
    def _():
        tot = md[...] + dxm_s[...].astype(F32)
        for s in range(1, NT):
            remote(dxm_s, dxm_r.at[s], gsend.at[0], grecv.at[s], tensor=0).wait_recv()
            tot = tot + dxm_r[s].astype(F32)
        for r in range(R):
            d32[r, 0:MP] += tot[r * MP:r * MP + MP]

    dx_copy = pltpu.make_async_copy(d32, dx_out, lsem.at[10])
    dx_copy.start()
    for k in range(CN):
        come(hand(k))

    dx_copy.wait()
    gone(n3)
    for k in range(CN):
        if k in (C_DOWN, C_UP):
            gone(over_z(k))
            gone(spread_x(k))
        else:
            gone(spread(k))
        if k in (C_Q, C_OUT):
            gone([over_tensor(k, q) for q in range(3)])
            gone(over_chips(k))
        if k == C_KV:
            gone(tensor_third(k))
        gone(hand(k))

    @pl.when(is_dec)
    def _():
        gone(tensor_third(C_CROSS))

    @pl.when(jnp.logical_and(is_enc, t > 0))
    def _():
        dxm_copy.wait_send()


def layer_call(chips, lens, x, cot, wqkv, wout, wcross, wup, wdown, gain, bias):
    any_ = pl.BlockSpec(memory_space=pl.ANY)
    vmem = pl.BlockSpec(memory_space=pltpu.VMEM)
    W = W_ENC
    S = pltpu.SemaphoreType.DMA
    C = len(CHUNKS)
    o = max(chips - 1, 1)
    late = G_KV // 2 - LAST
    mid = 1024

    def V(shape, kind):
        return pltpu.VMEM(shape, kind)

    scratch = dict(
        x_ext=V((R, W, D), BF), cotm=V((R, MP, D), F32), d32=V((R, T, D), F32),
        wqkv=V((NT, 3, D, 128), BF), wout=V((NT, 128, D), BF), wcross=V((NT, 2, D, 128), BF),
        wup=V((NT, D, D), BF), wdown=V((NT, D, D), BF),
        kk=V((NT, R, W, 128), BF), vv=V((NT, R, W, 128), BF),
        qs=V((NT, R, 2, T, 128), BF), pt=V((NT, R, 2, 512, T), BF), ctx=V((R, NT, T, 128), BF),
        mask=V((R, 2, 512, 128), F32), hmask=V((2, T, 128), BF),
        xh1=V((R, T, D), F32), xh2=V((R, T, D), F32), rs1=V((R, T, 1), F32), rs2=V((R, T, 1), F32),
        h32=V((R, T, D), F32), hb=V((R, T, D), BF), h1b=V((R, T, D), BF),
        act=V((R, NT, T, D), BF), gp=V((R, NT, T, D), BF), dab=V((R, T, D), BF), dr=V((R, NT, T, 128), BF),
        dkv=V((NT, R, 2, T, 128), F32), halo_s=V((2, NT, R, 2, HALO, 128), BF),
        halo_r=V((2, NT, R, 2, HALO, 128), BF), mg_s=V((NT, R, 3, MP, 128), BF), mg_r=V((3, R, 3, MP, 128), BF),
        dxm_s=V((M, D), BF), dxm_r=V((NT, M, D), BF), mdu=V((NT, M, D), BF),
        ex_o=V((NT, NT, M, 128), BF), ex_st=V((NT, M, 128), F32), ex_f=V((NT, M, D), BF), ex_m=V((NT, M, D), BF),
        qm=V((NT, R, 2 * MP, 128), BF),
        kvm=V((NT, 2, M, 128), BF), dkvm_s=V((NT, 2, M, 128), F32), dkvm_r=V((NT, 2, M, 128), F32),
        kblk=V((R, 256, D), BF), vblk=V((R, 256, D), BF), cpt=V((R, 256, T), BF), cq=V((R, T, D), BF),
        cctx=V((R, T, D), BF), cdb=V((R, T, D), BF),
        mx1=V((M, D), F32), mx2=V((M, D), F32), mx3=V((M, D), F32), mr1=V((M, 1), F32), mr2=V((M, 1), F32),
        mr3=V((M, 1), F32), mh=V((M, D), F32), mact=V((M, D), BF), mc=V((M, D), F32),
        mm=V((M, D), BF), mst=V((2, M, 128), F32), md=V((M, D), F32), dmb=V((M, D), BF),
        g=V((NT, G_ROWS, 128), BF), r1=V((NT, HALF, 128), BF),
        rx=V((3, NT, LATE // 4, 128), BF), ry_s=V((NT, LATE // 4, 128), BF),
        ry_r=V((3, LATE // 4, 128), BF), zz=V((2, LATE // 4, 128), BF),
        rq=V((o, NT, mid // chips, 128), BF), rqs=V((NT, mid // chips, 128), BF), rqr=V((3, mid // chips, 128), BF),
        r2=V((3, late, 128), BF), r3=V((o, late // chips, 128), BF), ysum=V((late, 128), BF),
        ng=V((8, D), F32), ny=V((NT, 8, D), F32), nc=V((2, 8, D), F32),
        nx=V((chips, 8, D), F32),
        lsem=S((11,)), wsend=S((5, 6)), wrecv=S((5, 6)), w2send=S((3, 3, 3)), w2recv=S((3, 3, 3)), xsend=S((2,)), xrecv=S((2,)), msend=S((2, 3)), mrecv=S((2,)),
        esend=S((5, 3)), erecv=S((5, 3)), ksend=S((NT,)), krecv=S((NT,)), dsend=S((NT,)), drecv=S((NT,)),
        hsend=S((2, NT)), hrecv=S((2, NT)), gsend=S((1,)), grecv=S((NT,)), qsend=S((3,)), qrecv=S((3,)), sq=S((C, NT, o)), qq=S((C, NT, o)), s3=S((C, o)), q3=S((C, o)),
        s1=S((C, NT)), q1=S((C, NT)), s2=S((C, 3)), q2=S((C, 3)),
        s4=S((C, o)), q4=S((C, o)), s5=S((C,)), q5=S((C,)), ns=S((4 + o,)), nq=S((4 + o,)),
        sx=S((2, 2, 3)), qx=S((2, 2, 3)), sz=S((2,)), qz=S((2,)),
    )
    names = tuple(scratch)

    def kernel(*refs):
        layer_kernel(chips, names, *refs)

    return pl.pallas_call(
        kernel,
        out_shape=(
            jax.ShapeDtypeStruct((R, T, D), F32),
            jax.ShapeDtypeStruct((R, T, D), F32),
            jax.ShapeDtypeStruct((G_ROWS, 128), BF),
            jax.ShapeDtypeStruct((8, D), F32),
        ),
        in_specs=[pl.BlockSpec(memory_space=pltpu.SMEM)] + [any_] * 7 + [vmem] * 2,
        out_specs=(any_, any_, vmem, vmem),
        scratch_shapes=list(scratch.values()),
        compiler_params=pltpu.CompilerParams(
            collective_id=0, has_side_effects=True, vmem_limit_bytes=VMEM_BYTES
        ),
        name="layers",
    )(lens, x, cot, wqkv, wout, wcross, wup, wdown, gain, bias)


def finish_kernel(y_in, dx_in, full_in, ng, y, dx, o_qkv, o_out, o_cross, o_up, o_down, o_gain, o_bias,
                  b_y, b_dx, full, b_qkv, b_out, b_cross, b_up, b_down, s_in, s_out):
    parts = ((G_DOWN, G_UP), (G_UP, G_CROSS), (G_CROSS, G_ROWS))
    loads = [pltpu.make_async_copy(full_in.at[pl.ds(lo, hi - lo), :], full.at[pl.ds(lo, hi - lo), :], s_in.at[i])
             for i, (lo, hi) in enumerate(parts)]
    loads.append(pltpu.make_async_copy(y_in, b_y, s_in.at[3]))
    loads.append(pltpu.make_async_copy(dx_in, b_dx, s_in.at[4]))
    for c in loads:
        c.start()
    for i in range(3):
        o_gain[i] = ng[i:i + 1]
        o_bias[i] = ng[i + 3:i + 4]
    stores = []

    def store(src, dst):
        c = pltpu.make_async_copy(src, dst.at[0], s_out.at[len(stores)])
        c.start()
        stores.append(c)

    for i, (base, buf, out) in enumerate(((G_DOWN, b_down, o_down), (G_UP, b_up, o_up))):
        loads[i].wait()
        for j in range(4):
            buf[:, 128 * j:128 * j + 128] = full[base + D * j:base + D * j + D].astype(F32)
        store(buf, out)
    loads[3].wait()
    store(b_y, y)
    loads[4].wait()
    store(b_dx, dx)
    loads[2].wait()
    for j in range(3):
        b_qkv[j] = full[G_QKV + D * j:G_QKV + D * j + D].astype(F32)
    store(b_qkv, o_qkv)
    for j in range(2):
        b_cross[j] = full[G_CROSS + D * j:G_CROSS + D * j + D].astype(F32)
    store(b_cross, o_cross)
    for j in range(4):
        b_out[:, 128 * j:128 * j + 128] = full[G_OUT + 128 * j:G_OUT + 128 * j + 128].astype(F32)
    store(b_out, o_out)
    for c in stores:
        c.wait()


def finish_call(y, dx, full, ng):
    any_ = pl.BlockSpec(memory_space=pl.ANY)
    vmem = pl.BlockSpec(memory_space=pltpu.VMEM)
    shapes = ((1, R, T, D), (1, R, T, D), (1, 3, D, 128), (1, 128, D), (1, 2, D, 128), (1, D, D), (1, D, D),
              (3, 1, D), (3, 1, D))
    return pl.pallas_call(
        finish_kernel,
        out_shape=tuple(jax.ShapeDtypeStruct(s, F32) for s in shapes),
        in_specs=[any_] * 3 + [vmem],
        out_specs=(any_,) * 7 + (vmem,) * 2,
        scratch_shapes=[pltpu.VMEM((R, T, D), F32)] * 2 + [pltpu.VMEM((G_ROWS, 128), BF)]
        + [pltpu.VMEM(s[1:], F32) for s in shapes[2:7]]
        + [pltpu.SemaphoreType.DMA((5,)), pltpu.SemaphoreType.DMA((7,))],
        compiler_params=pltpu.CompilerParams(vmem_limit_bytes=VMEM_BYTES),
        name="finish",
    )(y, dx, full, ng)


def solution(mesh):
    chips = mesh.shape["dp"] // 2

    def shards(inputs, lengths, w_qkv, w_out, w_cross, w_up, w_down, norm_gain, norm_bias, cotangent):
        y, dx, full, ng = layer_call(
            chips, lengths, inputs[0], cotangent[0], w_qkv[0], w_out[0], w_cross[0], w_up[0], w_down[0],
            jnp.transpose(norm_gain, (1, 0, 2)), jnp.transpose(norm_bias, (1, 0, 2)))
        outs = finish_call(y, dx, full, ng)
        return outs[:7] + tuple(jnp.transpose(v, (1, 0, 2)) for v in outs[7:])

    return jax.shard_map(
        shards,
        mesh=mesh,
        in_specs=(
            P("section", "dp", "tensor", None),
            P("dp", None),
            P("section", None, None, "tensor"),
            P("section", "tensor", None),
            P("section", None, None, "tensor"),
            P("section", None, "tensor"),
            P("section", "tensor", None),
            P("section", None, None),
            P("section", None, None),
            P("section", "dp", "tensor", None),
        ),
        out_specs=(
            P("section", "dp", "tensor", None),
            P("section", "dp", "tensor", None),
            P("section", None, None, "tensor"),
            P("section", "tensor", None),
            P("section", None, None, "tensor"),
            P("section", None, "tensor"),
            P("section", "tensor", None),
            P("section", None, None),
            P("section", None, None),
        ),
        check_vma=False,
    )
```
